128 devices in a mesh: ctx: 32 (over x_hi, y, z), fsdp: 4 (over x_lo, core).
Axes of the slice: x: 4 (x_hi: 2, x_lo: 2; x = x_hi * 2 + x_lo), y: 4, z: 4, core: 2. Of those that a mesh axis runs over, the one named last changes fastest.
Arguments:
- streams: bfloat16 [2, 4, 2048, 4, 2048], P(None, 'fsdp', 'ctx'), may hold values from -48 to 48
- doc_start: int32 [2, 4, 2048], P(None, 'fsdp', 'ctx'), may hold values from 0 to 2047, as said below
- cotangent: bfloat16 [2, 4, 2048, 4, 2048], P(None, 'fsdp', 'ctx'), may hold values from -6 to 6
- mixing: float32 [2, 4, 6], replicated, may hold values from -0.3 to 1
- w_project: float32 [2048, 2560], P(('ctx', 'fsdp')), may hold values from -0.125 to 0.125
- w_output: float32 [2048, 2048], P(('ctx', 'fsdp')), may hold values from -0.5 to 0.5
- w_expand: float32 [2048, 11264], P(('ctx', 'fsdp')), may hold values from -0.125 to 0.125
- w_reduce: float32 [5632, 2048], P(('ctx', 'fsdp')), may hold values from -0.078125 to 0.078125
- first_mixing: float32 [2, 4, 6], replicated, may hold values from -0.01953125 to 0.01953125
- second_mixing: float32 [2, 4, 6], replicated, may hold values from 7.338825e-06 to 2.9369252e-05
- first_project: float32 [2048, 2560], P(('ctx', 'fsdp')), may hold values from -0.00012207031 to 0.00012207031
- second_project: float32 [2048, 2560], P(('ctx', 'fsdp')), may hold values from 3.2250697e-10 to 1.2906409e-09
- first_output: float32 [2048, 2048], P(('ctx', 'fsdp')), may hold values from -6.1035156e-05 to 6.1035156e-05
- second_output: float32 [2048, 2048], P(('ctx', 'fsdp')), may hold values from 8.062674e-11 to 3.2266023e-10
- first_expand: float32 [2048, 11264], P(('ctx', 'fsdp')), may hold values from -0.00018310547 to 0.00018310547
- second_expand: float32 [2048, 11264], P(('ctx', 'fsdp')), may hold values from 7.2564066e-10 to 2.9039422e-09
- first_reduce: float32 [5632, 2048], P(('ctx', 'fsdp')), may hold values from -0.00036621094 to 0.00036621094
- second_reduce: float32 [5632, 2048], P(('ctx', 'fsdp')), may hold values from 2.9025626e-09 to 1.1615769e-08
Outputs:
- new_streams: bfloat16 [2, 4, 2048, 4, 2048], P(None, 'fsdp', 'ctx')
- streams_grad: float32 [2, 4, 2048, 4, 2048], P(None, 'fsdp', 'ctx')
- grad_norm: float32 [], replicated
- updated_mixing: float32 [2, 4, 6], replicated
- moment_mixing: float32 [2, 4, 6], replicated
- square_mixing: float32 [2, 4, 6], replicated
- updated_project: float32 [2048, 2560], P(('ctx', 'fsdp'))
- moment_project: float32 [2048, 2560], P(('ctx', 'fsdp'))
- square_project: float32 [2048, 2560], P(('ctx', 'fsdp'))
- updated_output: float32 [2048, 2048], P(('ctx', 'fsdp'))
- moment_output: float32 [2048, 2048], P(('ctx', 'fsdp'))
- square_output: float32 [2048, 2048], P(('ctx', 'fsdp'))
- updated_expand: float32 [2048, 11264], P(('ctx', 'fsdp'))
- moment_expand: float32 [2048, 11264], P(('ctx', 'fsdp'))
- square_expand: float32 [2048, 11264], P(('ctx', 'fsdp'))
- updated_reduce: float32 [5632, 2048], P(('ctx', 'fsdp'))
- moment_reduce: float32 [5632, 2048], P(('ctx', 'fsdp'))
- square_reduce: float32 [5632, 2048], P(('ctx', 'fsdp'))
The draws below stay inside these ranges and needn't reach their ends.
Inputs may be any that keep to these rules, and one draw needn't show every extreme that they name: doc_start[m, b, i] is the first position of the document that holds position i of sequence (m, b): 0 at i = 0, never falling along i, at most i, and equal to i where a document begins; the last position of every sequence begins a document of its own.
All inputs are finite; a program needn't handle non-finite values.
Results may differ from the reference program's by a relative error of at most 0.019.
Values may be sent and summed in bfloat16 or wider, within the bound.
A program may use at most 640 MiB of HBM per device.

```python
import math
import jax
import jax.numpy as jnp
from jax import lax

D = 2048
H = 32
KV = 4
HD = 64
FF = 5632
NS = 4
MICRO = 2
STEP = 10
CUTS = 8
SEQ_LEN = 2048
BATCH = 4
N_CTX = 32


def draw_streams(key, part):
    key = jax.random.fold_in(key, 11)
    keys = jax.random.split(key, 3)
    shape = (MICRO, BATCH, SEQ_LEN, NS, D)
    ramp = jnp.arange(D, dtype=jnp.float32) / D - 0.5
    feature = jnp.exp(ramp * math.log(3.0) + jax.random.uniform(keys[0], (D,), minval=-0.55, maxval=0.55))
    scales = jnp.exp(jax.random.uniform(keys[1], (MICRO, BATCH, SEQ_LEN, NS, 1), minval=math.log(0.4), maxval=math.log(4.0)))
    base = jnp.clip(jax.random.normal(keys[2], shape), -4.0, 4.0)
    return (base * feature * scales).astype(jnp.bfloat16)


def draw_mixing(key, part):
    key = jax.random.fold_in(key, 23)
    keys = jax.random.split(key, 4)
    feed_least, feed_most, gain_least = (0.3, 0.7, 0.5)
    feed = jax.random.uniform(keys[0], (2, NS, 1), minval=feed_least, maxval=feed_most)
    gained = jax.random.uniform(keys[1], (2, NS, 1), minval=gain_least, maxval=1.0)
    identity = jnp.eye(NS, dtype=jnp.float32)
    diagonal = jax.random.uniform(keys[2], (2, NS, NS), minval=0.7, maxval=1.0)
    offside = jax.random.uniform(keys[3], (2, NS, NS), minval=-0.3, maxval=0.3)
    route = identity * diagonal + (1.0 - identity) * offside
    return jnp.concatenate([feed, gained, route], axis=-1).astype(jnp.float32)


def draw_doc_start(key, part):
    key = jax.random.fold_in(key, 37)
    keys = jax.random.split(key, 4)
    span = SEQ_LEN // N_CTX
    chosen = jax.random.randint(keys[0], (1, BATCH), 0, MICRO)
    spanning = jnp.arange(MICRO, dtype=jnp.int32)[:, None] == chosen
    scattered = jax.random.randint(keys[1], (MICRO, BATCH, CUTS), 0, SEQ_LEN)
    opening = jax.random.randint(keys[2], (MICRO, BATCH, 1), 1, span)
    closing = jax.random.randint(keys[3], (MICRO, BATCH, 1), SEQ_LEN - span + 1, SEQ_LEN)
    steady = jnp.concatenate([opening, closing, jnp.broadcast_to(opening, (MICRO, BATCH, CUTS - 2))], axis=-1)
    cuts = jnp.where(spanning[..., None], steady, scattered)
    ending = jnp.full((MICRO, BATCH, 1), SEQ_LEN - 1, jnp.int32)
    cuts = jnp.concatenate([cuts, ending], axis=-1)
    places = jnp.arange(SEQ_LEN, dtype=jnp.int32)
    marked = jnp.any(cuts[..., None, :] == places[:, None], axis=-1)
    return lax.cummax(jnp.where(marked, places, 0), axis=2).astype(jnp.int32)


def steps_of(own_key, extent, cuts, least, largest):
    def one(dim, parts):
        heights = jax.random.uniform(jax.random.fold_in(jax.random.fold_in(own_key, 6), dim), (parts,), jnp.float32, least / len(cuts), largest / len(cuts))
        return jnp.repeat(jnp.exp(heights), extent[dim] // parts).reshape((-1,) + (1,) * (len(extent) - dim - 1))

    loudness = one(*cuts[0])
    for cut in cuts[1:]:
        loudness = loudness * one(*cut)
    return loudness


def noise(rng, extent, deviation, limit, cuts=(), held_as=jnp.bfloat16):
    drawn = deviation * jax.random.normal(rng, extent, jnp.float32)
    if cuts:
        drawn = drawn * steps_of(rng, extent, cuts, -0.22, 0.18)
    return jnp.clip(drawn, -limit, limit).astype(held_as)


def setup_inputs(seed: int = 0) -> dict:
    splits = jax.random.split(jax.random.key(seed), 19)
    return {
        "streams": draw_streams(jax.random.fold_in(splits[18], 71), 0),
        "doc_start": draw_doc_start(jax.random.fold_in(splits[18], 71), 0),
        "cotangent": noise(splits[2], (MICRO, BATCH, SEQ_LEN, NS, D), 1.0, 6.0, ((1, 4), (2, 32))),
        "mixing": draw_mixing(jax.random.fold_in(splits[18], 71), 0),
        "w_project": noise(splits[4], (D, (H + 2 * KV) * HD), D ** -0.5, 0.125, ((0, 128),), jnp.float32),
        "w_output": noise(splits[5], (D, D), (D // 16) ** -0.5, 0.5, ((0, 128),), jnp.float32),
        "w_expand": noise(splits[6], (D, 2 * FF), D ** -0.5, 0.125, ((0, 128),), jnp.float32),
        "w_reduce": noise(splits[7], (FF, D), FF ** -0.5, 0.078125, ((0, 128),), jnp.float32),
        "first_mixing": noise(splits[8], (2, NS, NS + 2), (0.111 * D ** 0.5 / (0.09 * D * (H + 2 * KV) * HD + 0.0225 * D * D + 0.405 * D * FF + 0.81 * FF * D + D * 2 * NS * (NS + 2)) ** 0.5), 0.01953125, (), jnp.float32),
        "second_mixing": jnp.clip(jnp.exp(jax.random.uniform(splits[9], (2, NS, NS + 2), jnp.float32, math.log(7.338825071201427e-06), math.log(2.9369251933530904e-05))), 7.338825071201427e-06, 2.9369251933530904e-05),
        "first_project": noise(splits[10], (D, (H + 2 * KV) * HD), (0.111 * 0.3 / (0.09 * D * (H + 2 * KV) * HD + 0.0225 * D * D + 0.405 * D * FF + 0.81 * FF * D + D * 2 * NS * (NS + 2)) ** 0.5), 0.00012207031, ((0, 128),), jnp.float32),
        "second_project": jnp.clip(jnp.exp(math.log(1.2906409274648922e-09) - 1.3867695 * jax.random.uniform(splits[11], (D, (H + 2 * KV) * HD), jnp.float32) ** steps_of(splits[11], (D, (H + 2 * KV) * HD), ((0, 128),), -0.2, 0.2)), 3.2250696557767355e-10, 1.2906409274648922e-09),
        "first_output": noise(splits[12], (D, D), (0.111 * 0.15 / (0.09 * D * (H + 2 * KV) * HD + 0.0225 * D * D + 0.405 * D * FF + 0.81 * FF * D + D * 2 * NS * (NS + 2)) ** 0.5), 6.103515625e-05, ((0, 128),), jnp.float32),
        "second_output": jnp.clip(jnp.exp(math.log(3.2266023186622306e-10) - 1.3867695 * jax.random.uniform(splits[13], (D, D), jnp.float32) ** steps_of(splits[13], (D, D), ((0, 128),), -0.2, 0.2)), 8.062674139441839e-11, 3.2266023186622306e-10),
        "first_expand": noise(splits[14], (D, 2 * FF), (0.111 * 0.45 / (0.09 * D * (H + 2 * KV) * HD + 0.0225 * D * D + 0.405 * D * FF + 0.81 * FF * D + D * 2 * NS * (NS + 2)) ** 0.5), 0.00018310547, ((0, 128),), jnp.float32),
        "second_expand": jnp.clip(jnp.exp(math.log(2.90394219781831e-09) - 1.3867695 * jax.random.uniform(splits[15], (D, 2 * FF), jnp.float32) ** steps_of(splits[15], (D, 2 * FF), ((0, 128),), -0.2, 0.2)), 7.256406586719777e-10, 2.90394219781831e-09),
        "first_reduce": noise(splits[16], (FF, D), (0.111 * 0.9 / (0.09 * D * (H + 2 * KV) * HD + 0.0225 * D * D + 0.405 * D * FF + 0.81 * FF * D + D * 2 * NS * (NS + 2)) ** 0.5), 0.00036621094, ((0, 128),), jnp.float32),
        "second_reduce": jnp.clip(jnp.exp(math.log(1.161576879127324e-08) - 1.3867695 * jax.random.uniform(splits[17], (FF, D), jnp.float32) ** steps_of(splits[17], (FF, D), ((0, 128),), -0.2, 0.2)), 2.9025626346879108e-09, 1.161576879127324e-08),
    }


@jax.custom_vjp
def low(v):
    return lax.optimization_barrier(v.astype(jnp.bfloat16)).astype(jnp.float32)

@jax.custom_vjp
def low_back(v):
    return v

def low_keep(v):
    return (low(v), None)

def low_pass(kept, grad):
    return (grad,)

def back_keep(v):
    return (v, None)

def back_low(kept, grad):
    return (low(grad),)
low.defvjp(low_keep, low_pass)
low_back.defvjp(back_keep, back_low)
NORM_EPS = 1e-05
THETA_BASE = 10000.0
BETA_ONE = 0.9
BETA_TWO = 0.95
ADAM_EPS = 1e-08
RATE_MATRIX = 0.06
RATE_MIXING = 0.5
DECAY_MATRIX = 0.1
THRESHOLD = 1.0
HIGH = lax.Precision.HIGHEST

def layer_norm(entry):
    center = entry - lax.optimization_barrier(jnp.mean(entry, axis=-1, keepdims=True))
    return center * lax.rsqrt(lax.optimization_barrier(jnp.mean(center * center, axis=-1, keepdims=True)) + NORM_EPS)

def rotary(values, spots):
    half = values.shape[-1] // 2
    freq = jnp.exp(jnp.arange(half, dtype=jnp.float32) * (-2.0 * math.log(THETA_BASE) / values.shape[-1]))
    angle = spots[:, None] * freq[None, :]
    cosine = jnp.cos(angle)[:, None, :]
    sine = jnp.sin(angle)[:, None, :]
    first = values[..., :half]
    second = values[..., half:]
    return jnp.concatenate([first * cosine - second * sine, second * cosine + first * sine], axis=-1)

def mix_in(tokens, weights):
    return jnp.einsum('lsd,s->ld', tokens, weights[:, 0], precision=HIGH)

def write_back(tokens, weights, branch):
    kept = jnp.einsum('lsd,st->ltd', tokens, weights[:, 2:], precision=HIGH)
    return kept + weights[None, :, 1, None] * branch[:, None, :]

def attention(query, keys, values, starts):
    length = query.shape[0]
    block = math.gcd(length, 512)
    count = length // block
    scale = query.shape[-1] ** (-0.5)
    places = jnp.arange(length, dtype=jnp.int32)

    def one_block(item):
        rows, row_places, row_starts = item
        inner = jnp.einsum('bkgd,nkd->kgbn', rows, keys, precision=HIGH) * scale
        scores = low_back(inner)
        allowed = (places[None, :] >= row_starts[:, None]) & (places[None, :] <= row_places[:, None])
        scores = jnp.where(allowed, scores, -1e+30)
        top = lax.optimization_barrier(jnp.max(scores, axis=-1, keepdims=True))
        weights = jnp.exp(scores - top)
        probs = weights / lax.optimization_barrier(jnp.sum(weights, axis=-1, keepdims=True))
        return jnp.einsum('kgbn,nkd->bkgd', low(probs), values, precision=HIGH)
    blocks = (query.reshape((count, block) + query.shape[1:]), places.reshape(count, block), starts.reshape(count, block))
    return lax.map(jax.checkpoint(one_block), blocks).reshape(query.shape)

def forward(tokens, starts, mixing, w_project, w_output, w_expand, w_reduce):
    length = tokens.shape[0]
    groups = H // KV
    places = jnp.arange(length, dtype=jnp.int32)
    spots = (places - starts).astype(jnp.float32)
    normed = low(layer_norm(mix_in(tokens, mixing[0])))
    joined = low_back(jnp.dot(normed, low(w_project), precision=HIGH))
    query = low(rotary(joined[:, :H * HD].reshape(length, H, HD), spots)).reshape(length, KV, groups, HD)
    keys = low(rotary(joined[:, H * HD:(H + KV) * HD].reshape(length, KV, HD), spots))
    values = low(joined[:, (H + KV) * HD:].reshape(length, KV, HD))
    mixed = attention(query, keys, values, starts).reshape(length, H * HD)
    attended = low_back(low(mixed))
    branch = low_back(jnp.dot(attended, low(w_output), precision=HIGH))
    middle = write_back(tokens, mixing[0], branch)
    normed = low(layer_norm(mix_in(middle, mixing[1])))
    opened = low_back(jnp.dot(normed, low(w_expand), precision=HIGH))
    hidden = low(jax.nn.silu(opened[:, :FF]) * opened[:, FF:])
    branch = low_back(jnp.dot(hidden, low(w_reduce), precision=HIGH))
    return write_back(middle, mixing[1], branch)

def adam(weight, grad, first, second, factor, rate, decay):
    grad = grad * factor
    first = BETA_ONE * first + (1.0 - BETA_ONE) * grad
    second = BETA_TWO * second + (1.0 - BETA_TWO) * grad * grad
    ahead = first / (1.0 - BETA_ONE ** STEP)
    scaled = second / (1.0 - BETA_TWO ** STEP)
    weight = weight - rate * (ahead / (jnp.sqrt(scaled) + ADAM_EPS) + decay * weight)
    return (weight, first, second)

def reference(streams, doc_start, cotangent, mixing, w_project, w_output, w_expand, w_reduce, first_mixing, second_mixing, first_project, second_project, first_output, second_output, first_expand, second_expand, first_reduce, second_reduce):
    count = MICRO * BATCH
    flat_streams = streams.reshape(count, SEQ_LEN, NS, D)
    flat_starts = doc_start.reshape(count, SEQ_LEN)
    flat_cot = cotangent.reshape(count, SEQ_LEN, NS, D)
    params = (mixing, w_project, w_output, w_expand, w_reduce)

    def one(totals, item):
        tokens, starts, coming = item

        def run(inputs, mix, proj, outp, expd, redc):
            return forward(inputs, starts, mix, proj, outp, expd, redc)
        result, pull = jax.vjp(run, tokens.astype(jnp.float32), *params)
        grads = pull(coming.astype(jnp.float32))
        totals = tuple((a + b for a, b in zip(totals, grads[1:])))
        return (totals, (result.astype(jnp.bfloat16), grads[0]))
    zeros = tuple((jnp.zeros_like(p) for p in params))
    totals, (fresh, backed) = lax.scan(one, zeros, (flat_streams, flat_starts, flat_cot))
    squares = jnp.sum(totals[0] * totals[0])
    for grad in totals[1:]:
        squares = squares + jnp.sum(grad * grad)
    norm = jnp.sqrt(squares)
    factor = THRESHOLD / jnp.maximum(norm, THRESHOLD)
    mix_new = adam(mixing, totals[0], first_mixing, second_mixing, factor, RATE_MIXING, 0.0)
    proj_new = adam(w_project, totals[1], first_project, second_project, factor, RATE_MATRIX, DECAY_MATRIX)
    outp_new = adam(w_output, totals[2], first_output, second_output, factor, RATE_MATRIX, DECAY_MATRIX)
    expd_new = adam(w_expand, totals[3], first_expand, second_expand, factor, RATE_MATRIX, DECAY_MATRIX)
    redc_new = adam(w_reduce, totals[4], first_reduce, second_reduce, factor, RATE_MATRIX, DECAY_MATRIX)
    return (fresh.reshape(streams.shape), backed.reshape(streams.shape), norm, mix_new[0], mix_new[1], mix_new[2], proj_new[0], proj_new[1], proj_new[2], outp_new[0], outp_new[1], outp_new[2], expd_new[0], expd_new[1], expd_new[2], redc_new[0], redc_new[1], redc_new[2])
```

```python
import functools
import math

import jax
import jax.numpy as jnp
from jax import lax
from jax.experimental import pallas as pl
from jax.experimental.pallas import tpu as pltpu
from jax.sharding import PartitionSpec as P

H = 32
FF = 5632
STEP = 10
THETA_BASE = 10000.0
BETA_ONE = 0.9
BETA_TWO = 0.95
ADAM_EPS = 1e-08
RATE_MATRIX = 0.06
RATE_MIXING = 0.5
DECAY_MATRIX = 0.1
THRESHOLD = 1.0


MESH = pl.DeviceIdType.MESH


def place():
    ctx = lax.axis_index("ctx")
    fsdp = lax.axis_index("fsdp")
    return (2 * (ctx // 16) + fsdp // 2, (ctx // 4) % 4, ctx % 4, fsdp % 2)


def ident(x, y, z, c):
    return ((x // 2) * 16 + y * 4 + z, (x % 2) * 2 + c)


def moved(spot, axis, step):
    spot = list(spot)
    spot[axis] = (spot[axis] + step + 4) % 4
    return tuple(spot)


def neighbours(spot):
    x, y, z, c = spot
    out = [(x, y, z, 1 - c)]
    for axis in range(3):
        out += [moved(spot, axis, 1), moved(spot, axis, -1)]
    return out


def meet(spot):
    barrier = pltpu.get_barrier_semaphore()
    for other in neighbours(spot):
        pl.semaphore_signal(barrier, inc=1, device_id=ident(*other), device_id_type=MESH)
    pl.semaphore_wait(barrier, 7)


def box(spot, known, axis=None, at=None):
    x, y, z, c = spot
    place = [x, y, z]
    if axis is not None:
        place[axis] = at
    index = []
    for d in range(3):
        whole = d in known
        if d == 0:
            xs = (slice(None), slice(None)) if whole else (place[0] // 2, place[0] % 2)
        elif whole:
            index.append(slice(None))
        else:
            index.append(place[d])
    return (xs[0], index[0], index[1], xs[1])


def thirds(tiles):
    cuts = [0, (tiles + 2) // 3, (tiles + 2) // 3 + (tiles + 1) // 3, tiles]
    out = []
    for a, b in zip(cuts[:-1], cuts[1:]):
        mid = a + (b - a + 1) // 2
        out.append((a * 128, mid * 128, b * 128))
    return out


def gather_kernel(n, *refs):
    shards = refs[:n]
    outs = refs[n : 2 * n]
    own_sem, send, recv, csend, crecv = refs[2 * n :]
    spot = place()
    x, y, z, c = spot
    sibling = ident(x, y, z, 1 - c)
    pieces = [thirds(o.shape[-1] // 128) for o in outs]
    local = []
    for w in range(n):
        copy = pltpu.make_async_copy(shards[w], outs[w].at[x // 2, y, z, x % 2, c], own_sem.at[w])
        copy.start()
        local.append(copy)
    meet(spot)
    cross = []

    def core_copy(w, slot, index, a, b):
        view = outs[w].at[index + (c, slice(None), slice(a, b))]
        copy = pltpu.make_async_remote_copy(
            view, view, csend.at[w, slot], crecv.at[w, slot], device_id=sibling, device_id_type=MESH
        )
        copy.start()
        cross.append(copy)

    def ring_copy(w, p, k, j, index, a, b, to):
        view = outs[w].at[index + (c, slice(None), slice(a, b))]
        copy = pltpu.make_async_remote_copy(
            view, view, send.at[w, p, k, j], recv.at[w, p, k, j], device_id=ident(*to), device_id_type=MESH
        )
        copy.start()
        return copy

    for w in range(n):
        local[w].wait()
        core_copy(w, 0, (x // 2, y, z, x % 2), 0, outs[w].shape[-1])
    ring = {}
    for k in range(3):
        for w in range(n):
            for p in range(3):
                order = (p, (p + 1) % 3, (p + 2) % 3)
                axis, known = order[k], order[:k]
                a, m, b = pieces[w][p]
                if k:
                    for j in (2, 3):
                        ring[w, p, k - 1, j].wait_recv()
                    prev = order[k - 1]
                    core_copy(w, 3 * (3 * p + k - 1) + 3, box(spot, order[: k - 1], prev, (spot[prev] + 2) % 4), a, b)
                mine = box(spot, known)
                ring[w, p, k, 0] = ring_copy(w, p, k, 0, mine, a, b, moved(spot, axis, 1))
                ring[w, p, k, 1] = ring_copy(w, p, k, 1, mine, a, b, moved(spot, axis, -1))
        for w in range(n):
            for p in range(3):
                order = (p, (p + 1) % 3, (p + 2) % 3)
                axis, known = order[k], order[:k]
                a, m, b = pieces[w][p]
                ring[w, p, k, 0].wait_recv()
                left = box(spot, known, axis, (spot[axis] + 3) % 4)
                ring[w, p, k, 2] = ring_copy(w, p, k, 2, left, a, m, moved(spot, axis, 1))
                core_copy(w, 3 * (3 * p + k) + 1, left, a, b)
                ring[w, p, k, 1].wait_recv()
                right = box(spot, known, axis, (spot[axis] + 1) % 4)
                ring[w, p, k, 3] = ring_copy(w, p, k, 3, right, m, b, moved(spot, axis, -1))
                core_copy(w, 3 * (3 * p + k) + 2, right, a, b)
    for w in range(n):
        for p in range(3):
            order = (p, (p + 1) % 3, (p + 2) % 3)
            a, m, b = pieces[w][p]
            for j in (2, 3):
                ring[w, p, 2, j].wait_recv()
            prev = order[2]
            core_copy(w, 3 * (3 * p + 2) + 3, box(spot, order[:2], prev, (spot[prev] + 2) % 4), a, b)
    for copy in ring.values():
        copy.wait_send()
    for copy in cross:
        copy.wait()


def gather(shards, collective_id):
    n = len(shards)
    return pl.pallas_call(
        functools.partial(gather_kernel, n),
        out_shape=[jax.ShapeDtypeStruct((2, 4, 4, 2, 2) + s.shape, s.dtype) for s in shards],
        in_specs=[pl.BlockSpec(memory_space=pl.ANY)] * n,
        out_specs=[pl.BlockSpec(memory_space=pl.ANY)] * n,
        scratch_shapes=[
            pltpu.SemaphoreType.DMA((n,)),
            pltpu.SemaphoreType.DMA((n, 3, 3, 4)),
            pltpu.SemaphoreType.DMA((n, 3, 3, 4)),
            pltpu.SemaphoreType.DMA((n, 28)),
            pltpu.SemaphoreType.DMA((n, 28)),
        ],
        compiler_params=pltpu.CompilerParams(collective_id=collective_id, has_side_effects=True),
    )(*shards)


W = 512
HALF = 256
UNITS = 45
CHUNKS = 15
SLOTS = 3
STAGES = 6
COLS = 2048 + 12288 + 2048 + 2560


def unit_spot(u):
    early = u // 12
    early = 1 - (1 // (1 + early))
    left = (1 - early) * (u // 4) + early * (3 + u // 36 + u // 40)
    column = (1 - early) * ((u % 4) * W) + early * (2048 + (u - 12) * W)
    return left, pl.multiple_of(column, W)


def scatter_kernel(lhs, rhs, mix, grads, total, left, right, acc1, acc2,
                   sa, ra, sb, rb, sc, rc, sd, rd, se, re, sf, rf, vsend, vrecv, out,
                   send_sem, recv_sem, free_sem, local_sem, side_send, side_recv, out_sem, v_send_sem, v_recv_sem):
    spot = place()
    x, y, z, c = spot
    pos = (x, y, z)
    sibling = (x, y, z, 1 - c)
    barrier = pltpu.get_barrier_semaphore()
    others = [sibling] + [moved(spot, axis, step) for axis in range(3) for step in (1, 2, 3)]
    for other in others:
        pl.semaphore_signal(barrier, inc=1, device_id=ident(*other), device_id_type=MESH)
    pl.semaphore_wait(barrier, len(others))

    parts = (((0, 3), (0, 2048)), ((3, 4), (2048, 14336)), ((4, 6), (14336, COLS)))
    moves = []
    for j, ((l0, l1), (c0, c1)) in enumerate(parts):
        own = [
            pltpu.make_async_copy(lhs.at[c, l0:l1], left.at[l0:l1, :, :, :, :, 0:128], local_sem.at[j, 0]),
            pltpu.make_async_copy(rhs.at[:, c0:c1], right.at[0:128, c0:c1], local_sem.at[j, 1]),
        ]
        far = [
            pltpu.make_async_remote_copy(
                lhs.at[1 - c, l0:l1], left.at[l0:l1, :, :, :, :, 128:256], side_send.at[j, 0], side_recv.at[j, 0],
                device_id=ident(*sibling), device_id_type=MESH),
            pltpu.make_async_remote_copy(
                rhs.at[:, c0:c1], right.at[128:256, c0:c1], side_send.at[j, 1], side_recv.at[j, 1],
                device_id=ident(*sibling), device_id_type=MESH),
        ]
        for copy in own + far:
            copy.start()
        moves.append((own, far))

    def arrive(j):
        for copy in moves[j][0]:
            copy.wait()
        for copy in moves[j][1]:
            copy.wait_recv()

    arrive(0)

    sends = (sa, sb, sc, sd, se, sf)
    recvs = (ra, rb, rc, rd, re, rf)

    def hop(stage, p, d, slot):
        axis = (p + stage // 2) % 3
        return pltpu.make_async_remote_copy(
            sends[stage].at[p, d, slot], recvs[stage].at[p, d, slot],
            send_sem.at[stage, p, d, slot], recv_sem.at[stage, p, d, slot],
            device_id=ident(*moved(spot, axis, 1 - 2 * d)), device_id_type=MESH)

    def before_send(stage, p, q):
        @pl.when(q >= SLOTS)
        def _():
            for d in (0, 1):
                hop(stage, p, d, q % SLOTS).wait_send()
                pl.semaphore_wait(free_sem.at[stage, p, d], 1)

    def give_back(stage, p, q):
        @pl.when(q < CHUNKS - SLOTS)
        def _():
            axis = (p + stage // 2) % 3
            for d in (0, 1):
                pl.semaphore_signal(free_sem.at[stage, p, d], inc=1,
                                    device_id=ident(*moved(spot, axis, 2 * d - 1)), device_id_type=MESH)

    def go(stage, p, q):
        for d in (0, 1):
            hop(stage, p, d, q % SLOTS).start()

    def come(stage, p, q):
        for d in (0, 1):
            hop(stage, p, d, q % SLOTS).wait_recv()

    def rows(p, l, a):
        if p == 0:
            got = left[l, a]
        elif p == 1:
            got = left[l, :, a]
        else:
            got = left[l, :, :, a]
        return got.reshape(256, 256)

    def product(p, q, a, lo, hi):
        l, column = unit_spot(3 * q + p)
        return jnp.dot(rows(p, l, a), right[:, pl.ds(pl.multiple_of(column + lo, HALF), hi - lo)],
                       preferred_element_type=jnp.float32)

    def at(p, step):
        return (pos[p] + step + 4) % 4

    bf = jnp.bfloat16
    f32 = jnp.float32

    def stage1(q):
        s = q % SLOTS
        for p in range(3):
            before_send(0, p, q)
            for d in (0, 1):
                sa[p, d, s] = product(p, q, at(p, 2), d * HALF, d * HALF + HALF).astype(bf)
            go(0, p, q)

    def stage2(q):
        s = q % SLOTS
        for p in range(3):
            before_send(1, p, q)
            come(0, p, q)
            for d in (0, 1):
                lo = d * HALF
                near = at(p, 1 - 2 * d)
                sb[p, d, s, :, lo : lo + HALF] = (
                    product(p, q, near, lo, lo + HALF) + ra[p, d, s].astype(f32)).astype(bf)
                other = HALF - lo
                sb[p, d, s, :, other : other + HALF] = product(p, q, near, other, other + HALF).astype(bf)
            give_back(0, p, q)
            go(1, p, q)

    def part(p, ref, b):
        return ref.at[:, b] if p == 1 else ref.at[b]

    def stage3(q):
        s = q % SLOTS
        for p in range(3):
            come(1, p, q)
            for lo in (0, HALF):
                both = (product(p, q, pos[p], lo, lo + HALF)
                        + rb[p, 0, s, :, lo : lo + HALF].astype(f32) + rb[p, 1, s, :, lo : lo + HALF].astype(f32))
                acc1[p, s, :, :, :, lo : lo + HALF] = both.reshape(4, 4, 16, HALF)
            give_back(1, p, q)
            before_send(2, p, q)
            ahead = at((p + 1) % 3, 2)
            for d in (0, 1):
                sc[p, d, s] = part(p, acc1.at[p, s], ahead)[:, :, d * HALF : d * HALF + HALF].astype(bf)
            go(2, p, q)

    def stage4(q):
        s = q % SLOTS
        for p in range(3):
            before_send(3, p, q)
            come(2, p, q)
            for d in (0, 1):
                lo = d * HALF
                other = HALF - lo
                mine = part(p, acc1.at[p, s], at((p + 1) % 3, 1 - 2 * d))
                sd[p, d, s, :, :, lo : lo + HALF] = (
                    mine[:, :, lo : lo + HALF] + rc[p, d, s].astype(f32)).astype(bf)
                sd[p, d, s, :, :, other : other + HALF] = mine[:, :, other : other + HALF].astype(bf)
            give_back(2, p, q)
            go(3, p, q)

    def stage5(q):
        s = q % SLOTS
        for p in range(3):
            come(3, p, q)
            acc2[p, s] = (part(p, acc1.at[p, s], pos[(p + 1) % 3])[...]
                          + rd[p, 0, s].astype(f32) + rd[p, 1, s].astype(f32))
            give_back(3, p, q)
            before_send(4, p, q)
            ahead = at((p + 2) % 3, 2)
            for d in (0, 1):
                se[p, d, s] = acc2[p, s, ahead, :, d * HALF : d * HALF + HALF].astype(bf)
            go(4, p, q)

    def stage6(q):
        s = q % SLOTS
        for p in range(3):
            before_send(5, p, q)
            come(4, p, q)
            for d in (0, 1):
                lo = d * HALF
                other = HALF - lo
                near = at((p + 2) % 3, 1 - 2 * d)
                sf[p, d, s, :, lo : lo + HALF] = (
                    acc2[p, s, near, :, lo : lo + HALF] + re[p, d, s].astype(f32)).astype(bf)
                sf[p, d, s, :, other : other + HALF] = acc2[p, s, near, :, other : other + HALF].astype(bf)
            give_back(4, p, q)
            go(5, p, q)

    def stage7(q):
        s = q % SLOTS
        for p in range(3):
            come(5, p, q)
            out[3 * q + p] = (acc2[p, s, pos[(p + 2) % 3]]
                              + rf[p, 0, s].astype(f32) + rf[p, 1, s].astype(f32))
            give_back(5, p, q)

    def step(t, carry):
        @pl.when(t == 4)
        def _():
            arrive(1)

        @pl.when(t == 12)
        def _():
            arrive(2)

        for lag, stage in enumerate((stage1, stage2, stage3, stage4, stage5, stage6, stage7)):
            @pl.when((t >= lag) & (t < CHUNKS + lag))
            def _(stage=stage, lag=lag):
                stage(t - lag)
        return carry

    lax.fori_loop(0, CHUNKS + 6, step, 0)

    def tail(q, carry):
        for stage in range(STAGES):
            for p in range(3):
                for d in (0, 1):
                    hop(stage, p, d, q % SLOTS).wait_send()
        return carry

    lax.fori_loop(CHUNKS - SLOTS, CHUNKS, tail, 0)
    for own, far in moves:
        for copy in far:
            copy.wait_send()

    write = pltpu.make_async_copy(out, grads, out_sem)
    write.start()

    def squares(u, carry):
        g = out[u]
        return carry + g * g

    summed = lax.fori_loop(0, UNITS, squares, jnp.zeros((16, W), f32))
    lanes = jnp.sum(summed, axis=0, keepdims=True)
    lanes = lanes[:, 0:128] + lanes[:, 128:256] + lanes[:, 256:384] + lanes[:, 384:512]
    vector = mix[...] + jnp.where(lax.broadcasted_iota(jnp.int32, (8, 128), 0) == 7, lanes, 0.0)
    for phase in range(4):
        vsend[phase] = vector
        if phase == 0:
            targets = [(0, sibling)]
        else:
            targets = [(step - 1, moved(spot, phase - 1, step)) for step in (1, 2, 3)]
        copies = [
            pltpu.make_async_remote_copy(
                vsend.at[phase], vrecv.at[phase, k], v_send_sem.at[phase, k], v_recv_sem.at[phase, k],
                device_id=ident(*to), device_id_type=MESH)
            for k, to in targets
        ]
        for copy in copies:
            copy.start()
        for copy in copies:
            copy.wait()
        for k, _ in targets:
            vector = vector + vrecv[phase, k]
    total[...] = vector
    write.wait()


def scatter(lhs, rhs, mix, collective_id):
    bf = jnp.bfloat16
    f32 = jnp.float32
    pair = lambda shape: [pltpu.VMEM((3, 2, SLOTS) + shape, bf)] * 2
    return pl.pallas_call(
        scatter_kernel,
        out_shape=[jax.ShapeDtypeStruct((UNITS, 16, W), f32), jax.ShapeDtypeStruct((8, 128), f32)],
        in_specs=[pl.BlockSpec(memory_space=pl.ANY)] * 2 + [pl.BlockSpec(memory_space=pltpu.VMEM)],
        out_specs=[pl.BlockSpec(memory_space=pl.ANY), pl.BlockSpec(memory_space=pltpu.VMEM)],
        scratch_shapes=[
            pltpu.VMEM((6, 4, 4, 4, 16, 256), bf),
            pltpu.VMEM((256, COLS), bf),
            pltpu.VMEM((3, SLOTS, 4, 4, 16, W), f32),
            pltpu.VMEM((3, SLOTS, 4, 16, W), f32),
            *pair((256, HALF)),
            *pair((256, W)),
            *pair((4, 16, HALF)),
            *pair((4, 16, W)),
            *pair((16, HALF)),
            *pair((16, W)),
            pltpu.VMEM((4, 8, 128), f32),
            pltpu.VMEM((4, 3, 8, 128), f32),
            pltpu.VMEM((UNITS, 16, W), f32),
            pltpu.SemaphoreType.DMA((STAGES, 3, 2, SLOTS)),
            pltpu.SemaphoreType.DMA((STAGES, 3, 2, SLOTS)),
            pltpu.SemaphoreType.REGULAR((STAGES, 3, 2)),
            pltpu.SemaphoreType.DMA((3, 2)),
            pltpu.SemaphoreType.DMA((3, 2)),
            pltpu.SemaphoreType.DMA((3, 2)),
            pltpu.SemaphoreType.DMA,
            pltpu.SemaphoreType.DMA((4, 3)),
            pltpu.SemaphoreType.DMA((4, 3)),
        ],
        compiler_params=pltpu.CompilerParams(
            collective_id=collective_id, has_side_effects=True, vmem_limit_bytes=60 * 1024 * 1024),
    )(lhs, rhs, mix)


def kv_meet(spot):
    barrier = pltpu.get_barrier_semaphore()
    others = [moved(spot, 0, 2)] + [moved(spot, axis, step) for axis in (1, 2) for step in (1, -1)]
    for other in others:
        pl.semaphore_signal(barrier, inc=1, device_id=ident(*other), device_id_type=MESH)
    pl.semaphore_wait(barrier, len(others))


def kv_gather_kernel(shard, whole, own_sem, send, recv):
    spot = place()
    x, y, z, c = spot
    xh = x // 2
    own = pltpu.make_async_copy(shard, whole.at[:, xh, y, z], own_sem)
    own.start()
    kv_meet(spot)

    def copy(p, j, src, dst, to):
        made = pltpu.make_async_remote_copy(
            src, dst, send.at[p, j], recv.at[p, j], device_id=ident(*to), device_id_type=MESH)
        made.start()
        return made

    cols = [slice(0, 256), slice(256, 512)]
    made = {}
    for p in range(2):
        made[p, 0] = copy(p, 0, shard.at[:, :, cols[p]], whole.at[:, xh, y, z, :, cols[p]], moved(spot, 0, 2))
    own.wait()
    for k in range(2):
        for p in range(2):
            axis = (1, 2)[(p + k) % 2]
            if k == 0:
                made[p, 0].wait_recv()
                view = whole.at[:, :, y, z, :, cols[p]]
            else:
                made[p, 3].wait_recv()
                made[p, 4].wait_recv()
                view = whole.at[:, :, :, z, :, cols[p]] if axis == 2 else whole.at[:, :, y, :, :, cols[p]]
            made[p, 4 * k + 1] = copy(p, 4 * k + 1, view, view, moved(spot, axis, 1))
            made[p, 4 * k + 2] = copy(p, 4 * k + 2, view, view, moved(spot, axis, -1))
        for p in range(2):
            axis = (1, 2)[(p + k) % 2]
            for d in (0, 1):
                made[p, 4 * k + 1 + d].wait_recv()
                near = (spot[axis] + 3 + 2 * d) % 4
                if k == 0:
                    view = whole.at[d, :, y, near, :, cols[p]] if axis == 2 else whole.at[d, :, near, z, :, cols[p]]
                else:
                    view = whole.at[d, :, :, near, :, cols[p]] if axis == 2 else whole.at[d, :, near, :, :, cols[p]]
                made[p, 4 * k + 3 + d] = copy(p, 4 * k + 3 + d, view, view, moved(spot, axis, 1 - 2 * d))
    for p in range(2):
        made[p, 7].wait_recv()
        made[p, 8].wait_recv()
    for each in made.values():
        each.wait_send()


def kv_gather(shard, collective_id):
    return pl.pallas_call(
        kv_gather_kernel,
        out_shape=jax.ShapeDtypeStruct((2, 2, 4, 4, 64, 512), shard.dtype),
        in_specs=[pl.BlockSpec(memory_space=pltpu.VMEM)],
        out_specs=pl.BlockSpec(memory_space=pltpu.VMEM),
        scratch_shapes=[
            pltpu.SemaphoreType.DMA,
            pltpu.SemaphoreType.DMA((2, 9)),
            pltpu.SemaphoreType.DMA((2, 9)),
        ],
        compiler_params=pltpu.CompilerParams(
            collective_id=collective_id, has_side_effects=True, vmem_limit_bytes=32 * 1024 * 1024),
    )(shard)


def kv_scatter_kernel(terms, got, s1, r1, s2, r2, s3, r3, s4, r4, s5, r5, acc, acc2, send, recv):
    spot = place()
    x, y, z, c = spot
    xh = x // 2
    kv_meet(spot)
    bf, f32 = jnp.bfloat16, jnp.float32
    cols = [slice(0, 256), slice(256, 512)]
    axes = [(2, 1), (1, 2)]

    def copy(stage, p, d, src, dst, to):
        made = pltpu.make_async_remote_copy(
            src, dst, send.at[stage, p, d], recv.at[stage, p, d], device_id=ident(*to), device_id_type=MESH)
        made.start()
        return made

    def block(p, m, at):
        if p == 0:
            return terms[m, :, :, at, :, cols[p]]
        return terms[m, :, at, :, :, cols[p]]

    made = {}
    for p in range(2):
        axis = axes[p][0]
        for d in (0, 1):
            s1[p, d] = block(p, d, (spot[axis] + 2) % 4)
            made[1, p, d] = copy(0, p, d, s1.at[p, d], r1.at[p, d], moved(spot, axis, 1 - 2 * d))
    for p in range(2):
        axis = axes[p][0]
        for d in (0, 1):
            near = (spot[axis] + 1 + 2 * d) % 4
            made[1, p, d].wait_recv()
            s2[p, d, d] = (block(p, d, near).astype(f32) + r1[p, d].astype(f32)).astype(bf)
            s2[p, d, 1 - d] = block(p, 1 - d, near)
            made[2, p, d] = copy(1, p, d, s2.at[p, d], r2.at[p, d], moved(spot, axis, 1 - 2 * d))
    for p in range(2):
        made[2, p, 0].wait_recv()
        made[2, p, 1].wait_recv()
        for m in (0, 1):
            acc[p, m] = (block(p, m, spot[axes[p][0]]).astype(f32)
                         + r2[p, 0, m].astype(f32) + r2[p, 1, m].astype(f32))
        axis = axes[p][1]
        for d in (0, 1):
            s3[p, d] = acc[p, d, :, (spot[axis] + 2) % 4].astype(bf)
            made[3, p, d] = copy(2, p, d, s3.at[p, d], r3.at[p, d], moved(spot, axis, 1 - 2 * d))
    for p in range(2):
        axis = axes[p][1]
        for d in (0, 1):
            near = (spot[axis] + 1 + 2 * d) % 4
            made[3, p, d].wait_recv()
            s4[p, d, d] = (acc[p, d, :, near] + r3[p, d].astype(f32)).astype(bf)
            s4[p, d, 1 - d] = acc[p, 1 - d, :, near].astype(bf)
            made[4, p, d] = copy(3, p, d, s4.at[p, d], r4.at[p, d], moved(spot, axis, 1 - 2 * d))
    for p in range(2):
        axis = axes[p][1]
        made[4, p, 0].wait_recv()
        made[4, p, 1].wait_recv()
        acc2[p] = acc[p, :, :, spot[axis]] + r4[p, 0].astype(f32) + r4[p, 1].astype(f32)
        s5[p] = acc2[p, :, 1 - xh].astype(bf)
        made[5, p, 0] = copy(4, p, 0, s5.at[p], r5.at[p], moved(spot, 0, 2))
    for p in range(2):
        made[5, p, 0].wait_recv()
        got[:, :, cols[p]] = acc2[p, :, xh] + r5[p].astype(f32)
    for each in made.values():
        each.wait_send()


def kv_scatter(terms, collective_id):
    bf, f32 = jnp.bfloat16, jnp.float32
    v = pltpu.VMEM
    return pl.pallas_call(
        kv_scatter_kernel,
        out_shape=jax.ShapeDtypeStruct((2, 64, 512), f32),
        in_specs=[pl.BlockSpec(memory_space=pltpu.VMEM)],
        out_specs=pl.BlockSpec(memory_space=pltpu.VMEM),
        scratch_shapes=[
            v((2, 2, 2, 4, 64, 256), bf), v((2, 2, 2, 4, 64, 256), bf),
            v((2, 2, 2, 2, 4, 64, 256), bf), v((2, 2, 2, 2, 4, 64, 256), bf),
            v((2, 2, 2, 64, 256), bf), v((2, 2, 2, 64, 256), bf),
            v((2, 2, 2, 2, 64, 256), bf), v((2, 2, 2, 2, 64, 256), bf),
            v((2, 2, 64, 256), bf), v((2, 2, 64, 256), bf),
            v((2, 2, 2, 4, 64, 256), f32), v((2, 2, 2, 64, 256), f32),
            pltpu.SemaphoreType.DMA((5, 2, 2)),
            pltpu.SemaphoreType.DMA((5, 2, 2)),
        ],
        compiler_params=pltpu.CompilerParams(
            collective_id=collective_id, has_side_effects=True, vmem_limit_bytes=48 * 1024 * 1024),
    )(terms)


BK = 512
ROWS = 512
HD = 64
KV = 4


def last(left, right):
    return lax.dot_general(left, right, (((1,), (1,)), ((), ())), preferred_element_type=jnp.float32)


def first(left, right):
    return lax.dot_general(left, right, (((0,), (0,)), ((), ())), preferred_element_type=jnp.float32)


def allowed_in(block, start, spot):
    columns = block * BK + lax.broadcasted_iota(jnp.int32, (ROWS, BK), 1)
    return (columns >= start) & (columns <= spot)


def forward_kernel(bounds, q, kv, marks, out, lse, top, total):
    micro = pl.program_id(0)
    start, spot = marks[0, :, 0:1], marks[0, :, 1:2]
    top[...] = jnp.full_like(top, -1e30)
    total[...] = jnp.zeros_like(total)
    out[...] = jnp.zeros_like(out)

    def step(block, carry):
        keep = allowed_in(block, start, spot)
        rows = pl.ds(pl.multiple_of(block * BK, BK), BK)
        for h in range(KV):
            s = last(q[0, h], kv[0, rows, h * HD : (h + 1) * HD]) * (HD**-0.5)
            s = jnp.where(keep, s, -1e30)
            high = jnp.maximum(top[h], jnp.max(s, axis=1, keepdims=True))
            fade = jnp.exp(top[h] - high)
            e = jnp.where(keep, jnp.exp(s - high), 0.0)
            total[h] = total[h] * fade + jnp.sum(e, axis=1, keepdims=True)
            out[0, h] = out[0, h] * fade + jnp.dot(
                e.astype(jnp.bfloat16), kv[0, rows, 256 + h * HD : 256 + (h + 1) * HD],
                preferred_element_type=jnp.float32)
            top[h] = high
        return carry

    lax.fori_loop(bounds[micro, 0], bounds[micro, 1], step, 0)
    for h in range(KV):
        out[0, h] = out[0, h] / total[h]
        lse[0, h] = top[h] + jnp.log(total[h])


def backward_kernel(bounds, q, kv, marks, out, lse, dout, dq, terms, lean):
    micro = pl.program_id(0)
    start, spot = marks[0, :, 0:1], marks[0, :, 1:2]
    dq[...] = jnp.zeros_like(dq)
    terms[...] = jnp.zeros_like(terms)
    for h in range(KV):
        lean[h] = jnp.sum(out[0, h] * dout[0, h].astype(jnp.float32), axis=1, keepdims=True)

    def step(block, carry):
        keep = allowed_in(block, start, spot)
        rows = pl.ds(pl.multiple_of(block * BK, BK), BK)
        keys, values = [], []
        for h in range(KV):
            k = kv[0, rows, h * HD : (h + 1) * HD]
            v = kv[0, rows, 256 + h * HD : 256 + (h + 1) * HD]
            s = last(q[0, h], k) * (HD**-0.5)
            p = jnp.where(keep, jnp.exp(jnp.where(keep, s - lse[0, h], -1e30)), 0.0)
            dp = last(dout[0, h], v)
            ds = (p * (dp - lean[h])).astype(jnp.bfloat16)
            dq[0, h] += jnp.dot(ds, k, preferred_element_type=jnp.float32) * (HD**-0.5)
            keys.append(first(ds, q[0, h]) * (HD**-0.5))
            values.append(first(p.astype(jnp.bfloat16), dout[0, h]))
        terms[0, rows, :] = jnp.concatenate(keys + values, axis=1).astype(jnp.bfloat16)
        return carry

    lax.fori_loop(bounds[micro, 0], bounds[micro, 1], step, 0)


def each(shape):
    zeros = (0,) * (len(shape) - 1)
    return pl.BlockSpec((1,) + shape[1:], lambda m, b: (m,) + zeros)


def attend(bounds, q, kv, marks):
    f32 = jnp.float32
    shapes = [(2, KV, ROWS, HD), (2, KV, ROWS, 1)]
    return pl.pallas_call(
        forward_kernel,
        out_shape=[jax.ShapeDtypeStruct(s, f32) for s in shapes],
        grid_spec=pltpu.PrefetchScalarGridSpec(
            num_scalar_prefetch=1, grid=(2,),
            in_specs=[each(q.shape), each(kv.shape), each(marks.shape)],
            out_specs=[each(s) for s in shapes],
            scratch_shapes=[pltpu.VMEM((KV, ROWS, 1), f32), pltpu.VMEM((KV, ROWS, 1), f32)],
        ),
        compiler_params=pltpu.CompilerParams(vmem_limit_bytes=48 * 1024 * 1024),
    )(bounds, q, kv, marks)


def attend_back(bounds, q, kv, marks, out, lse, dout):
    f32 = jnp.float32
    shapes = [((2, KV, ROWS, HD), f32), ((2, 2048, 512), jnp.bfloat16)]
    return pl.pallas_call(
        backward_kernel,
        out_shape=[jax.ShapeDtypeStruct(s, d) for s, d in shapes],
        grid_spec=pltpu.PrefetchScalarGridSpec(
            num_scalar_prefetch=1, grid=(2,),
            in_specs=[each(a.shape) for a in (q, kv, marks, out, lse, dout)],
            out_specs=[each(s) for s, _ in shapes],
            scratch_shapes=[pltpu.VMEM((KV, ROWS, 1), f32)],
        ),
        compiler_params=pltpu.CompilerParams(vmem_limit_bytes=48 * 1024 * 1024),
    )(bounds, q, kv, marks, out, lse, dout)


TB = 32
D = 2048
NORM_EPS = 1e-05


def stream(ref, s):
    return ref[:, s * D : (s + 1) * D].astype(jnp.float32)


def weight(mix, k, s, j):
    return mix[k * 24 + s * 6 + j]


def entry_of(parts, mix, k):
    return sum(weight(mix, k, s, 0) * parts[s] for s in range(4))


def normed_of(entry):
    center = entry - jnp.mean(entry, axis=-1, keepdims=True)
    inverse = lax.rsqrt(jnp.mean(center * center, axis=-1, keepdims=True) + NORM_EPS)
    return center * inverse, inverse


def norm_back(grad, normed, inverse):
    return inverse * (
        grad
        - jnp.mean(grad, axis=-1, keepdims=True)
        - normed * jnp.mean(grad * normed, axis=-1, keepdims=True)
    )


def mixed_out(parts, branch, mix, k, t):
    return sum(weight(mix, k, s, 2 + t) * parts[s] for s in range(4)) + weight(mix, k, t, 1) * branch


def inner(a, b):
    both = a * b
    folded = both[:, 0:128]
    for j in range(1, D // 128):
        folded = folded + both[:, j * 128 : (j + 1) * 128]
    return jnp.sum(folded, axis=0, keepdims=True)


def note(ref, row, value):
    ref[row : row + 1, :] += value


def start_notes(ref):
    @pl.when(pl.program_id(0) == 0)
    def _():
        ref[...] = jnp.zeros_like(ref)


def open_kernel(mix, tokens, entry):
    parts = [stream(tokens, s) for s in range(4)]
    entry[...] = normed_of(entry_of(parts, mix, 0))[0].astype(jnp.bfloat16)


def middle_kernel(mix, tokens, branch, middle, entry):
    parts = [stream(tokens, s) for s in range(4)]
    y = branch[...]
    x = None
    for t in range(4):
        out = mixed_out(parts, y, mix, 0, t)
        middle[:, t * D : (t + 1) * D] = out
        term = weight(mix, 1, t, 0) * out
        x = term if x is None else x + term
    entry[...] = normed_of(x)[0].astype(jnp.bfloat16)


def close_kernel(mix, middle, branch, coming, fresh, grad, notes):
    start_notes(notes)
    y = branch[...]
    e = None
    for t in range(4):
        g = stream(coming, t)
        fresh[:, t * D : (t + 1) * D] = mixed_out(
            [stream(middle, s) for s in range(4)], y, mix, 1, t).astype(jnp.bfloat16)
        term = weight(mix, 1, t, 1) * g
        e = term if e is None else e + term
        note(notes, t, inner(y, g))
        for s in range(4):
            note(notes, 4 + 4 * s + t, inner(stream(middle, s), g))
    grad[...] = e.astype(jnp.bfloat16)


def between_kernel(mix, tokens, middle, coming, dn, branch, middle_grad, grad, notes):
    start_notes(notes)
    parts = [stream(middle, s) for s in range(4)]
    normed, inverse = normed_of(entry_of(parts, mix, 1))
    dx = norm_back(dn[...], normed, inverse)
    y = branch[...]
    e = None
    for s in range(4):
        note(notes, s, inner(stream(middle, s), dx))
        g = sum(weight(mix, 1, s, 2 + t) * stream(coming, t) for t in range(4)) + weight(mix, 1, s, 0) * dx
        middle_grad[:, s * D : (s + 1) * D] = g
        term = weight(mix, 0, s, 1) * g
        e = term if e is None else e + term
        note(notes, 4 + s, inner(y, g))
        for r in range(4):
            note(notes, 8 + 4 * r + s, inner(stream(tokens, r), g))
    grad[...] = e.astype(jnp.bfloat16)


def last_kernel(mix, tokens, middle_grad, dn, tokens_grad, notes):
    start_notes(notes)
    parts = [stream(tokens, s) for s in range(4)]
    normed, inverse = normed_of(entry_of(parts, mix, 0))
    dx = norm_back(dn[...], normed, inverse)
    for s in range(4):
        note(notes, s, inner(stream(tokens, s), dx))
        tokens_grad[:, s * D : (s + 1) * D] = (
            sum(weight(mix, 0, s, 2 + t) * stream(middle_grad, t) for t in range(4)) + weight(mix, 0, s, 0) * dx)


def call(kernel, mix, arrays, outs, notes=0):
    rows = arrays[0].shape[0]
    shapes = [jax.ShapeDtypeStruct((rows, n), d) for n, d in outs]
    specs = [pl.BlockSpec((TB, n), lambda i: (i, 0)) for n, _ in outs]
    if notes:
        shapes.append(jax.ShapeDtypeStruct((notes, 128), jnp.float32))
        specs.append(pl.BlockSpec((notes, 128), lambda i: (0, 0)))
    return pl.pallas_call(
        kernel,
        out_shape=shapes,
        grid=(rows // TB,),
        in_specs=[pl.BlockSpec(memory_space=pltpu.SMEM)]
        + [pl.BlockSpec((TB, a.shape[1]), lambda i: (i, 0)) for a in arrays],
        out_specs=specs,
        compiler_params=pltpu.CompilerParams(vmem_limit_bytes=48 * 1024 * 1024),
    )(mix, *arrays)


def rotary(values, spots, sign):
    half = values.shape[-1] // 2
    freq = jnp.exp(
        jnp.arange(half, dtype=jnp.float32) * (-2.0 * math.log(THETA_BASE) / values.shape[-1])
    )
    angle = spots[:, None] * freq[None, :]
    cosine = jnp.cos(angle)[:, None, :]
    sine = sign * jnp.sin(angle)[:, None, :]
    first_half = values[..., :half]
    second_half = values[..., half:]
    return jnp.concatenate(
        [first_half * cosine - second_half * sine, second_half * cosine + first_half * sine], axis=-1
    )


def adam(weight, grad, first, second, factor, rate, decay):
    grad = grad * factor
    first = BETA_ONE * first + (1.0 - BETA_ONE) * grad
    second = BETA_TWO * second + (1.0 - BETA_TWO) * grad * grad
    ahead = first / (1.0 - BETA_ONE**STEP)
    scaled = second / (1.0 - BETA_TWO**STEP)
    weight = weight - rate * (ahead / (jnp.sqrt(scaled) + ADAM_EPS) + decay * weight)
    return (weight, first, second)


def padded(columns):
    shape = columns.shape[:-1]
    split = columns.reshape(shape + (128, 44))
    split = jnp.pad(split, ((0, 0),) * len(shape) + ((0, 0), (0, 4)))
    return split.reshape(shape + (128 * 48,))


def unpadded(columns):
    shape = columns.shape[:-1]
    return columns.reshape(shape + (128, 48))[..., :44].reshape(shape + (FF,))


def head_rows(flat):
    return flat.reshape(2, 64, KV, 8, HD).transpose(0, 2, 3, 1, 4).reshape(2, KV, ROWS, HD)


def head_flat(rows):
    return rows.reshape(2, KV, 8, 64, HD).transpose(0, 3, 1, 2, 4).reshape(128, 2048)


def left_side(tokens_by_rows, subs):
    turned = tokens_by_rows.T.reshape(2, 4, 4, 2, 2, subs, 16, 128)
    return turned.transpose(4, 5, 0, 3, 1, 2, 6, 7).reshape(2, subs, 4, 4, 4, 16, 128)


def body(streams, doc_start, cotangent, mixing, w_project, w_output, w_expand, w_reduce,
         first_mixing, second_mixing, first_project, second_project, first_output, second_output,
         first_expand, second_expand, first_reduce, second_reduce):
    bf, f32 = jnp.bfloat16, jnp.float32
    anchor = lax.axis_index("ctx") * 64
    tokens = streams.reshape(128, 8192)
    coming = cotangent.reshape(128, 8192)
    starts = doc_start.reshape(2, 64)
    places = anchor + jnp.arange(64, dtype=jnp.int32)
    spots = (places[None, :] - starts).astype(f32).reshape(128)
    mix = mixing.reshape(48)

    bf_expand = w_expand.astype(bf)
    shards = [
        w_project.astype(bf),
        w_output.astype(bf),
        jnp.concatenate([padded(bf_expand[:, :FF]), padded(bf_expand[:, FF:])], axis=1),
        jnp.pad(w_reduce.astype(bf), ((0, 4), (0, 0))),
    ]
    gathered = gather(shards, 1)
    project, output, expand = (g.reshape(2048, g.shape[-1]) for g in gathered[:3])
    reduce = gathered[3].reshape(6144, 2048)

    (entry_one,) = call(open_kernel, mix, [tokens], [(2048, bf)])
    joined = jnp.dot(entry_one, project, preferred_element_type=f32)
    query = head_rows(rotary(joined[:, :2048].reshape(128, H, HD), spots, 1.0).astype(bf).reshape(128, 2048))
    keys = rotary(joined[:, 2048:2304].reshape(128, KV, HD), spots, 1.0).astype(bf).reshape(128, 256)
    own = jnp.concatenate([keys, joined[:, 2304:].astype(bf)], axis=1).reshape(2, 64, 512)
    kv = kv_gather(own, 2).reshape(2, 2048, 512)
    bounds = jnp.stack([starts[:, 0] // BK, jnp.broadcast_to((anchor + 63) // BK + 1, (2,))], axis=1).astype(jnp.int32)
    marks = jnp.stack([jnp.tile(starts, (1, 8)), jnp.broadcast_to(jnp.tile(places, 8), (2, ROWS))], axis=2)
    mixed, lse = attend(bounds, query, kv, marks)
    attended = head_flat(mixed.astype(bf))
    branch_one = jnp.dot(attended, output, preferred_element_type=f32)
    middle, entry_two = call(middle_kernel, mix, [tokens, branch_one], [(8192, f32), (2048, bf)])
    opened = jnp.dot(entry_two, expand, preferred_element_type=f32)
    gate, upper = opened[:, :6144], opened[:, 6144:]
    sigma = jax.nn.sigmoid(gate)
    hidden = (gate * sigma * upper).astype(bf)
    branch_two = jnp.dot(hidden, reduce, preferred_element_type=f32)
    fresh, grad_two, notes_two = call(
        close_kernel, mix, [middle, branch_two, coming], [(8192, bf), (2048, bf)], 24)

    back_hidden = lax.dot_general(grad_two, reduce, (((1,), (1,)), ((), ())), preferred_element_type=f32)
    opened_grad = jnp.concatenate(
        [back_hidden * upper * sigma * (1.0 + gate * (1.0 - sigma)), back_hidden * gate * sigma], axis=1).astype(bf)
    dn_two = lax.dot_general(opened_grad, expand, (((1,), (1,)), ((), ())), preferred_element_type=f32)
    middle_grad, grad_one, notes_one = call(
        between_kernel, mix, [tokens, middle, coming, dn_two, branch_one], [(8192, f32), (2048, bf)], 24)
    attended_grad = lax.dot_general(
        grad_one, output, (((1,), (1,)), ((), ())), preferred_element_type=f32).astype(bf)
    query_grad, terms = attend_back(bounds, query, kv, marks, mixed, lse, head_rows(attended_grad))
    kv_grad = kv_scatter(terms.reshape(2, 2, 4, 4, 64, 512), 3).reshape(128, 512)
    joined_grad = jnp.concatenate(
        [
            rotary(head_flat(query_grad).reshape(128, H, HD), spots, -1.0).reshape(128, 2048),
            rotary(kv_grad[:, :256].reshape(128, KV, HD), spots, -1.0).reshape(128, 256),
            kv_grad[:, 256:],
        ], axis=1).astype(bf)
    dn_one = lax.dot_general(joined_grad, project, (((1,), (1,)), ((), ())), preferred_element_type=f32)
    tokens_grad, notes_zero = call(last_kernel, mix, [tokens, middle_grad, dn_one], [(8192, f32)], 8)

    zero, one, two = (jnp.sum(n, axis=1) for n in (notes_zero, notes_one, notes_two))
    mix_grad = jnp.stack([
        jnp.concatenate([zero[:4, None], one[4:8, None], one[8:24].reshape(4, 4)], axis=1),
        jnp.concatenate([one[:4, None], two[:4, None], two[4:20].reshape(4, 4)], axis=1),
    ])
    vector = jnp.pad(mix_grad.reshape(1, 48), ((0, 7), (0, 80)))
    lhs = jnp.concatenate(
        [left_side(hidden, 3), left_side(entry_two, 1), left_side(attended, 1), left_side(entry_one, 1)], axis=1)
    rhs = jnp.concatenate([grad_two, opened_grad, grad_one, joined_grad], axis=1)
    grads, total = scatter(lhs, rhs, vector, 4)

    def units(lo, hi):
        return grads[lo:hi].transpose(1, 0, 2).reshape(16, (hi - lo) * W)

    reduce_grad = grads[:12].reshape(3, 4, 16, W).transpose(0, 2, 1, 3).reshape(48, 2048)[:44]
    expand_grad = units(12, 36)
    expand_grad = jnp.concatenate([unpadded(expand_grad[:, :6144]), unpadded(expand_grad[:, 6144:])], axis=1)
    output_grad = units(36, 40)
    project_grad = units(40, 45)
    mix_total = total[0, :48].reshape(2, 4, 6)
    norm = jnp.sqrt(jnp.sum(total[7]) + jnp.sum(mix_total * mix_total))
    factor = THRESHOLD / jnp.maximum(norm, THRESHOLD)
    mix_new = adam(mixing, mix_total, first_mixing, second_mixing, factor, RATE_MIXING, 0.0)
    proj_new = adam(w_project, project_grad, first_project, second_project, factor, RATE_MATRIX, DECAY_MATRIX)
    outp_new = adam(w_output, output_grad, first_output, second_output, factor, RATE_MATRIX, DECAY_MATRIX)
    expd_new = adam(w_expand, expand_grad, first_expand, second_expand, factor, RATE_MATRIX, DECAY_MATRIX)
    redc_new = adam(w_reduce, reduce_grad, first_reduce, second_reduce, factor, RATE_MATRIX, DECAY_MATRIX)
    return (fresh.reshape(streams.shape), tokens_grad.reshape(streams.shape), norm,
            *mix_new, *proj_new, *outp_new, *expd_new, *redc_new)


def solution(mesh):
    acts = P(None, "fsdp", "ctx", None, None)
    rows = P(("ctx", "fsdp"), None)
    return jax.shard_map(
        body,
        mesh=mesh,
        in_specs=(acts, P(None, "fsdp", "ctx"), acts, P()) + (rows,) * 4 + (P(), P()) + (rows,) * 8,
        out_specs=(acts, acts, P(), P(), P(), P()) + (rows,) * 12,
        check_vma=False,
    )
```

```python
import functools
import math

import jax
import jax.numpy as jnp
from jax import lax
from jax.experimental import pallas as pl
from jax.experimental.pallas import tpu as pltpu
from jax.sharding import PartitionSpec as P

H = 32
FF = 5632
STEP = 10
THETA_BASE = 10000.0
BETA_ONE = 0.9
BETA_TWO = 0.95
ADAM_EPS = 1e-08
RATE_MATRIX = 0.06
RATE_MIXING = 0.5
DECAY_MATRIX = 0.1
THRESHOLD = 1.0


MESH = pl.DeviceIdType.MESH


def place():
    ctx = lax.axis_index("ctx")
    fsdp = lax.axis_index("fsdp")
    return (2 * (ctx // 16) + fsdp // 2, (ctx // 4) % 4, ctx % 4, fsdp % 2)


def ident(x, y, z, c):
    return ((x // 2) * 16 + y * 4 + z, (x % 2) * 2 + c)


def moved(spot, axis, step):
    spot = list(spot)
    spot[axis] = (spot[axis] + step + 4) % 4
    return tuple(spot)


def box(spot, known, axis=None, at=None):
    x, y, z, c = spot
    place = [x, y, z]
    if axis is not None:
        place[axis] = at
    index = []
    for d in range(3):
        whole = d in known
        if d == 0:
            xs = (slice(None), slice(None)) if whole else (place[0] // 2, place[0] % 2)
        elif whole:
            index.append(slice(None))
        else:
            index.append(place[d])
    return (xs[0], index[0], index[1], xs[1])


ROWS = 512
HD = 64
KV = 4


def last(left, right):
    return lax.dot_general(left, right, (((1,), (1,)), ((), ())), preferred_element_type=jnp.float32)


def first(left, right):
    return lax.dot_general(left, right, (((0,), (0,)), ((), ())), preferred_element_type=jnp.float32)


TB = 32
D = 2048
NORM_EPS = 1e-05


def stream(ref, s):
    return ref[:, s * D : (s + 1) * D].astype(jnp.float32)


def weight(mix, k, s, j):
    return mix[k * 24 + s * 6 + j]


def entry_of(parts, mix, k):
    return sum(weight(mix, k, s, 0) * parts[s] for s in range(4))


def normed_of(entry):
    center = entry - jnp.mean(entry, axis=-1, keepdims=True)
    inverse = lax.rsqrt(jnp.mean(center * center, axis=-1, keepdims=True) + NORM_EPS)
    return center * inverse, inverse


def norm_back(grad, normed, inverse):
    return inverse * (
        grad
        - jnp.mean(grad, axis=-1, keepdims=True)
        - normed * jnp.mean(grad * normed, axis=-1, keepdims=True)
    )


def mixed_out(parts, branch, mix, k, t):
    return sum(weight(mix, k, s, 2 + t) * parts[s] for s in range(4)) + weight(mix, k, t, 1) * branch


def inner(a, b):
    both = a * b
    folded = both[:, 0:128]
    for j in range(1, D // 128):
        folded = folded + both[:, j * 128 : (j + 1) * 128]
    return jnp.sum(folded, axis=0, keepdims=True)


def note(ref, row, value):
    ref[row : row + 1, :] += value


def start_notes(ref):
    @pl.when(pl.program_id(0) == 0)
    def _():
        ref[...] = jnp.zeros_like(ref)


def close_kernel(mix, middle, branch, coming, fresh, notes):
    start_notes(notes)
    y = branch[...]
    for t in range(4):
        g = stream(coming, t)
        fresh[:, t * D : (t + 1) * D] = mixed_out(
            [stream(middle, s) for s in range(4)], y, mix, 1, t).astype(jnp.bfloat16)
        note(notes, t, inner(y, g))
        for s in range(4):
            note(notes, 4 + 4 * s + t, inner(stream(middle, s), g))


def between_kernel(mix, tokens, middle, coming, dn, branch, middle_grad, grad, notes):
    start_notes(notes)
    parts = [stream(middle, s) for s in range(4)]
    normed, inverse = normed_of(entry_of(parts, mix, 1))
    dx = norm_back(dn[...], normed, inverse)
    y = branch[...]
    e = None
    for s in range(4):
        note(notes, s, inner(stream(middle, s), dx))
        g = sum(weight(mix, 1, s, 2 + t) * stream(coming, t) for t in range(4)) + weight(mix, 1, s, 0) * dx
        middle_grad[:, s * D : (s + 1) * D] = g
        term = weight(mix, 0, s, 1) * g
        e = term if e is None else e + term
        note(notes, 4 + s, inner(y, g))
        for r in range(4):
            note(notes, 8 + 4 * r + s, inner(stream(tokens, r), g))
    grad[...] = e.astype(jnp.bfloat16)


def call(kernel, mix, arrays, outs, notes=0):
    rows = arrays[0].shape[0]
    shapes = [jax.ShapeDtypeStruct((rows, n), d) for n, d in outs]
    specs = [pl.BlockSpec((TB, n), lambda i: (i, 0)) for n, _ in outs]
    if notes:
        shapes.append(jax.ShapeDtypeStruct((notes, 128), jnp.float32))
        specs.append(pl.BlockSpec((notes, 128), lambda i: (0, 0)))
    return pl.pallas_call(
        kernel,
        out_shape=shapes,
        grid=(rows // TB,),
        in_specs=[pl.BlockSpec(memory_space=pltpu.SMEM)]
        + [pl.BlockSpec((TB, a.shape[1]), lambda i: (i, 0)) for a in arrays],
        out_specs=specs,
        compiler_params=pltpu.CompilerParams(vmem_limit_bytes=48 * 1024 * 1024),
    )(mix, *arrays)


W = 512
HALF = 256
UNITS = 45
CHUNKS = 15
SLOTS = 2
STAGES = 6
COLS = 2048 + 12288 + 2048 + 2560
JOINED = 16384
KB = 512
KEY_SCALE = HD**-0.5


def unit_spot(u):
    early = u // 12
    early = 1 - (1 // (1 + early))
    left = (1 - early) * (u // 4) + early * (3 + u // 36 + u // 40)
    column = (1 - early) * ((u % 4) * W) + early * (2048 + (u - 12) * W)
    return left, pl.multiple_of(column, W)


def turned(x, cosine, sine):
    lane = lax.broadcasted_iota(jnp.int32, x.shape, 1)
    swapped = jnp.where(lane % HD < HD // 2, pltpu.roll(x, x.shape[1] - HD // 2, 1), pltpu.roll(x, HD // 2, 1))
    return x * cosine + swapped * sine


def backward_pass(lhs, rhs, grad_one, query, dout, kv, stats, cosine, sine, project, tokens, middle_grad, mix, notes_in,
                  grads, tokens_grad, total, left, right, acc1, acc2,
                  sa, ra, sb, rb, sc, rc, sd, rd, se, re, sf, rf, vsend, vrecv, out,
                  dq, terms, k1, k2, k3s, k3, k4s, k4, k5s, k5, kacc, kacc2, dn, notes,
                  send_sem, recv_sem, free_sem, local_sem, side_send, side_recv, out_sem, v_send_sem, v_recv_sem,
                  k_send, k_recv, tile_sem, late_send, late_recv):
    bf = jnp.bfloat16
    f32 = jnp.float32
    spot = place()
    x, y, z, c = spot
    pos = (x, y, z)
    xh = x // 2
    anchor = ((xh * 4 + y) * 4 + z) * 64
    sibling = (x, y, z, 1 - c)
    barrier = pltpu.get_barrier_semaphore()
    others = [sibling] + [moved(spot, axis, step) for axis in range(3) for step in (1, 2, 3)]
    for other in others:
        pl.semaphore_signal(barrier, inc=1, device_id=ident(*other), device_id_type=MESH)
    pl.semaphore_wait(barrier, len(others))

    parts = (((0, 3), (0, 2048)), ((3, 4), (2048, 14336)), ((4, 6), (14336, JOINED)))
    moves = []
    for j, ((l0, l1), (c0, c1)) in enumerate(parts):
        source = grad_one if j == 2 else rhs.at[:, c0:c1]
        own = [
            pltpu.make_async_copy(lhs.at[c, l0:l1], left.at[l0:l1, :, :, :, :, 0:128], local_sem.at[j, 0]),
            pltpu.make_async_copy(source, right.at[0:128, c0:c1], local_sem.at[j, 1]),
        ]
        far = [
            pltpu.make_async_remote_copy(
                lhs.at[1 - c, l0:l1], left.at[l0:l1, :, :, :, :, 128:256], side_send.at[j, 0], side_recv.at[j, 0],
                device_id=ident(*sibling), device_id_type=MESH),
            pltpu.make_async_remote_copy(
                source, right.at[128:256, c0:c1], side_send.at[j, 1], side_recv.at[j, 1],
                device_id=ident(*sibling), device_id_type=MESH),
        ]
        for copy in own + far:
            copy.start()
        moves.append((own, far))
    late = pltpu.make_async_remote_copy(
        right.at[0:128, JOINED:COLS], right.at[128:256, JOINED:COLS], late_send, late_recv,
        device_id=ident(*sibling), device_id_type=MESH)

    def arrive(j):
        for copy in moves[j][0]:
            copy.wait()
        for copy in moves[j][1]:
            copy.wait_recv()

    arrive(0)
    dq[...] = jnp.zeros_like(dq)
    notes[...] = jnp.zeros_like(notes)

    sends = (sa, sb, sc, sd, se, sf)
    recvs = (ra, rb, rc, rd, re, rf)

    def hop(stage, p, d, slot):
        axis = (p + stage // 2) % 3
        return pltpu.make_async_remote_copy(
            sends[stage].at[p, d, slot], recvs[stage].at[p, d, slot],
            send_sem.at[stage, p, d, slot], recv_sem.at[stage, p, d, slot],
            device_id=ident(*moved(spot, axis, 1 - 2 * d)), device_id_type=MESH)

    def before_send(stage, p, q):
        @pl.when(q >= SLOTS)
        def _():
            for d in (0, 1):
                hop(stage, p, d, q % SLOTS).wait_send()
                pl.semaphore_wait(free_sem.at[stage, p, d], 1)

    def give_back(stage, p, q):
        @pl.when(q < CHUNKS - SLOTS)
        def _():
            axis = (p + stage // 2) % 3
            for d in (0, 1):
                pl.semaphore_signal(free_sem.at[stage, p, d], inc=1,
                                    device_id=ident(*moved(spot, axis, 2 * d - 1)), device_id_type=MESH)

    def go(stage, p, q):
        for d in (0, 1):
            hop(stage, p, d, q % SLOTS).start()

    def come(stage, p, q):
        for d in (0, 1):
            hop(stage, p, d, q % SLOTS).wait_recv()

    def rows(p, l, a):
        if p == 0:
            got = left[l, a]
        elif p == 1:
            got = left[l, :, a]
        else:
            got = left[l, :, :, a]
        return got.reshape(256, 256)

    def product(p, q, a, lo, hi):
        l, column = unit_spot(3 * q + p)
        return jnp.dot(rows(p, l, a), right[:, pl.ds(pl.multiple_of(column + lo, HALF), hi - lo)],
                       preferred_element_type=f32)

    def at(p, step):
        return (pos[p] + step + 4) % 4

    def stage1(q):
        s = q % SLOTS
        for p in range(3):
            before_send(0, p, q)
            for d in (0, 1):
                sa[p, d, s] = product(p, q, at(p, 2), d * HALF, d * HALF + HALF).astype(bf)
            go(0, p, q)

    def stage2(q):
        s = q % SLOTS
        for p in range(3):
            before_send(1, p, q)
            come(0, p, q)
            for d in (0, 1):
                lo = d * HALF
                near = at(p, 1 - 2 * d)
                sb[p, d, s, :, lo : lo + HALF] = (
                    product(p, q, near, lo, lo + HALF) + ra[p, d, s].astype(f32)).astype(bf)
                other = HALF - lo
                sb[p, d, s, :, other : other + HALF] = product(p, q, near, other, other + HALF).astype(bf)
            give_back(0, p, q)
            go(1, p, q)

    def part(p, ref, b):
        return ref.at[:, b] if p == 1 else ref.at[b]

    def stage3(q):
        s = q % SLOTS
        for p in range(3):
            come(1, p, q)
            for lo in (0, HALF):
                both = (product(p, q, pos[p], lo, lo + HALF)
                        + rb[p, 0, s, :, lo : lo + HALF].astype(f32) + rb[p, 1, s, :, lo : lo + HALF].astype(f32))
                acc1[p, s, :, :, :, lo : lo + HALF] = both.reshape(4, 4, 16, HALF)
            give_back(1, p, q)
            before_send(2, p, q)
            ahead = at((p + 1) % 3, 2)
            for d in (0, 1):
                sc[p, d, s] = part(p, acc1.at[p, s], ahead)[:, :, d * HALF : d * HALF + HALF].astype(bf)
            go(2, p, q)

    def stage4(q):
        s = q % SLOTS
        for p in range(3):
            before_send(3, p, q)
            come(2, p, q)
            for d in (0, 1):
                lo = d * HALF
                other = HALF - lo
                mine = part(p, acc1.at[p, s], at((p + 1) % 3, 1 - 2 * d))
                sd[p, d, s, :, :, lo : lo + HALF] = (
                    mine[:, :, lo : lo + HALF] + rc[p, d, s].astype(f32)).astype(bf)
                sd[p, d, s, :, :, other : other + HALF] = mine[:, :, other : other + HALF].astype(bf)
            give_back(2, p, q)
            go(3, p, q)

    def stage5(q):
        s = q % SLOTS
        for p in range(3):
            come(3, p, q)
            acc2[p, s] = (part(p, acc1.at[p, s], pos[(p + 1) % 3])[...]
                          + rd[p, 0, s].astype(f32) + rd[p, 1, s].astype(f32))
            give_back(3, p, q)
            before_send(4, p, q)
            ahead = at((p + 2) % 3, 2)
            for d in (0, 1):
                se[p, d, s] = acc2[p, s, ahead, :, d * HALF : d * HALF + HALF].astype(bf)
            go(4, p, q)

    def stage6(q):
        s = q % SLOTS
        for p in range(3):
            before_send(5, p, q)
            come(4, p, q)
            for d in (0, 1):
                lo = d * HALF
                other = HALF - lo
                near = at((p + 2) % 3, 1 - 2 * d)
                sf[p, d, s, :, lo : lo + HALF] = (
                    acc2[p, s, near, :, lo : lo + HALF] + re[p, d, s].astype(f32)).astype(bf)
                sf[p, d, s, :, other : other + HALF] = acc2[p, s, near, :, other : other + HALF].astype(bf)
            give_back(4, p, q)
            go(5, p, q)

    def stage7(q):
        s = q % SLOTS
        for p in range(3):
            come(5, p, q)
            out[3 * q + p] = (acc2[p, s, pos[(p + 2) % 3]]
                              + rf[p, 0, s].astype(f32) + rf[p, 1, s].astype(f32))
            give_back(5, p, q)

    def attend(m, block):
        where = (m, block // 2, pl.ds((block % 2) * 2, 2))

        @pl.when(block * KB <= anchor + 63)
        def _():
            columns = (block * KB + lax.broadcasted_iota(jnp.int32, (ROWS, KB), 1)).astype(f32)
            keep = (columns >= stats[m, :, 8:9]) & (columns <= stats[m, :, 9:10])
            span = pl.ds(pl.multiple_of(block * KB, KB), KB)
            keys, values, queries = [], [], []
            for h in range(KV):
                lanes = slice(h * HD, (h + 1) * HD)
                k = kv[m, span, lanes]
                v = kv[m, span, 256 + h * HD : 256 + (h + 1) * HD]
                qh = query[m, :, lanes]
                doh = dout[m, :, lanes]
                s = last(qh, k) * KEY_SCALE
                p = jnp.exp(jnp.where(keep, s - stats[m, :, h : h + 1], -1e30))
                ds = (p * (last(doh, v) - stats[m, :, 4 + h : 5 + h])).astype(bf)
                queries.append(jnp.dot(ds, k, preferred_element_type=f32) * KEY_SCALE)
                keys.append(first(ds, qh) * KEY_SCALE)
                values.append(first(p.astype(bf), doh))
            dq[m] += jnp.concatenate(queries, axis=1)
            terms[where] = jnp.concatenate(keys + values, axis=1).astype(bf).reshape(2, 4, 64, 512)

        @pl.when(block * KB > anchor + 63)
        def _():
            terms[where] = jnp.zeros((2, 4, 64, 512), bf)

    cols = [slice(0, 256), slice(256, 512)]
    axes = [(2, 1), (1, 2)]

    def view(p, m, a):
        return terms.at[m, :, :, a, :, cols[p]] if p == 0 else terms.at[m, :, a, :, :, cols[p]]

    def khop(stage, p, d):
        if stage == 4:
            src, dst, to = k5s.at[p], k5.at[p], moved(spot, 0, 2)
        else:
            axis = axes[p][stage // 2]
            to = moved(spot, axis, 1 - 2 * d)
            if stage == 0:
                src, dst = view(p, d, (spot[axis] + 2) % 4), k1.at[p, d]
            elif stage == 1:
                src, dst = view(p, slice(None), (spot[axis] + 1 + 2 * d) % 4), k2.at[p, d]
            elif stage == 2:
                src, dst = k3s.at[p, d], k3.at[p, d]
            else:
                src, dst = k4s.at[p, d], k4.at[p, d]
        return pltpu.make_async_remote_copy(
            src, dst, k_send.at[stage, p, d], k_recv.at[stage, p, d], device_id=ident(*to), device_id_type=MESH)

    def terms1():
        for p in range(2):
            for d in (0, 1):
                khop(0, p, d).start()

    def terms2():
        for p in range(2):
            for d in (0, 1):
                khop(0, p, d).wait_recv()
                mine = view(p, d, (spot[axes[p][0]] + 1 + 2 * d) % 4)
                mine[...] = (mine[...].astype(f32) + k1[p, d].astype(f32)).astype(bf)
                khop(1, p, d).start()

    def terms3():
        for p in range(2):
            for d in (0, 1):
                khop(1, p, d).wait_recv()
            for m in (0, 1):
                kacc[p, m] = (view(p, m, spot[axes[p][0]])[...].astype(f32)
                              + k2[p, 0, m].astype(f32) + k2[p, 1, m].astype(f32))
            for d in (0, 1):
                k3s[p, d] = kacc[p, d, :, (spot[axes[p][1]] + 2) % 4].astype(bf)
                khop(2, p, d).start()

    def terms4():
        for p in range(2):
            for d in (0, 1):
                near = (spot[axes[p][1]] + 1 + 2 * d) % 4
                khop(2, p, d).wait_recv()
                k4s[p, d, d] = (kacc[p, d, :, near] + k3[p, d].astype(f32)).astype(bf)
                k4s[p, d, 1 - d] = kacc[p, 1 - d, :, near].astype(bf)
                khop(3, p, d).start()

    def terms5():
        for p in range(2):
            for d in (0, 1):
                khop(3, p, d).wait_recv()
            kacc2[p] = kacc[p, :, :, spot[axes[p][1]]] + k4[p, 0].astype(f32) + k4[p, 1].astype(f32)
            k5s[p] = kacc2[p, :, 1 - xh].astype(bf)
            khop(4, p, 0).start()

    def join():
        for m in (0, 1):
            here = slice(m * 64, m * 64 + 64)
            for g in range(8):
                right[here, JOINED + g * 256 : JOINED + (g + 1) * 256] = turned(
                    dq[m, g * 64 : (g + 1) * 64, :], cosine[m], sine[m]).astype(bf)
        for p in range(2):
            khop(4, p, 0).wait_recv()
        for m in (0, 1):
            here = slice(m * 64, m * 64 + 64)
            right[here, JOINED + 2048 : JOINED + 2304] = turned(
                kacc2[0, m, xh] + k5[0, m].astype(f32), cosine[m], sine[m]).astype(bf)
            right[here, JOINED + 2304 : COLS] = (kacc2[1, m, xh] + k5[1, m].astype(f32)).astype(bf)
        late.start()

    def entry(i):
        def inside(tiles):
            copies = [
                pltpu.make_async_copy(
                    project.at[pl.ds(pl.multiple_of((2 * i + j) * 256, 256), 256)], tiles.at[j], tile_sem.at[j])
                for j in (0, 1)
            ]
            for copy in copies:
                copy.start()
            for j in (0, 1):
                copies[j].wait()
                dn[:, pl.ds(pl.multiple_of((2 * i + j) * 256, 256), 256)] = last(right[0:128, JOINED:COLS], tiles[j])

        pl.run_scoped(inside, pltpu.VMEM((2, 256, 2560), bf))

    def finish(i):
        span = pl.ds(pl.multiple_of(i * 32, 32), 32)

        def inside(held, grad, back):
            ins = [pltpu.make_async_copy(tokens.at[span], held, tile_sem.at[0]),
                   pltpu.make_async_copy(middle_grad.at[span], grad, tile_sem.at[1])]
            for copy in ins:
                copy.start()
            for copy in ins:
                copy.wait()
            normed, inverse = normed_of(entry_of([stream(held, s) for s in range(4)], mix, 0))
            dx = norm_back(dn[span, :], normed, inverse)
            for s in range(4):
                note(notes, s, inner(stream(held, s), dx))
                back[:, s * D : (s + 1) * D] = (
                    sum(weight(mix, 0, s, 2 + t) * stream(grad, t) for t in range(4)) + weight(mix, 0, s, 0) * dx)
            away = pltpu.make_async_copy(back, tokens_grad.at[span], tile_sem.at[0])
            away.start()
            away.wait()

        pl.run_scoped(inside, pltpu.VMEM((32, 4 * D), bf), pltpu.VMEM((32, 4 * D), f32), pltpu.VMEM((32, 4 * D), f32))

    def step(t, carry):
        @pl.when(t == 4)
        def _():
            arrive(1)

        @pl.when(t == 12)
        def _():
            arrive(2)

        @pl.when(t == 13)
        def _():
            late.wait_recv()

        stages = (stage1, stage2, stage3, stage4, stage5, stage6, stage7)
        for lag in (0, 1, 6, 5, 4, 3, 2):
            @pl.when((t >= lag) & (t < CHUNKS + lag))
            def _(lag=lag):
                stages[lag](t - lag)

        @pl.when(t < 4)
        def _():
            attend(t // 2, 2 * (t % 2))
            attend(t // 2, 2 * (t % 2) + 1)

        for when, task in ((4, terms1), (5, terms2), (6, terms3), (7, terms4), (8, terms5), (9, join)):
            pl.when(t == when)(task)

        @pl.when((t >= 10) & (t < 14))
        def _():
            entry(t - 10)

        @pl.when((t >= 14) & (t < 18))
        def _():
            finish(t - 14)
        return carry

    lax.fori_loop(0, CHUNKS + 6, step, 0)

    def tail(q, carry):
        for stage in range(STAGES):
            for p in range(3):
                for d in (0, 1):
                    hop(stage, p, d, q % SLOTS).wait_send()
        return carry

    lax.fori_loop(CHUNKS - SLOTS, CHUNKS, tail, 0)
    for own, far in moves:
        for copy in far:
            copy.wait_send()
    late.wait_send()
    for stage in range(5):
        for p in range(2):
            for d in (0, 1) if stage < 4 else (0,):
                khop(stage, p, d).wait_send()

    write = pltpu.make_async_copy(out, grads, out_sem)
    write.start()

    def squares(u, carry):
        g = out[u]
        return carry + g * g

    summed = lax.fori_loop(0, UNITS, squares, jnp.zeros((16, W), f32))
    lanes = jnp.sum(summed, axis=0, keepdims=True)
    lanes = lanes[:, 0:128] + lanes[:, 128:256] + lanes[:, 256:384] + lanes[:, 384:512]
    last_rows = lax.broadcasted_iota(jnp.int32, (8, 128), 0)
    vector = jnp.concatenate([notes_in[...], notes[...] + jnp.where(last_rows == 7, lanes, 0.0)], axis=0)
    for phase in range(4):
        vsend[phase] = vector
        if phase == 0:
            targets = [(0, sibling)]
        else:
            targets = [(step - 1, moved(spot, phase - 1, step)) for step in (1, 2, 3)]
        copies = [
            pltpu.make_async_remote_copy(
                vsend.at[phase], vrecv.at[phase, k], v_send_sem.at[phase, k], v_recv_sem.at[phase, k],
                device_id=ident(*to), device_id_type=MESH)
            for k, to in targets
        ]
        for copy in copies:
            copy.start()
        for copy in copies:
            copy.wait()
        for k, _ in targets:
            vector = vector + vrecv[phase, k]
    total[...] = vector
    write.wait()


def run_backward(lhs, rhs, grad_one, query, dout, kv, stats, cosine, sine, project, tokens, middle_grad, mix, notes, collective_id):
    bf = jnp.bfloat16
    f32 = jnp.float32
    v = pltpu.VMEM
    dma = pltpu.SemaphoreType.DMA
    pair = lambda shape: [v((3, 2, SLOTS) + shape, bf)] * 2
    hbm = pl.BlockSpec(memory_space=pl.ANY)
    near = pl.BlockSpec(memory_space=pltpu.VMEM)
    return pl.pallas_call(
        backward_pass,
        out_shape=[jax.ShapeDtypeStruct((UNITS, 16, W), f32), jax.ShapeDtypeStruct((128, 4 * D), f32),
                   jax.ShapeDtypeStruct((56, 128), f32)],
        in_specs=[hbm, hbm, hbm, near, near, near, near, near, near, hbm, hbm, hbm,
                  pl.BlockSpec(memory_space=pltpu.SMEM), near],
        out_specs=[hbm, hbm, near],
        scratch_shapes=[
            v((6, 4, 4, 4, 16, 256), bf),
            v((256, COLS), bf),
            v((3, SLOTS, 4, 4, 16, W), f32),
            v((3, SLOTS, 4, 16, W), f32),
            *pair((256, HALF)),
            *pair((256, W)),
            *pair((4, 16, HALF)),
            *pair((4, 16, W)),
            *pair((16, HALF)),
            *pair((16, W)),
            v((4, 56, 128), f32),
            v((4, 3, 56, 128), f32),
            v((UNITS, 16, W), f32),
            v((2, ROWS, 256), f32),
            v((2, 2, 4, 4, 64, 512), bf),
            v((2, 2, 2, 4, 64, 256), bf),
            v((2, 2, 2, 2, 4, 64, 256), bf),
            v((2, 2, 2, 64, 256), bf), v((2, 2, 2, 64, 256), bf),
            v((2, 2, 2, 2, 64, 256), bf), v((2, 2, 2, 2, 64, 256), bf),
            v((2, 2, 64, 256), bf), v((2, 2, 64, 256), bf),
            v((2, 2, 2, 4, 64, 256), f32), v((2, 2, 2, 64, 256), f32),
            v((128, D), f32),
            v((8, 128), f32),
            dma((STAGES, 3, 2, SLOTS)),
            dma((STAGES, 3, 2, SLOTS)),
            pltpu.SemaphoreType.REGULAR((STAGES, 3, 2)),
            dma((3, 2)),
            dma((3, 2)),
            dma((3, 2)),
            dma,
            dma((4, 3)),
            dma((4, 3)),
            dma((5, 2, 2)),
            dma((5, 2, 2)),
            dma((2,)),
            dma,
            dma,
        ],
        compiler_params=pltpu.CompilerParams(
            collective_id=collective_id, has_side_effects=True, vmem_limit_bytes=62 * 1024 * 1024),
    )(lhs, rhs, grad_one, query, dout, kv, stats, cosine, sine, project, tokens, middle_grad, mix, notes)


PARTS = 8
GATE = 1536
QUART = 2 * GATE


def thirds(first, tiles):
    cuts = [0, (tiles + 2) // 3, (tiles + 2) // 3 + (tiles + 1) // 3, tiles]
    out = []
    for a, b in zip(cuts[:-1], cuts[1:]):
        mid = a + (b - a + 1) // 2
        out.append((slice(None), first + a * 128, first + mid * 128, first + b * 128))
    return out


def gather_parts():
    bands = [slice(16 * p, 16 * p + 16) for p in range(3)]
    parts = [(0, thirds(0, 20)), (1, thirds(0, 16))]
    parts += [(2, [(band, n, n + 512, n + 1024) for band in bands]) for n in (0, 1024)]
    parts += [(3, thirds(QUART * j, 24)) for j in range(4)]
    return parts


def pumped(n, source, tiles, sems, use):
    def copy(i):
        return pltpu.make_async_copy(source(i), tiles.at[i % 2], sems.at[i % 2])

    copy(0).start()

    def step(i, carry):
        @pl.when(i + 1 < n)
        def _():
            copy(i + 1).start()

        copy(i).wait()
        use(i, i % 2)
        return carry

    lax.fori_loop(0, n, step, 0)


def forward_pass(w0, w1, w2, w3, tokens, coming, mix, cosine, sine, marks,
                 g0, g1, g2, g3, lhs, rhs, query, kv, rows_out, lse, branch_one, middle, branch_two, dn,
                 entry, lhs_v, rhs_v, top, bottom, dz, joined,
                 own_sem, send, recv, csend, crecv, osend, orecv, k_send, k_recv, tile_sem, out_sem, move_sem):
    bf = jnp.bfloat16
    f32 = jnp.float32
    shards, outs = (w0, w1, w2, w3), (g0, g1, g2, g3)
    spot = place()
    x, y, z, c = spot
    xh = x // 2
    anchor = ((xh * 4 + y) * 4 + z) * 64
    sibling = (x, y, z, 1 - c)
    parts = gather_parts()
    own = []
    for w in range(4):
        copy = pltpu.make_async_copy(shards[w], outs[w].at[xh, y, z, x % 2, c], own_sem.at[w])
        copy.start()
        own.append(copy)
    barrier = pltpu.get_barrier_semaphore()
    others = [sibling, moved(spot, 0, 2)] + [moved(spot, axis, step) for axis in range(3) for step in (1, 3)]
    for other in others:
        pl.semaphore_signal(barrier, inc=1, device_id=ident(*other), device_id_type=MESH)
    pl.semaphore_wait(barrier, len(others))

    def order(p):
        return (p, (p + 1) % 3, (p + 2) % 3)

    def spread(i, p, slot):
        w, pieces = parts[i]
        band, a, _, b = pieces[p]
        k, d = slot // 3, slot % 3
        axis = order(p)[k]
        index = box(spot, order(p)[:k], axis, (spot[axis] + (3, 5, 2)[d]) % 4)
        view = outs[w].at[index + (c, band, slice(a, b))]
        return pltpu.make_async_remote_copy(
            view, view, csend.at[i, p, slot], crecv.at[i, p, slot], device_id=ident(*sibling), device_id_type=MESH)

    def ring(i, p, k, j):
        w, pieces = parts[i]
        band, a, m, b = pieces[p]
        cut = slice(a, b) if j < 2 else slice(a, m) if j == 2 else slice(m, b)
        axis = order(p)[k]
        if j < 2:
            index = box(spot, order(p)[:k])
        else:
            index = box(spot, order(p)[:k], axis, (spot[axis] + 3 + 2 * (j - 2)) % 4)
        view = outs[w].at[index + (c, band, cut)]
        return pltpu.make_async_remote_copy(
            view, view, send.at[i, p, k, j], recv.at[i, p, k, j],
            device_id=ident(*moved(spot, axis, 1 - 2 * (j % 2))), device_id_type=MESH)

    def own_copy(w):
        view = outs[w].at[xh, y, z, x % 2, c]
        return pltpu.make_async_remote_copy(
            view, view, osend.at[w], orecv.at[w], device_id=ident(*sibling), device_id_type=MESH)

    def first_step(i, k):
        for p in range(3):
            if k:
                far_come(i, p, k - 1)
            ring(i, p, k, 0).start()
            ring(i, p, k, 1).start()

    def far_come(i, p, k):
        ring(i, p, k, 2).wait_recv()
        ring(i, p, k, 3).wait_recv()
        spread(i, p, 3 * k + 2).start()

    def second_step(i, k):
        for p in range(3):
            for d in (0, 1):
                ring(i, p, k, d).wait_recv()
                ring(i, p, k, 2 + d).start()
                spread(i, p, 3 * k + d).start()

    def event(i, e):
        if e == 6:
            for p in range(3):
                far_come(i, p, 2)
        elif e % 2:
            second_step(i, e // 2)
        else:
            first_step(i, e // 2)

    queue = []
    for i in range(1, PARTS):
        if i + 1 < PARTS:
            queue += [(i + 1, 2), (i + 1, 3), (i + 1, 4)]
        queue += [(i, 5), (i, 6)]

    def serve(n):
        for _ in range(min(n, len(queue))):
            event(*queue.pop(0))

    def ready(i):
        while (i, 6) in queue:
            serve(1)
        w = parts[i][0]
        if w not in seen:
            seen.append(w)
            own_copy(w).wait_recv()
        for p in range(3):
            for slot in range(9):
                spread(i, p, slot).wait_recv()

    seen = []
    for w in range(4):
        own[w].wait()
        own_copy(w).start()
    for i in range(PARTS):
        event(i, 0)

    def turn(value, l, sub=None):
        flat = value.T.astype(bf).reshape(2, 4, 4, 2, 2, 16, 128)
        for cc in (0, 1):
            for xx in range(4):
                lhs_v[cc, l, xx] = flat[xx // 2, :, :, xx % 2, cc]

    def opening(held, normed_rows):
        ins = [pltpu.make_async_copy(tokens, held.at[0], move_sem.at[0]),
               pltpu.make_async_copy(coming, held.at[1], move_sem.at[1])]
        for copy in ins:
            copy.start()
        for copy in ins:
            copy.wait()

        def step(i, carry):
            span = pl.ds(pl.multiple_of(i * 32, 32), 32)
            block = held.at[0, span]
            normed_rows[span, :] = normed_of(entry_of([stream(block, s) for s in range(4)], mix, 0))[0]
            given = held.at[1, span]
            rhs_v[span, 0:D] = sum(weight(mix, 1, t, 1) * stream(given, t) for t in range(4)).astype(bf)
            return carry

        lax.fori_loop(0, 4, step, 0)
        entry[...] = normed_rows[...].astype(bf)
        turn(normed_rows[...], 5)

    pl.run_scoped(opening, pltpu.VMEM((2, 128, 4 * D), bf), pltpu.VMEM((128, D), f32))
    for i in range(PARTS):
        event(i, 1)
    for e in (2, 3, 4):
        event(0, e)
    for e in (2, 3, 4):
        event(1, e)
    event(0, 5)
    event(0, 6)
    ready(0)

    joined[...] = jnp.zeros_like(joined)

    def project(tiles):
        def use(i, s):
            block = tiles[s].reshape(256, 2560)
            joined[...] += jnp.dot(entry[:, pl.ds(pl.multiple_of(i * 256, 256), 256)], block,
                                   preferred_element_type=f32)

        pumped(8, lambda i: g0.at[i // 4, i % 4], tiles, tile_sem, use)

    pl.run_scoped(project, pltpu.VMEM((2, 4, 2, 2, 16, 2560), bf))
    serve(2)
    for m in (0, 1):
        here = slice(m * 64, m * 64 + 64)
        kv[m, xh, y, z, :, 0:256] = turned(joined[here, 2048:2304], cosine[m], -sine[m]).astype(bf)
        kv[m, xh, y, z, :, 256:512] = joined[here, 2304:2560].astype(bf)

    cols = [slice(0, 256), slice(256, 512)]
    made = {}

    def kv_copy(p, j, view, to):
        copy = pltpu.make_async_remote_copy(
            view, view, k_send.at[p, j], k_recv.at[p, j], device_id=ident(*to), device_id_type=MESH)
        copy.start()
        made[p, j] = copy

    def kv_event(e):
        for p in range(2):
            if e == 0:
                kv_copy(p, 0, kv.at[:, xh, y, z, :, cols[p]], moved(spot, 0, 2))
            elif e in (1, 3):
                k = e // 2
                axis = (1, 2)[(p + k) % 2]
                if k == 0:
                    made[p, 0].wait_recv()
                    view = kv.at[:, :, y, z, :, cols[p]]
                else:
                    made[p, 3].wait_recv()
                    made[p, 4].wait_recv()
                    view = kv.at[:, :, :, z, :, cols[p]] if axis == 2 else kv.at[:, :, y, :, :, cols[p]]
                kv_copy(p, 4 * k + 1, view, moved(spot, axis, 1))
                kv_copy(p, 4 * k + 2, view, moved(spot, axis, -1))
            elif e in (2, 4):
                k = e // 2 - 1
                axis = (1, 2)[(p + k) % 2]
                for d in (0, 1):
                    made[p, 4 * k + 1 + d].wait_recv()
                    near = (spot[axis] + 3 + 2 * d) % 4
                    if k == 0:
                        view = kv.at[d, :, y, near, :, cols[p]] if axis == 2 else kv.at[d, :, near, z, :, cols[p]]
                    else:
                        view = kv.at[d, :, :, near, :, cols[p]] if axis == 2 else kv.at[d, :, near, :, :, cols[p]]
                    kv_copy(p, 4 * k + 3 + d, view, moved(spot, axis, 1 - 2 * d))
            else:
                made[p, 7].wait_recv()
                made[p, 8].wait_recv()

    kv_event(0)
    for m in (0, 1):
        here = slice(m * 64, m * 64 + 64)
        for g in range(8):
            query[m, g * 64 : (g + 1) * 64, :] = turned(
                joined[here, g * 256 : (g + 1) * 256], cosine[m], -sine[m]).astype(bf)
    for e in range(1, 6):
        serve(1)
        kv_event(e)

    def attend(m, block):
        @pl.when(block * KB <= anchor + 63)
        def _():
            columns = (block * KB + lax.broadcasted_iota(jnp.int32, (ROWS, KB), 1)).astype(f32)
            keep = (columns >= marks[m, :, 8:9]) & (columns <= marks[m, :, 9:10])
            held = kv[m, block // 2, (block % 2) * 2 : (block % 2) * 2 + 2].reshape(KB, 512)
            done = []
            for h in range(KV):
                lanes = slice(h * HD, (h + 1) * HD)
                s = jnp.where(keep, last(query[m, :, lanes], held[:, lanes]) * KEY_SCALE, -1e30)
                high = jnp.maximum(top[h], jnp.max(s, axis=1, keepdims=True))
                fade = jnp.exp(top[h] - high)
                e = jnp.where(keep, jnp.exp(s - high), 0.0)
                bottom[h] = bottom[h] * fade + jnp.sum(e, axis=1, keepdims=True)
                done.append(rows_out[m, :, lanes] * fade + jnp.dot(
                    e.astype(bf), held[:, 256 + h * HD : 256 + (h + 1) * HD], preferred_element_type=f32))
                top[h] = high
            rows_out[m] = jnp.concatenate(done, axis=1)

    for m in (0, 1):
        top[...] = jnp.full_like(top, -1e30)
        bottom[...] = jnp.zeros_like(bottom)
        rows_out[m] = jnp.zeros((ROWS, KV * HD), f32)
        for block in range(4):
            attend(m, block)
            serve(1 + block % 2)
        rows_out[m] = jnp.concatenate(
            [rows_out[m, :, h * HD : (h + 1) * HD] / bottom[h] for h in range(KV)], axis=1)
        lse[m] = jnp.concatenate(
            [top[h] + jnp.log(bottom[h]) for h in range(KV)] + [jnp.zeros((ROWS, 124), f32)], axis=1)

    ready(1)
    branch_one[...] = jnp.zeros_like(branch_one)

    def output(tiles):
        def copies(g):
            return [
                pltpu.make_async_copy(g1.at[h // 2, (h % 2) * 2 + g // 4, g % 4], tiles.at[g % 2, h], out_sem.at[g % 2, h])
                for h in range(KV)
            ]

        for copy in copies(0):
            copy.start()
        for g in range(8):
            if g < 7:
                for copy in copies(g + 1):
                    copy.start()
            left = jnp.concatenate([rows_out[m, g * 64 : (g + 1) * 64, :] for m in (0, 1)], axis=0).astype(bf)
            flat = left.astype(f32).T.astype(bf).reshape(4, 2, 2, 16, 128)
            for h in range(KV):
                for cc in (0, 1):
                    for xl in (0, 1):
                        lhs_v[cc, 4, 2 * (h // 2) + xl, (h % 2) * 2 + g // 4, g % 4] = flat[h, xl, cc]
            for copy in copies(g):
                copy.wait()
            branch_one[...] += jnp.dot(left, tiles[g % 2].reshape(256, D), preferred_element_type=f32)

    pl.run_scoped(output, pltpu.VMEM((2, KV, 2, 2, 16, D), bf))
    serve(1)

    def between(held, made_rows, normed_rows):
        def step(i, carry):
            span = pl.ds(pl.multiple_of(i * 32, 32), 32)
            inward = pltpu.make_async_copy(tokens.at[span], held, move_sem.at[0])
            inward.start()
            inward.wait()
            branch = branch_one[span, :]
            after = None
            for t in range(4):
                out = mixed_out([stream(held, s) for s in range(4)], branch, mix, 0, t)
                made_rows[:, t * D : (t + 1) * D] = out
                term = weight(mix, 1, t, 0) * out
                after = term if after is None else after + term
            outward = pltpu.make_async_copy(made_rows, middle.at[span], move_sem.at[1])
            outward.start()
            normed_rows[span, :] = normed_of(after)[0]
            outward.wait()
            return carry

        lax.fori_loop(0, 4, step, 0)
        entry[...] = normed_rows[...].astype(bf)
        turn(normed_rows[...], 3)

    pl.run_scoped(between, pltpu.VMEM((32, 4 * D), bf), pltpu.VMEM((32, 4 * D), f32), pltpu.VMEM((128, D), f32))
    serve(1)

    ready(2)
    ready(3)

    def hidden_back(tiles):
        def use(i, s):
            dz[:, pl.ds(pl.multiple_of(i * 768, 256), 768)] = last(rhs_v[:, 0:D], tiles[s].reshape(768, D))

        pumped(8, lambda i: g2.at[i // 4, i % 4], tiles, tile_sem, use)

    pl.run_scoped(hidden_back, pltpu.VMEM((2, 4, 2, 2, 48, D), bf))
    serve(2)
    branch_two[...] = jnp.zeros_like(branch_two)
    dn[...] = jnp.zeros_like(dn)

    def feed(quarter, lower, opened):
        for j in range(4):
            ready(4 + j)
            ins = [
                pltpu.make_async_copy(
                    g3.at[i // 4, i % 4, :, :, :, :, QUART * j : QUART * (j + 1)], quarter.at[i], out_sem.at[i // 4, i % 4])
                for i in range(8)
            ]
            for copy in ins:
                copy.start()
            downs = [
                pltpu.make_async_copy(g2.at[j // 2, 2 * (j % 2) + i], lower.at[i], tile_sem.at[i]) for i in (0, 1)
            ]
            for copy in downs:
                copy.start()
            opened[...] = jnp.zeros_like(opened)
            for i in range(8):
                ins[i].wait()
                opened[...] += jnp.dot(entry[:, i * 256 : (i + 1) * 256], quarter[i].reshape(256, QUART),
                                       preferred_element_type=f32)
            serve(1)

            def act(i, carry):
                lanes = pl.ds(pl.multiple_of(i * 256, 256), 256)
                gate = opened[:, lanes]
                upper = opened[:, pl.ds(pl.multiple_of(GATE + i * 256, 256), 256)]
                given = dz[:, pl.ds(pl.multiple_of(j * GATE + i * 256, 256), 256)]
                sigma = jax.nn.sigmoid(gate)
                shut = gate * sigma
                rhs_v[:, pl.ds(pl.multiple_of(D + QUART * j + i * 256, 256), 256)] = (
                    given * upper * sigma * (1.0 + gate * (1.0 - sigma))).astype(bf)
                rhs_v[:, pl.ds(pl.multiple_of(D + QUART * j + GATE + i * 256, 256), 256)] = (given * shut).astype(bf)
                opened[:, lanes] = shut * upper
                return carry

            lax.fori_loop(0, GATE // 256, act, 0)
            hidden = opened[:, 0:GATE]
            flat = hidden.T.astype(bf).reshape(2, 4, 2, 2, 3, 16, 128)
            for cc in (0, 1):
                for sub in range(3):
                    for xl in (0, 1):
                        lhs_v[cc, sub, 2 * (j // 2) + xl, 2 * (j % 2) : 2 * (j % 2) + 2] = flat[:, :, xl, cc, sub]
            hidden = hidden.astype(bf)
            for i in (0, 1):
                downs[i].wait()
                branch_two[...] += jnp.dot(hidden[:, i * 768 : (i + 1) * 768], lower[i].reshape(768, D),
                                           preferred_element_type=f32)
            serve(1)

            def back(i, carry):
                lanes = pl.ds(pl.multiple_of(i * 256, 256), 256)
                dn[:, lanes] += last(rhs_v[:, D + QUART * j : D + QUART * (j + 1)], quarter[i].reshape(256, QUART))
                return carry

            lax.fori_loop(0, 8, back, 0)
            serve(1)

    pl.run_scoped(feed, pltpu.VMEM((8, 4, 2, 2, 16, QUART), bf), pltpu.VMEM((2, 4, 2, 2, 48, D), bf),
                  pltpu.VMEM((128, QUART), f32))
    serve(len(queue))
    aways = [pltpu.make_async_copy(lhs_v, lhs, move_sem.at[0]), pltpu.make_async_copy(rhs_v, rhs, move_sem.at[1])]
    for copy in aways:
        copy.start()
    for i in range(PARTS):
        for p in range(3):
            for k in range(3):
                for n in range(4):
                    ring(i, p, k, n).wait_send()
            for slot in range(9):
                spread(i, p, slot).wait_send()
    for w in range(4):
        own_copy(w).wait_send()
    for copy in made.values():
        copy.wait_send()
    for copy in aways:
        copy.wait()


def run_forward(shards, tokens, coming, mix, cosine, sine, marks, collective_id):
    bf = jnp.bfloat16
    f32 = jnp.float32
    v = pltpu.VMEM
    dma = pltpu.SemaphoreType.DMA
    hbm = pl.BlockSpec(memory_space=pl.ANY)
    near = pl.BlockSpec(memory_space=pltpu.VMEM)
    S = jax.ShapeDtypeStruct
    return pl.pallas_call(
        forward_pass,
        out_shape=[S((2, 4, 4, 2, 2) + s.shape, bf) for s in shards] + [
            S((2, 6, 4, 4, 4, 16, 128), bf),
            S((128, D + 4 * QUART), bf),
            S((2, ROWS, 256), bf),
            S((2, 2, 4, 4, 64, 512), bf),
            S((2, ROWS, 256), f32),
            S((2, ROWS, 128), f32),
            S((128, D), f32),
            S((128, 4 * D), f32),
            S((128, D), f32),
            S((128, D), f32),
        ],
        in_specs=[hbm] * 6 + [pl.BlockSpec(memory_space=pltpu.SMEM)] + [near] * 3,
        out_specs=[hbm] * 6 + [near] * 5 + [hbm] + [near] * 2,
        scratch_shapes=[
            v((128, D), bf),
            v((2, 6, 4, 4, 4, 16, 128), bf),
            v((128, D + 4 * QUART), bf),
            v((KV, ROWS, 1), f32),
            v((KV, ROWS, 1), f32),
            v((128, 4 * GATE), f32),
            v((128, 2560), f32),
            dma((4,)),
            dma((PARTS, 3, 3, 4)),
            dma((PARTS, 3, 3, 4)),
            dma((PARTS, 3, 9)),
            dma((PARTS, 3, 9)),
            dma((4,)),
            dma((4,)),
            dma((2, 9)),
            dma((2, 9)),
            dma((2,)),
            dma((2, 4)),
            dma((2,)),
        ],
        compiler_params=pltpu.CompilerParams(
            collective_id=collective_id, has_side_effects=True, vmem_limit_bytes=62 * 1024 * 1024),
    )(*shards, tokens, coming, mix, cosine, sine, marks)


def adam(weight, grad, first, second, factor, rate, decay):
    grad = grad * factor
    first = BETA_ONE * first + (1.0 - BETA_ONE) * grad
    second = BETA_TWO * second + (1.0 - BETA_TWO) * grad * grad
    ahead = first / (1.0 - BETA_ONE**STEP)
    scaled = second / (1.0 - BETA_TWO**STEP)
    weight = weight - rate * (ahead / (jnp.sqrt(scaled) + ADAM_EPS) + decay * weight)
    return (weight, first, second)


def padded(columns):
    shape = columns.shape[:-1]
    split = columns.reshape(shape + (128, 44))
    split = jnp.pad(split, ((0, 0),) * len(shape) + ((0, 0), (0, 4)))
    return split.reshape(shape + (128 * 48,))


def unpadded(columns):
    shape = columns.shape[:-1]
    return columns.reshape(shape + (128, 48))[..., :44].reshape(shape + (FF,))


def head_rows(flat):
    return flat.reshape(2, 64, KV, 8, HD).transpose(0, 3, 1, 2, 4).reshape(2, ROWS, KV * HD)


def by_group(columns):
    turned_columns = columns[:, :2048].reshape(-1, KV, 8, HD).transpose(0, 2, 1, 3).reshape(-1, 2048)
    return jnp.concatenate([turned_columns, columns[:, 2048:]], axis=1)


def by_head(columns):
    turned_columns = columns[:, :2048].reshape(-1, 8, KV, HD).transpose(0, 2, 1, 3).reshape(-1, 2048)
    return jnp.concatenate([turned_columns, columns[:, 2048:]], axis=1)


def tables(spots):
    freq = jnp.exp(jnp.arange(HD // 2, dtype=jnp.float32) * (-2.0 * math.log(THETA_BASE) / HD))
    angle = spots.reshape(2, 64, 1) * freq
    cosine, sine = jnp.cos(angle), jnp.sin(angle)
    return (jnp.tile(jnp.concatenate([cosine, cosine], axis=2), (1, 1, KV)),
            jnp.tile(jnp.concatenate([sine, -sine], axis=2), (1, 1, KV)))


def body(streams, doc_start, cotangent, mixing, w_project, w_output, w_expand, w_reduce,
         first_mixing, second_mixing, first_project, second_project, first_output, second_output,
         first_expand, second_expand, first_reduce, second_reduce):
    bf, f32 = jnp.bfloat16, jnp.float32
    anchor = lax.axis_index("ctx") * 64
    tokens = streams.reshape(128, 8192)
    coming = cotangent.reshape(128, 8192)
    starts = doc_start.reshape(2, 64)
    places = anchor + jnp.arange(64, dtype=jnp.int32)
    spots = (places[None, :] - starts).astype(f32).reshape(128)
    mix = mixing.reshape(48)

    cosine, sine = tables(spots)
    edges = jnp.stack([jnp.tile(starts, (1, 8)), jnp.broadcast_to(jnp.tile(places, 8), (2, ROWS))], axis=2).astype(f32)
    marks = jnp.pad(edges, ((0, 0), (0, 0), (8, 118)))

    bf_expand = w_expand.astype(bf)
    halves = [padded(bf_expand[:, :FF]).reshape(16, 4, 1, GATE), padded(bf_expand[:, FF:]).reshape(16, 4, 1, GATE)]
    shards = [
        by_group(w_project.astype(bf)),
        w_output.astype(bf),
        jnp.pad(w_reduce.astype(bf), ((0, 4), (0, 0))),
        jnp.concatenate(halves, axis=2).reshape(16, 4 * QUART),
    ]
    (project, output, _, _, lhs, rhs, query, kv, mixed, lse, branch_one, middle, branch_two, dn_two) = run_forward(
        shards, tokens, coming, mix, cosine, sine, marks, 1)
    project, output = project.reshape(2048, 2560), output.reshape(2048, 2048)
    fresh, notes_two = call(close_kernel, mix, [middle, branch_two, coming], [(8192, bf)], 24)
    middle_grad, grad_one, notes_one = call(
        between_kernel, mix, [tokens, middle, coming, dn_two, branch_one], [(8192, f32), (2048, bf)], 24)
    attended_grad = lax.dot_general(
        grad_one, output, (((1,), (1,)), ((), ())), preferred_element_type=f32).astype(bf)
    dout = head_rows(attended_grad)
    lean = jnp.sum((mixed * dout.astype(f32)).reshape(2, ROWS, KV, HD), axis=3)
    stats = jnp.concatenate([lse[:, :, :4], lean, marks[:, :, 8:]], axis=2)
    grads, tokens_grad, total = run_backward(
        lhs, rhs, grad_one, query, dout, kv.reshape(2, 2048, 512), stats, cosine, sine, project, tokens, middle_grad, mix,
        jnp.concatenate([notes_two, notes_one], axis=0), 2)
    sums = jnp.sum(total, axis=1)
    two, one, zero = sums[:24], sums[24:48], sums[48:]
    mix_total = jnp.stack([
        jnp.concatenate([zero[:4, None], one[4:8, None], one[8:24].reshape(4, 4)], axis=1),
        jnp.concatenate([one[:4, None], two[:4, None], two[4:20].reshape(4, 4)], axis=1),
    ])

    def units(lo, hi):
        return grads[lo:hi].transpose(1, 0, 2).reshape(16, (hi - lo) * W)

    reduce_grad = grads[:12].reshape(3, 4, 16, W).transpose(0, 2, 1, 3).reshape(48, 2048)[:44]
    expand_grad = units(12, 36).reshape(16, 4, 2, GATE)
    expand_grad = jnp.concatenate([unpadded(expand_grad[:, :, k].reshape(16, 6144)) for k in (0, 1)], axis=1)
    output_grad = units(36, 40)
    project_grad = by_head(units(40, 45))
    norm = jnp.sqrt(zero[7] + jnp.sum(mix_total * mix_total))
    factor = THRESHOLD / jnp.maximum(norm, THRESHOLD)
    mix_new = adam(mixing, mix_total, first_mixing, second_mixing, factor, RATE_MIXING, 0.0)
    proj_new = adam(w_project, project_grad, first_project, second_project, factor, RATE_MATRIX, DECAY_MATRIX)
    outp_new = adam(w_output, output_grad, first_output, second_output, factor, RATE_MATRIX, DECAY_MATRIX)
    expd_new = adam(w_expand, expand_grad, first_expand, second_expand, factor, RATE_MATRIX, DECAY_MATRIX)
    redc_new = adam(w_reduce, reduce_grad, first_reduce, second_reduce, factor, RATE_MATRIX, DECAY_MATRIX)
    return (fresh.reshape(streams.shape), tokens_grad.reshape(streams.shape), norm,
            *mix_new, *proj_new, *outp_new, *expd_new, *redc_new)


def solution(mesh):
    acts = P(None, "fsdp", "ctx", None, None)
    rows = P(("ctx", "fsdp"), None)
    return jax.shard_map(
        body,
        mesh=mesh,
        in_specs=(acts, P(None, "fsdp", "ctx"), acts, P()) + (rows,) * 4 + (P(), P()) + (rows,) * 8,
        out_specs=(acts, acts, P(), P(), P(), P()) + (rows,) * 12,
        check_vma=False,
    )
```

```python
import functools
import math

import jax
import jax.numpy as jnp
from jax import lax
from jax.experimental import pallas as pl
from jax.experimental.pallas import tpu as pltpu
from jax.sharding import PartitionSpec as P

H = 32
FF = 5632
STEP = 10
THETA_BASE = 10000.0
BETA_ONE = 0.9
BETA_TWO = 0.95
ADAM_EPS = 1e-08
RATE_MATRIX = 0.06
RATE_MIXING = 0.5
DECAY_MATRIX = 0.1
THRESHOLD = 1.0


MESH = pl.DeviceIdType.MESH


def place():
    ctx = lax.axis_index("ctx")
    fsdp = lax.axis_index("fsdp")
    return (2 * (ctx // 16) + fsdp // 2, (ctx // 4) % 4, ctx % 4, fsdp % 2)


def ident(x, y, z, c):
    return ((x // 2) * 16 + y * 4 + z, (x % 2) * 2 + c)


def moved(spot, axis, step):
    spot = list(spot)
    spot[axis] = (spot[axis] + step + 4) % 4
    return tuple(spot)


ROWS = 512
HD = 64
KV = 4


UNIT = 1024
WIDTHS = ((2, 1, 1), (6, 5, 5), (5, 6, 5), (16, 16, 16), (12, 10, 10), (10, 12, 10), (10, 10, 12))
ARRAYS = 7


def offsets(w):
    a, b, _ = WIDTHS[w]
    return (0, 128 * a, 128 * (a + b))


def order(p):
    return (p, (p + 1) % 3, (p + 2) % 3)


def last(left, right):
    return lax.dot_general(left, right, (((1,), (1,)), ((), ())), preferred_element_type=jnp.float32)


def first(left, right):
    return lax.dot_general(left, right, (((0,), (0,)), ((), ())), preferred_element_type=jnp.float32)


def put_back(native, p, value, first=0, count=8):
    value = value.reshape(count, 4, 4, 16, 128)
    for i in range(count):
        c, a = (first + i) // 4, (first + i) % 4
        for b in range(4):
            if p == 0:
                native[:, b, a, :, c] += value[i, b].reshape(2, 2, 16, 128)
            elif p == 1:
                native[a // 2, :, b, a % 2, c] += value[i, b]
            else:
                native[b // 2, a, :, b % 2, c] += value[i, b]


def native_columns(native, out):
    for xh in (0, 1):
        for y in range(4):
            out[:, (xh * 4 + y) * 256 : (xh * 4 + y + 1) * 256] = native[xh, y].reshape(256, 128).T


def unit_place(s, c, a, b, n):
    at = [0, 0, 0]
    for axis, value in zip(order(s), (n, b, a)):
        at[axis] = value
    x, y, z = at
    return (x // 2) * 64 + y * 16 + z * 4 + (x % 2) * 2 + c


def unit_rows(s, c, read):
    got = []
    for a in range(4):
        for b in range(4):
            for n in range(4):
                got.append(read(unit_place(s, c, a, b, n)))
                if s == 2:
                    got.append(jnp.zeros((4, 16), jnp.float32))
    return jnp.concatenate(got, axis=0)


TB = 16
D = 2048
NORM_EPS = 1e-05


def stream(ref, s):
    return ref[:, s * D : (s + 1) * D].astype(jnp.float32)


def weight(mix, k, s, j):
    return mix[k * 24 + s * 6 + j]


def entry_of(parts, mix, k):
    return sum(weight(mix, k, s, 0) * parts[s] for s in range(4))


def normed_of(entry):
    center = entry - jnp.mean(entry, axis=-1, keepdims=True)
    inverse = lax.rsqrt(jnp.mean(center * center, axis=-1, keepdims=True) + NORM_EPS)
    return center * inverse, inverse


def norm_back(grad, normed, inverse):
    return inverse * (
        grad
        - jnp.mean(grad, axis=-1, keepdims=True)
        - normed * jnp.mean(grad * normed, axis=-1, keepdims=True)
    )


def mixed_out(parts, branch, mix, k, t):
    return sum(weight(mix, k, s, 2 + t) * parts[s] for s in range(4)) + weight(mix, k, t, 1) * branch


def inner(a, b):
    both = a * b
    folded = both[:, 0:128]
    for j in range(1, D // 128):
        folded = folded + both[:, j * 128 : (j + 1) * 128]
    return jnp.sum(folded, axis=0, keepdims=True)


def note(ref, row, value):
    ref[row : row + 1, :] += value


def start_notes(ref):
    @pl.when(pl.program_id(0) == 0)
    def _():
        ref[...] = jnp.zeros_like(ref)


def between_kernel(mix, middle, coming, dn, middle_grad, grad, notes):
    start_notes(notes)
    normed, inverse = normed_of(entry_of([stream(middle, s) for s in range(4)], mix, 1))
    dx = norm_back(dn[...], normed, inverse)
    e = None
    for s in range(4):
        note(notes, s, inner(stream(middle, s), dx))
        g = sum(weight(mix, 1, s, 2 + t) * stream(coming, t) for t in range(4)) + weight(mix, 1, s, 0) * dx
        middle_grad[:, s * D : (s + 1) * D] = g
        term = weight(mix, 0, s, 1) * g
        e = term if e is None else e + term
    grad[...] = e.astype(jnp.bfloat16)


def call(kernel, mix, arrays, outs, notes=0):
    rows = arrays[0].shape[0]
    shapes = [jax.ShapeDtypeStruct((rows, n), d) for n, d in outs]
    specs = [pl.BlockSpec((TB, n), lambda i: (i, 0)) for n, _ in outs]
    if notes:
        shapes.append(jax.ShapeDtypeStruct((notes, 128), jnp.float32))
        specs.append(pl.BlockSpec((notes, 128), lambda i: (0, 0)))
    return pl.pallas_call(
        kernel,
        out_shape=shapes,
        grid=(rows // TB,),
        in_specs=[pl.BlockSpec(memory_space=pltpu.SMEM)]
        + [pl.BlockSpec((TB, a.shape[1]), lambda i: (i, 0)) for a in arrays],
        out_specs=specs,
        compiler_params=pltpu.CompilerParams(vmem_limit_bytes=62 * 1024 * 1024),
    )(mix, *arrays)


def output_back_kernel(grad, piece0, piece1, piece2, rows_out, lse, marks, dout, stats, native):
    native[...] = jnp.zeros_like(native)
    for p, piece in enumerate((piece0, piece1, piece2)):
        n = piece.shape[1]
        lo = offsets(2)[p]

        def step(i, carry, p=p, piece=piece, lo=lo, n=n):
            cc = i // 4
            value = last(piece[pl.ds(pl.multiple_of(i * 256, 256), 256), :], grad[:, lo : lo + n]).reshape(4, 4, 16, 128)
            for b in range(4):
                if p == 0:
                    native[:, b, i % 4, :, cc] += value[b].reshape(2, 2, 16, 128)
                elif p == 1:
                    native[(i % 4) // 2, :, b, i % 2, cc] += value[b]
                else:
                    native[b // 2, i % 4, :, b % 2, cc] += value[b]
            return carry

        lax.fori_loop(0, 8, step, 0)
    for g in range(8):
        turned_rows = jnp.concatenate(
            [native[h // 2, (h % 2) * 2 + g // 4, g % 4].reshape(64, 128) for h in range(KV)], axis=0).T.astype(jnp.bfloat16)
        for m in (0, 1):
            dout[m, g * 64 : (g + 1) * 64, :] = turned_rows[m * 64 : (m + 1) * 64]
    for m in (0, 1):
        lean = [
            jnp.sum(rows_out[m, :, h * HD : (h + 1) * HD] * dout[m, :, h * HD : (h + 1) * HD].astype(jnp.float32),
                    axis=1, keepdims=True)
            for h in range(KV)
        ]
        stats[m] = jnp.concatenate([lse[m, :, 0:4]] + lean + [marks[m, :, 8:]], axis=1)


def output_back(grad, pieces, rows_out, lse, marks):
    return pl.pallas_call(
        output_back_kernel,
        out_shape=[jax.ShapeDtypeStruct((2, ROWS, 256), jnp.bfloat16), jax.ShapeDtypeStruct((2, ROWS, 128), jnp.float32)],
        scratch_shapes=[pltpu.VMEM((2, 4, 4, 2, 2, 16, 128), jnp.float32)],
        compiler_params=pltpu.CompilerParams(vmem_limit_bytes=62 * 1024 * 1024),
    )(grad, *pieces, rows_out, lse, marks)


W = 512
HALF = 256
UNITS = 45
CHUNKS = 15
SLOTS = 2
STAGES = 6
COLS = 2048 + 12288 + 2048 + 2560
JOINED = 16384
KB = 512
KEY_SCALE = HD**-0.5


def unit_spot(u):
    early = u // 12
    early = 1 - (1 // (1 + early))
    left = (1 - early) * (u // 4) + early * (3 + u // 36 + u // 40)
    column = (1 - early) * ((u % 4) * W) + early * (2048 + (u - 12) * W)
    return left, pl.multiple_of(column, W)


def turned(x, cosine, sine):
    lane = lax.broadcasted_iota(jnp.int32, x.shape, 1)
    swapped = jnp.where(lane % HD < HD // 2, pltpu.roll(x, x.shape[1] - HD // 2, 1), pltpu.roll(x, HD // 2, 1))
    return x * cosine + swapped * sine


def backward_pass(lhs, rhs, grad_one, query, dout, kv, stats, cosine, sine, keys0, keys1, keys2, query0, query1, query2, tokens, middle_grad, middle, coming, branch_one, branch_two, mix, notes_in,
                  grads, tokens_grad, fresh, total, left, right, acc1, acc2,
                  sa, ra, sb, rb, sc, rc, sd, rd, se, re, sf, rf, vsend, vrecv, out,
                  dq, terms, k1, k2, k3s, k3, k4s, k4, k5s, k5, kacc, kacc2, dn, native, notes,
                  send_sem, recv_sem, free_sem, local_sem, side_send, side_recv, out_sem, v_send_sem, v_recv_sem,
                  k_send, k_recv, tile_sem, late_send, late_recv):
    bf = jnp.bfloat16
    f32 = jnp.float32
    spot = place()
    x, y, z, c = spot
    pos = (x, y, z)
    xh = x // 2
    anchor = ((xh * 4 + y) * 4 + z) * 64
    sibling = (x, y, z, 1 - c)
    barrier = pltpu.get_barrier_semaphore()
    others = [sibling] + [moved(spot, axis, step) for axis in range(3) for step in (1, 2, 3)]
    for other in others:
        pl.semaphore_signal(barrier, inc=1, device_id=ident(*other), device_id_type=MESH)
    pl.semaphore_wait(barrier, len(others))

    parts = (((0, 3), (0, 2048)), ((3, 4), (2048, 14336)), ((4, 6), (14336, JOINED)))
    moves = []
    for j, ((l0, l1), (c0, c1)) in enumerate(parts):
        source = grad_one if j == 2 else rhs.at[:, c0:c1]
        own = [
            pltpu.make_async_copy(lhs.at[c, l0:l1], left.at[l0:l1, :, :, :, :, 0:128], local_sem.at[j, 0]),
            pltpu.make_async_copy(source, right.at[0:128, c0:c1], local_sem.at[j, 1]),
        ]
        far = [
            pltpu.make_async_remote_copy(
                lhs.at[1 - c, l0:l1], left.at[l0:l1, :, :, :, :, 128:256], side_send.at[j, 0], side_recv.at[j, 0],
                device_id=ident(*sibling), device_id_type=MESH),
            pltpu.make_async_remote_copy(
                source, right.at[128:256, c0:c1], side_send.at[j, 1], side_recv.at[j, 1],
                device_id=ident(*sibling), device_id_type=MESH),
        ]
        for copy in own + far:
            copy.start()
        moves.append((own, far))
    late = pltpu.make_async_remote_copy(
        right.at[0:128, JOINED:COLS], right.at[128:256, JOINED:COLS], late_send, late_recv,
        device_id=ident(*sibling), device_id_type=MESH)

    def arrive(j):
        for copy in moves[j][0]:
            copy.wait()
        for copy in moves[j][1]:
            copy.wait_recv()

    arrive(0)
    dq[...] = jnp.zeros_like(dq)
    notes[...] = jnp.zeros_like(notes)
    notes[24:32, :] = notes_in[...]
    native[...] = jnp.zeros_like(native)

    sends = (sa, sb, sc, sd, se, sf)
    recvs = (ra, rb, rc, rd, re, rf)

    def hop(stage, p, d, slot):
        axis = (p + stage // 2) % 3
        return pltpu.make_async_remote_copy(
            sends[stage].at[p, d, slot], recvs[stage].at[p, d, slot],
            send_sem.at[stage, p, d, slot], recv_sem.at[stage, p, d, slot],
            device_id=ident(*moved(spot, axis, 1 - 2 * d)), device_id_type=MESH)

    def before_send(stage, p, q):
        @pl.when(q >= SLOTS)
        def _():
            for d in (0, 1):
                hop(stage, p, d, q % SLOTS).wait_send()
                pl.semaphore_wait(free_sem.at[stage, p, d], 1)

    def give_back(stage, p, q):
        @pl.when(q < CHUNKS - SLOTS)
        def _():
            axis = (p + stage // 2) % 3
            for d in (0, 1):
                pl.semaphore_signal(free_sem.at[stage, p, d], inc=1,
                                    device_id=ident(*moved(spot, axis, 2 * d - 1)), device_id_type=MESH)

    def go(stage, p, q):
        for d in (0, 1):
            hop(stage, p, d, q % SLOTS).start()

    def come(stage, p, q):
        for d in (0, 1):
            hop(stage, p, d, q % SLOTS).wait_recv()

    def rows(p, l, a):
        if p == 0:
            got = left[l, a]
        elif p == 1:
            got = left[l, :, a]
        else:
            got = left[l, :, :, a]
        return got.reshape(256, 256)

    def product(p, q, a, lo, hi):
        l, column = unit_spot(3 * q + p)
        return jnp.dot(rows(p, l, a), right[:, pl.ds(pl.multiple_of(column + lo, HALF), hi - lo)],
                       preferred_element_type=f32)

    def at(p, step):
        return (pos[p] + step + 4) % 4

    def stage1(q):
        s = q % SLOTS
        for p in range(3):
            before_send(0, p, q)
            for d in (0, 1):
                sa[p, d, s] = product(p, q, at(p, 2), d * HALF, d * HALF + HALF).astype(bf)
            go(0, p, q)

    def stage2(q):
        s = q % SLOTS
        for p in range(3):
            before_send(1, p, q)
            come(0, p, q)
            for d in (0, 1):
                lo = d * HALF
                near = at(p, 1 - 2 * d)
                sb[p, d, s, :, lo : lo + HALF] = (
                    product(p, q, near, lo, lo + HALF) + ra[p, d, s].astype(f32)).astype(bf)
                other = HALF - lo
                sb[p, d, s, :, other : other + HALF] = product(p, q, near, other, other + HALF).astype(bf)
            give_back(0, p, q)
            go(1, p, q)

    def part(p, ref, b):
        return ref.at[:, b] if p == 1 else ref.at[b]

    def stage3(q):
        s = q % SLOTS
        for p in range(3):
            come(1, p, q)
            for lo in (0, HALF):
                both = (product(p, q, pos[p], lo, lo + HALF)
                        + rb[p, 0, s, :, lo : lo + HALF].astype(f32) + rb[p, 1, s, :, lo : lo + HALF].astype(f32))
                acc1[p, s, :, :, :, lo : lo + HALF] = both.reshape(4, 4, 16, HALF)
            give_back(1, p, q)
            before_send(2, p, q)
            ahead = at((p + 1) % 3, 2)
            for d in (0, 1):
                sc[p, d, s] = part(p, acc1.at[p, s], ahead)[:, :, d * HALF : d * HALF + HALF].astype(bf)
            go(2, p, q)

    def stage4(q):
        s = q % SLOTS
        for p in range(3):
            before_send(3, p, q)
            come(2, p, q)
            for d in (0, 1):
                lo = d * HALF
                other = HALF - lo
                mine = part(p, acc1.at[p, s], at((p + 1) % 3, 1 - 2 * d))
                sd[p, d, s, :, :, lo : lo + HALF] = (
                    mine[:, :, lo : lo + HALF] + rc[p, d, s].astype(f32)).astype(bf)
                sd[p, d, s, :, :, other : other + HALF] = mine[:, :, other : other + HALF].astype(bf)
            give_back(2, p, q)
            go(3, p, q)

    def stage5(q):
        s = q % SLOTS
        for p in range(3):
            come(3, p, q)
            acc2[p, s] = (part(p, acc1.at[p, s], pos[(p + 1) % 3])[...]
                          + rd[p, 0, s].astype(f32) + rd[p, 1, s].astype(f32))
            give_back(3, p, q)
            before_send(4, p, q)
            ahead = at((p + 2) % 3, 2)
            for d in (0, 1):
                se[p, d, s] = acc2[p, s, ahead, :, d * HALF : d * HALF + HALF].astype(bf)
            go(4, p, q)

    def stage6(q):
        s = q % SLOTS
        for p in range(3):
            before_send(5, p, q)
            come(4, p, q)
            for d in (0, 1):
                lo = d * HALF
                other = HALF - lo
                near = at((p + 2) % 3, 1 - 2 * d)
                sf[p, d, s, :, lo : lo + HALF] = (
                    acc2[p, s, near, :, lo : lo + HALF] + re[p, d, s].astype(f32)).astype(bf)
                sf[p, d, s, :, other : other + HALF] = acc2[p, s, near, :, other : other + HALF].astype(bf)
            give_back(4, p, q)
            go(5, p, q)

    def stage7(q):
        s = q % SLOTS
        for p in range(3):
            come(5, p, q)
            out[3 * q + p] = (acc2[p, s, pos[(p + 2) % 3]]
                              + rf[p, 0, s].astype(f32) + rf[p, 1, s].astype(f32))
            give_back(5, p, q)

    def attend(m, block):
        where = (m, block // 2, pl.ds((block % 2) * 2, 2))

        @pl.when(block * KB <= anchor + 63)
        def _():
            columns = (block * KB + lax.broadcasted_iota(jnp.int32, (ROWS, KB), 1)).astype(f32)
            keep = (columns >= stats[m, :, 8:9]) & (columns <= stats[m, :, 9:10])
            span = pl.ds(pl.multiple_of(block * KB, KB), KB)
            keys, values, queries = [], [], []
            for h in range(KV):
                lanes = slice(h * HD, (h + 1) * HD)
                k = kv[m, span, lanes]
                v = kv[m, span, 256 + h * HD : 256 + (h + 1) * HD]
                qh = query[m, :, lanes]
                doh = dout[m, :, lanes]
                p = jnp.exp(jnp.where(keep, last(qh, k) - stats[m, :, h : h + 1], -1e30))
                ds = (p * (last(doh, v) - stats[m, :, 4 + h : 5 + h])).astype(bf)
                queries.append(jnp.dot(ds, k, preferred_element_type=f32) * KEY_SCALE)
                keys.append(first(ds, qh))
                values.append(first(p.astype(bf), doh))
            dq[m] += jnp.concatenate(queries, axis=1)
            terms[where] = jnp.concatenate(keys + values, axis=1).astype(bf).reshape(2, 4, 64, 512)

        @pl.when(block * KB > anchor + 63)
        def _():
            terms[where] = jnp.zeros((2, 4, 64, 512), bf)

    cols = [slice(0, 256), slice(256, 512)]
    axes = [(2, 1), (1, 2)]

    def view(p, m, a):
        return terms.at[m, :, :, a, :, cols[p]] if p == 0 else terms.at[m, :, a, :, :, cols[p]]

    def khop(stage, p, d):
        if stage == 4:
            src, dst, to = k5s.at[p], k5.at[p], moved(spot, 0, 2)
        else:
            axis = axes[p][stage // 2]
            to = moved(spot, axis, 1 - 2 * d)
            if stage == 0:
                src, dst = view(p, d, (spot[axis] + 2) % 4), k1.at[p, d]
            elif stage == 1:
                src, dst = view(p, slice(None), (spot[axis] + 1 + 2 * d) % 4), k2.at[p, d]
            elif stage == 2:
                src, dst = k3s.at[p, d], k3.at[p, d]
            else:
                src, dst = k4s.at[p, d], k4.at[p, d]
        return pltpu.make_async_remote_copy(
            src, dst, k_send.at[stage, p, d], k_recv.at[stage, p, d], device_id=ident(*to), device_id_type=MESH)

    def terms1():
        for p in range(2):
            for d in (0, 1):
                khop(0, p, d).start()

    def terms2():
        for p in range(2):
            for d in (0, 1):
                khop(0, p, d).wait_recv()
                mine = view(p, d, (spot[axes[p][0]] + 1 + 2 * d) % 4)
                mine[...] = (mine[...].astype(f32) + k1[p, d].astype(f32)).astype(bf)
                khop(1, p, d).start()

    def terms3():
        for p in range(2):
            for d in (0, 1):
                khop(1, p, d).wait_recv()
            for m in (0, 1):
                kacc[p, m] = (view(p, m, spot[axes[p][0]])[...].astype(f32)
                              + k2[p, 0, m].astype(f32) + k2[p, 1, m].astype(f32))
            for d in (0, 1):
                k3s[p, d] = kacc[p, d, :, (spot[axes[p][1]] + 2) % 4].astype(bf)
                khop(2, p, d).start()

    def terms4():
        for p in range(2):
            for d in (0, 1):
                near = (spot[axes[p][1]] + 1 + 2 * d) % 4
                khop(2, p, d).wait_recv()
                k4s[p, d, d] = (kacc[p, d, :, near] + k3[p, d].astype(f32)).astype(bf)
                k4s[p, d, 1 - d] = kacc[p, 1 - d, :, near].astype(bf)
                khop(3, p, d).start()

    def terms5():
        for p in range(2):
            for d in (0, 1):
                khop(3, p, d).wait_recv()
            kacc2[p] = kacc[p, :, :, spot[axes[p][1]]] + k4[p, 0].astype(f32) + k4[p, 1].astype(f32)
            k5s[p] = kacc2[p, :, 1 - xh].astype(bf)
            khop(4, p, 0).start()

    def join():
        for m in (0, 1):
            here = slice(m * 64, m * 64 + 64)
            for g in range(8):
                right[here, JOINED + g * 256 : JOINED + (g + 1) * 256] = turned(
                    dq[m, g * 64 : (g + 1) * 64, :], cosine[m], sine[m]).astype(bf)
        for p in range(2):
            khop(4, p, 0).wait_recv()
        for m in (0, 1):
            here = slice(m * 64, m * 64 + 64)
            right[here, JOINED + 2048 : JOINED + 2304] = turned(
                kacc2[0, m, xh] + k5[0, m].astype(f32), cosine[m], sine[m]).astype(bf)
            right[here, JOINED + 2304 : COLS] = (kacc2[1, m, xh] + k5[1, m].astype(f32)).astype(bf)
        late.start()

    def entry(i):
        def inside(tiles):
            def copies(p):
                made = []
                for a, piece in enumerate(((keys0, keys1, keys2)[p], (query0, query1, query2)[p])):
                    n = piece.shape[1]
                    made.append(pltpu.make_async_copy(
                        piece.at[pl.ds(pl.multiple_of(i * 512, 512), 512)], tiles.at[p, a, :, 0:n], tile_sem.at[p, a]))
                return made

            for p in range(3):
                for copy in copies(p):
                    copy.start()
            for p in range(3):
                for copy in copies(p):
                    copy.wait()
                value = None
                for a, w in enumerate((0, 1)):
                    n = 128 * WIDTHS[w][p]
                    lo = JOINED + (2048 if w == 0 else 0) + offsets(w)[p]
                    term = last(tiles[p, a, :, 0:n], right[0:128, lo : lo + n])
                    value = term if value is None else value + term
                value = value.reshape(2, 4, 4, 16, 128)
                for r in (0, 1):
                    cc = i // 2
                    at_last = (i % 2) * 2 + r
                    for b in range(4):
                        if p == 0:
                            native[:, b, at_last, :, cc] += value[r, b].reshape(2, 2, 16, 128)
                        elif p == 1:
                            native[i % 2, :, b, r, cc] += value[r, b]
                        else:
                            native[b // 2, at_last, :, b % 2, cc] += value[r, b]

        pl.run_scoped(inside, pltpu.VMEM((3, 2, 512, 768), bf))

        @pl.when(i == 3)
        def _():
            native_columns(native, dn)

    def finish(i):
        span = pl.ds(pl.multiple_of(i * 32, 32), 32)

        def inside(held, grad, branch, back):
            ins = [pltpu.make_async_copy(tokens.at[span], held, tile_sem.at[0, 0]),
                   pltpu.make_async_copy(middle_grad.at[span], grad, tile_sem.at[1, 0]),
                   pltpu.make_async_copy(branch_one.at[span], branch, tile_sem.at[2, 0])]
            for copy in ins:
                copy.start()
            for copy in ins:
                copy.wait()
            normed, inverse = normed_of(entry_of([stream(held, s) for s in range(4)], mix, 0))
            dx = norm_back(dn[span, :], normed, inverse)
            for s in range(4):
                note(notes, 48 + s, inner(stream(held, s), dx))
                back[:, s * D : (s + 1) * D] = (
                    sum(weight(mix, 0, s, 2 + t) * stream(grad, t) for t in range(4)) + weight(mix, 0, s, 0) * dx)
            away = pltpu.make_async_copy(back, tokens_grad.at[span], tile_sem.at[0, 0])
            away.start()
            for s in range(4):
                g = stream(grad, s)
                note(notes, 28 + s, inner(branch[...], g))
                for r in range(4):
                    note(notes, 32 + 4 * r + s, inner(stream(held, r), g))
            away.wait()

        pl.run_scoped(inside, pltpu.VMEM((32, 4 * D), bf), pltpu.VMEM((32, 4 * D), f32),
                      pltpu.VMEM((32, D), f32), pltpu.VMEM((32, 4 * D), f32))

    def close(i):
        span = pl.ds(pl.multiple_of(i * 32, 32), 32)

        def inside(after, given, branch, made):
            ins = [pltpu.make_async_copy(middle.at[span], after, tile_sem.at[0, 0]),
                   pltpu.make_async_copy(coming.at[span], given, tile_sem.at[1, 0]),
                   pltpu.make_async_copy(branch_two.at[span], branch, tile_sem.at[2, 0])]
            for copy in ins:
                copy.start()
            for copy in ins:
                copy.wait()
            for t in range(4):
                made[:, t * D : (t + 1) * D] = mixed_out(
                    [stream(after, s) for s in range(4)], branch[...], mix, 1, t).astype(bf)
            away = pltpu.make_async_copy(made, fresh.at[span], tile_sem.at[0, 0])
            away.start()
            for t in range(4):
                g = stream(given, t)
                note(notes, t, inner(branch[...], g))
                for s in range(4):
                    note(notes, 4 + 4 * s + t, inner(stream(after, s), g))
            away.wait()

        pl.run_scoped(inside, pltpu.VMEM((32, 4 * D), f32), pltpu.VMEM((32, 4 * D), bf),
                      pltpu.VMEM((32, D), f32), pltpu.VMEM((32, 4 * D), bf))

    def step(t, carry):
        @pl.when(t == 4)
        def _():
            arrive(1)

        @pl.when(t == 12)
        def _():
            arrive(2)

        @pl.when(t == 13)
        def _():
            late.wait_recv()

        stages = (stage1, stage2, stage3, stage4, stage5, stage6, stage7)
        for lag in (0, 1, 6, 5, 4, 3, 2):
            @pl.when((t >= lag) & (t < CHUNKS + lag))
            def _(lag=lag):
                stages[lag](t - lag)

        @pl.when(t < 2)
        def _():
            attend(0, 2 * t)
            attend(0, 2 * t + 1)

        @pl.when((t >= 2) & (t < 6))
        def _():
            attend(1, t - 2)

        @pl.when((t >= 6) & (t < 10))
        def _():
            close(t - 6)

        for when, task in ((5, terms1), (6, terms2), (7, terms3), (8, terms4), (9, terms5), (10, join)):
            pl.when(t == when)(task)

        @pl.when((t >= 11) & (t < 15))
        def _():
            entry(t - 11)

        @pl.when((t >= 15) & (t < 19))
        def _():
            finish(t - 15)
        return carry

    lax.fori_loop(0, CHUNKS + 6, step, 0)

    def tail(q, carry):
        for stage in range(STAGES):
            for p in range(3):
                for d in (0, 1):
                    hop(stage, p, d, q % SLOTS).wait_send()
        return carry

    lax.fori_loop(CHUNKS - SLOTS, CHUNKS, tail, 0)
    for own, far in moves:
        for copy in far:
            copy.wait_send()
    late.wait_send()
    for stage in range(5):
        for p in range(2):
            for d in (0, 1) if stage < 4 else (0,):
                khop(stage, p, d).wait_send()

    write = pltpu.make_async_copy(out, grads, out_sem)
    write.start()

    def squares(u, carry):
        g = out[u]
        return carry + g * g

    summed = lax.fori_loop(0, UNITS, squares, jnp.zeros((16, W), f32))
    lanes = jnp.sum(summed, axis=0, keepdims=True)
    lanes = lanes[:, 0:128] + lanes[:, 128:256] + lanes[:, 256:384] + lanes[:, 384:512]
    notes[55:56, :] = lanes
    vector = notes[...]
    for phase in range(4):
        vsend[phase] = vector
        if phase == 0:
            targets = [(0, sibling)]
        else:
            targets = [(step - 1, moved(spot, phase - 1, step)) for step in (1, 2, 3)]
        copies = [
            pltpu.make_async_remote_copy(
                vsend.at[phase], vrecv.at[phase, k], v_send_sem.at[phase, k], v_recv_sem.at[phase, k],
                device_id=ident(*to), device_id_type=MESH)
            for k, to in targets
        ]
        for copy in copies:
            copy.start()
        for copy in copies:
            copy.wait()
        for k, _ in targets:
            vector = vector + vrecv[phase, k]
    total[...] = vector
    write.wait()


def run_backward(lhs, rhs, grad_one, query, dout, kv, stats, cosine, sine, pieces, arrays, mix, notes, collective_id):
    bf = jnp.bfloat16
    f32 = jnp.float32
    v = pltpu.VMEM
    dma = pltpu.SemaphoreType.DMA
    pair = lambda shape: [v((3, 2, SLOTS) + shape, bf)] * 2
    hbm = pl.BlockSpec(memory_space=pl.ANY)
    near = pl.BlockSpec(memory_space=pltpu.VMEM)
    return pl.pallas_call(
        backward_pass,
        out_shape=[jax.ShapeDtypeStruct((UNITS, 16, W), f32), jax.ShapeDtypeStruct((128, 4 * D), f32),
                   jax.ShapeDtypeStruct((128, 4 * D), bf), jax.ShapeDtypeStruct((56, 128), f32)],
        in_specs=[hbm, hbm, hbm, near, near, near, near, near, near] + [hbm] * 12 + [
                  pl.BlockSpec(memory_space=pltpu.SMEM), near],
        out_specs=[hbm, hbm, hbm, near],
        scratch_shapes=[
            v((6, 4, 4, 4, 16, 256), bf),
            v((256, COLS), bf),
            v((3, SLOTS, 4, 4, 16, W), f32),
            v((3, SLOTS, 4, 16, W), f32),
            *pair((256, HALF)),
            *pair((256, W)),
            *pair((4, 16, HALF)),
            *pair((4, 16, W)),
            *pair((16, HALF)),
            *pair((16, W)),
            v((4, 56, 128), f32),
            v((4, 3, 56, 128), f32),
            v((UNITS, 16, W), f32),
            v((2, ROWS, 256), f32),
            v((2, 2, 4, 4, 64, 512), bf),
            v((2, 2, 2, 4, 64, 256), bf),
            v((2, 2, 2, 2, 4, 64, 256), bf),
            v((2, 2, 2, 64, 256), bf), v((2, 2, 2, 64, 256), bf),
            v((2, 2, 2, 2, 64, 256), bf), v((2, 2, 2, 2, 64, 256), bf),
            v((2, 2, 64, 256), bf), v((2, 2, 64, 256), bf),
            v((2, 2, 2, 4, 64, 256), f32), v((2, 2, 2, 64, 256), f32),
            v((128, D), f32),
            v((2, 4, 4, 2, 2, 16, 128), f32),
            v((56, 128), f32),
            dma((STAGES, 3, 2, SLOTS)),
            dma((STAGES, 3, 2, SLOTS)),
            pltpu.SemaphoreType.REGULAR((STAGES, 3, 2)),
            dma((3, 2)),
            dma((3, 2)),
            dma((3, 2)),
            dma,
            dma((4, 3)),
            dma((4, 3)),
            dma((5, 2, 2)),
            dma((5, 2, 2)),
            dma((3, 2)),
            dma,
            dma,
        ],
        compiler_params=pltpu.CompilerParams(
            collective_id=collective_id, has_side_effects=True, vmem_limit_bytes=62 * 1024 * 1024),
    )(lhs, rhs, grad_one, query, dout, kv, stats, cosine, sine, *pieces, *arrays, mix, notes)


SEQUENCE = (
    (0, 0, 0), (0, 1, 0), (2, 41, 0), (0, 2, 0), (0, 3, 0), (0, 0, 1), (2, 0, 0), (0, 1, 1), (0, 2, 1), (2, 1, 0),
    (0, 0, 2), (0, 1, 2), (0, 2, 2), (2, 2, 0), (0, 0, 3), (0, 3, 1), (0, 1, 3), (2, 3, 0), (0, 0, 4), (0, 2, 3),
    (2, 4, 0), (0, 0, 5), (0, 1, 4), (0, 0, 6), (2, 5, 0), (0, 2, 4), (2, 6, 0), (1, 0, 0), (1, 1, 0), (0, 1, 5),
    (1, 0, 1), (1, 1, 1), (0, 2, 5), (0, 1, 6), (1, 0, 2), (1, 1, 2), (0, 3, 2), (2, 7, 0), (1, 0, 3), (1, 1, 3),
    (0, 2, 6), (2, 8, 0), (2, 42, 0), (1, 0, 4), (0, 4, 0), (0, 3, 3), (1, 1, 4), (1, 0, 5), (2, 9, 0), (0, 4, 1),
    (0, 5, 0), (2, 10, 0), (1, 1, 5), (0, 4, 2), (0, 3, 4), (2, 11, 0), (2, 12, 0), (2, 13, 0), (2, 14, 0), (0, 4, 3),
    (0, 5, 1), (0, 6, 0), (2, 15, 0), (2, 16, 0), (0, 3, 5), (0, 4, 4), (2, 17, 0), (2, 18, 0), (0, 3, 6), (0, 5, 2),
    (0, 6, 1), (0, 4, 5), (0, 5, 3), (0, 6, 2), (0, 4, 6), (0, 5, 4), (2, 19, 0), (2, 20, 0), (0, 6, 3), (2, 21, 0),
    (2, 22, 0), (2, 23, 0), (0, 5, 5), (0, 6, 4), (2, 24, 0), (2, 25, 0), (0, 5, 6), (2, 26, 0), (2, 27, 0), (2, 28, 0),
    (0, 6, 5), (2, 29, 0), (2, 30, 0), (2, 31, 0), (0, 6, 6), (2, 32, 0), (2, 33, 0), (2, 34, 0), (2, 35, 0), (2, 36, 0),
    (2, 37, 0), (2, 38, 0), (2, 39, 0), (2, 40, 0),
)


def forward_pass(*refs):
    w_project, w_output, w_expand, w_reduce, tokens, coming, mix, cosine, sine, marks = refs[:10]
    flat = refs[10 : 10 + 3 * ARRAYS]
    outs = [flat[3 * w : 3 * w + 3] for w in range(ARRAYS)]
    (lhs, rhs, query, kv, rows_out, lse, branch_one, middle, branch_two, dn,
     w0, w1, w2, w3, w4, units, entry, lhs_v, rhs_v, top, bottom, joined, native, opened, tiles, lower,
     own_sem, send, recv, csend, crecv, k_send, k_recv, tile_sem, low_sem, move_sem) = refs[10 + 3 * ARRAYS :]
    bf = jnp.bfloat16
    f32 = jnp.float32
    spot = place()
    x, y, z, c = spot
    xh = x // 2
    anchor = ((xh * 4 + y) * 4 + z) * 64
    sibling = (x, y, z, 1 - c)

    def rows_of(p, k, at=None):
        a = [spot[axis] for axis in order(p)]
        if at is not None:
            a[k] = at
        first_row = c * 4 + a[2]
        if k < 2:
            first_row = first_row * 4 + a[1]
        if k < 1:
            first_row = first_row * 4 + a[0]
        size = 16 * 4**k
        return first_row * size, size

    def rows(start, size):
        return pl.ds(pl.multiple_of(start, 16), size)

    def own_copies(w, p):
        n = 128 * WIDTHS[w][p]
        target = outs[w][p].at[rows(*rows_of(p, 0)), :]
        if w < 3:
            views = [((w0, w1, w2)[w].at[:, offsets(w)[p] : offsets(w)[p] + n], target)]
        elif w == 3:
            views = [(w3.at[16 * p : 16 * p + 16, :], target)]
        else:
            half = n // 2
            begin = offsets(w)[p] // 2
            views = [
                (w4.at[:, 2 * UNIT * (2 * (w - 4) + cc) + begin : 2 * UNIT * (2 * (w - 4) + cc) + begin + half],
                 outs[w][p].at[rows(*rows_of(p, 0)), cc * half : (cc + 1) * half])
                for cc in (0, 1)
            ]
        return [pltpu.make_async_copy(src, dst, own_sem.at[w, p, n]) for n, (src, dst) in enumerate(views)]

    def place_own(arrays):
        for w in arrays:
            for p in range(3):
                for copy in own_copies(w, p):
                    copy.start()
        for w in arrays:
            for p in range(3):
                for copy in own_copies(w, p):
                    copy.wait()

    def own_projection():
        w0[...] = w_project[:, 2048:].astype(bf)
        for g in range(8):
            for h in (0, 2):
                both = [w_project[:, (8 * (h + n) + g) * HD : (8 * (h + n) + g + 1) * HD] for n in (0, 1)]
                w1[:, (g * KV + h) * HD : (g * KV + h + 2) * HD] = jnp.concatenate(both, axis=1).astype(bf)
        place_own((0, 1))

    def own_others():
        w2[...] = w_output[...].astype(bf)
        w3[...] = jnp.concatenate([w_reduce[...], jnp.zeros((4, D), f32)], axis=0).astype(bf)
        place_own((2, 3))

    def own_expansion():
        def half(i, carry):
            units[...] = w_expand[:, pl.ds(pl.multiple_of(i * 5632, 128), 5632)].T
            for s in range(3):
                for cc in (0, 1):
                    got = unit_rows(s, cc, lambda d: units[44 * d + 16 * s : 44 * d + min(16 * s + 16, 44), :])
                    w4[:, pl.ds(pl.multiple_of(2 * UNIT * (2 * s + cc) + i * UNIT, UNIT), UNIT)] = got.T.astype(bf)
            return carry

        lax.fori_loop(0, 2, half, 0)
        place_own((4, 5, 6))

    def ring(w, p, k, j):
        axis = order(p)[k]
        if j < 2:
            start, size = rows_of(p, k)
        else:
            start, size = rows_of(p, k, (spot[axis] + 3 + 2 * (j - 2)) % 4)
            if k:
                size = size // 2
                start = start + size * (j - 2)
        view = outs[w][p].at[rows(start, size), :]
        return pltpu.make_async_remote_copy(
            view, view, send.at[w, p, k, j], recv.at[w, p, k, j],
            device_id=ident(*moved(spot, axis, 1 - 2 * (j % 2))), device_id_type=MESH)

    def onward(k):
        return (2, 3) if k else (2,)

    def spread(w, p, slot):
        axis = order(p)[2]
        view = outs[w][p].at[rows(*rows_of(p, 2, (spot[axis] + (0, 3, 1, 2)[slot]) % 4)), :]
        return pltpu.make_async_remote_copy(
            view, view, csend.at[w, p, slot], crecv.at[w, p, slot], device_id=ident(*sibling), device_id_type=MESH)

    def event(w, e):
        k = e // 2
        for p in range(3):
            if e % 2 == 0:
                if k:
                    for j in onward(k - 1):
                        ring(w, p, k - 1, j).wait_recv()
                if e == 6:
                    spread(w, p, 3).start()
                else:
                    ring(w, p, k, 0).start()
                    ring(w, p, k, 1).start()
                    if k == 2:
                        spread(w, p, 0).start()
            else:
                for d in (0, 1):
                    ring(w, p, k, d).wait_recv()
                    if 2 + d in onward(k):
                        ring(w, p, k, 2 + d).start()
                    if k == 2:
                        spread(w, p, 1 + d).start()

    def ready(w):
        for p in range(3):
            for slot in range(4):
                spread(w, p, slot).wait_recv()

    def turn(value, l):
        native_rows = value.T.astype(bf).reshape(2, 4, 4, 2, 2, 16, 128)
        for cc in (0, 1):
            for xx in range(4):
                lhs_v[cc, l, xx] = native_rows[xx // 2, :, :, xx % 2, cc]

    def arrange(l):
        def step(i, carry):
            cc, a = i // 4, i % 4
            for p in range(3):
                if p == 0:
                    got = jnp.concatenate([lhs_v[cc, l, :, b, a].reshape(64, 128) for b in range(4)], axis=0)
                elif p == 1:
                    got = jnp.concatenate([lhs_v[cc, l, a, :, b].reshape(64, 128) for b in range(4)], axis=0)
                else:
                    got = lhs_v[cc, l, :, a].reshape(256, 128)
                entry[p, :, pl.ds(pl.multiple_of(i * 256, 256), 256)] = got.astype(f32).T.astype(bf)
            return carry

        lax.fori_loop(0, 8, step, 0)

    def open_block(i):
        span = slice(32 * i, 32 * i + 32)

        def inside(held, given):
            ins = [pltpu.make_async_copy(tokens.at[span], held, move_sem.at[0]),
                   pltpu.make_async_copy(coming.at[span], given, move_sem.at[1])]
            for copy in ins:
                copy.start()
            for copy in ins:
                copy.wait()
            opened[span, :] = normed_of(entry_of([stream(held, s) for s in range(4)], mix, 0))[0]
            rhs_v[span, 0:D] = sum(weight(mix, 1, t, 1) * stream(given, t) for t in range(4)).astype(bf)

        pl.run_scoped(inside, pltpu.VMEM((32, 4 * D), bf), pltpu.VMEM((32, 4 * D), bf))

    def arrange_first():
        turn(opened[...], 5)
        arrange(5)

    def fetch(w, p, slot, cc=None):
        n = 128 * WIDTHS[w][p]
        view = outs[w][p]
        if cc is not None:
            n = n // 2
            view = view.at[:, cc * n : (cc + 1) * n]
        return pltpu.make_async_copy(view, tiles.at[slot, p, :, 0:n], tile_sem.at[slot, p])

    def multiply(w, slot, out, begin):
        for p in range(3):
            fetch(w, p, slot).start()
        for p in range(3):
            fetch(w, p, slot).wait()
            n = 128 * WIDTHS[w][p]
            lo = begin + offsets(w)[p]
            out[:, lo : lo + n] = jnp.dot(entry[p], tiles[slot, p, :, 0:n], preferred_element_type=f32)

    def project_keys():
        ready(0)
        multiply(0, 0, joined, 2048)

    def keys_turn():
        for m in (0, 1):
            here = slice(m * 64, m * 64 + 64)
            kv[m, xh, y, z, :, 0:256] = turned(joined[here, 2048:2304], cosine[m], -sine[m]).astype(bf)
            kv[m, xh, y, z, :, 256:512] = joined[here, 2304:2560].astype(bf)

    def project_queries():
        ready(1)
        multiply(1, 0, joined, 0)

    def queries_turn():
        for m in (0, 1):
            here = slice(m * 64, m * 64 + 64)
            for g in range(8):
                query[m, g * 64 : (g + 1) * 64, :] = (turned(
                    joined[here, g * 256 : (g + 1) * 256], cosine[m], -sine[m]) * KEY_SCALE).astype(bf)

    cols = [slice(0, 256), slice(256, 512)]

    def kv_hop(m, p, j):
        if j == 0:
            view, to = kv.at[m, xh, y, z, :, cols[p]], moved(spot, 0, 2)
        else:
            k, d = (j - 1) // 4, (j - 1) % 2
            axis = (1, 2)[(p + k) % 2]
            to = moved(spot, axis, 1 - 2 * d)
            if (j - 1) % 4 < 2:
                if k == 0:
                    view = kv.at[m, :, y, z, :, cols[p]]
                elif axis == 2:
                    view = kv.at[m, :, :, z, :, cols[p]]
                else:
                    view = kv.at[m, :, y, :, :, cols[p]]
            else:
                near = (spot[axis] + 3 + 2 * d) % 4
                half = slice(p * 256 + d * 128, p * 256 + d * 128 + 128)
                if k == 0:
                    view = kv.at[m, :, y, near, :, half] if axis == 2 else kv.at[m, :, near, z, :, half]
                else:
                    view = kv.at[m, :, :, near, :, half] if axis == 2 else kv.at[m, :, near, :, :, half]
        return pltpu.make_async_remote_copy(
            view, view, k_send.at[m, p, j], k_recv.at[m, p, j], device_id=ident(*to), device_id_type=MESH)

    def kv_event(m, e):
        for p in range(2):
            if e == 0:
                kv_hop(m, p, 0).start()
            elif e in (1, 3):
                for j in (0,) if e == 1 else (3, 4):
                    kv_hop(m, p, j).wait_recv()
                kv_hop(m, p, 2 * e - 1).start()
                kv_hop(m, p, 2 * e).start()
            elif e in (2, 4):
                for d in (0, 1):
                    kv_hop(m, p, 2 * e - 3 + d).wait_recv()
                    kv_hop(m, p, 2 * e - 1 + d).start()
            else:
                kv_hop(m, p, 7).wait_recv()
                kv_hop(m, p, 8).wait_recv()

    def attend(m, block):
        if block == 0:
            top[...] = jnp.full_like(top, -1e30)
            bottom[...] = jnp.zeros_like(bottom)
            rows_out[m] = jnp.zeros((ROWS, KV * HD), f32)

        @pl.when(block * KB <= anchor + 63)
        def _():
            columns = (block * KB + lax.broadcasted_iota(jnp.int32, (ROWS, KB), 1)).astype(f32)
            keep = (columns >= marks[m, :, 8:9]) & (columns <= marks[m, :, 9:10])
            held = kv[m, block // 2, (block % 2) * 2 : (block % 2) * 2 + 2].reshape(KB, 512)
            done = []
            for h in range(KV):
                lanes = slice(h * HD, (h + 1) * HD)
                s = jnp.where(keep, last(query[m, :, lanes], held[:, lanes]), -1e30)
                high = jnp.maximum(top[h], jnp.max(s, axis=1, keepdims=True))
                fade = jnp.exp(top[h] - high)
                e = jnp.exp(s - high)
                bottom[h] = bottom[h] * fade + jnp.sum(e, axis=1, keepdims=True)
                done.append(rows_out[m, :, lanes] * fade + jnp.dot(
                    e.astype(bf), held[:, 256 + h * HD : 256 + (h + 1) * HD], preferred_element_type=f32))
                top[h] = high
            rows_out[m] = jnp.concatenate(done, axis=1)

        if block == 3:
            rows_out[m] = jnp.concatenate(
                [rows_out[m, :, h * HD : (h + 1) * HD] / bottom[h] for h in range(KV)], axis=1)
            lse[m] = jnp.concatenate(
                [top[h] + jnp.log(bottom[h]) for h in range(KV)] + [jnp.zeros((ROWS, 124), f32)], axis=1)

    def output():
        for g in range(8):
            left = jnp.concatenate([rows_out[m, g * 64 : (g + 1) * 64, :] for m in (0, 1)], axis=0)
            native_rows = left.T.astype(bf).reshape(4, 2, 2, 16, 128)
            for h in range(KV):
                for cc in (0, 1):
                    for xl in (0, 1):
                        lhs_v[cc, 4, 2 * (h // 2) + xl, (h % 2) * 2 + g // 4, g % 4] = native_rows[h, xl, cc]
        arrange(4)
        ready(2)
        multiply(2, 1, branch_one, 0)

    def between():
        def inside(held, made_rows):
            def step(i, carry):
                span = pl.ds(pl.multiple_of(i * 32, 32), 32)
                inward = pltpu.make_async_copy(tokens.at[span], held, move_sem.at[0])
                inward.start()
                inward.wait()
                branch = branch_one[span, :]
                after = None
                for t in range(4):
                    out = mixed_out([stream(held, s) for s in range(4)], branch, mix, 0, t)
                    made_rows[:, t * D : (t + 1) * D] = out
                    term = weight(mix, 1, t, 0) * out
                    after = term if after is None else after + term
                outward = pltpu.make_async_copy(made_rows, middle.at[span], move_sem.at[1])
                outward.start()
                opened[span, :] = normed_of(after)[0]
                outward.wait()
                return carry

            lax.fori_loop(0, 4, step, 0)

        pl.run_scoped(inside, pltpu.VMEM((32, 4 * D), bf), pltpu.VMEM((32, 4 * D), f32))
        turn(opened[...], 3)
        arrange(3)
        branch_two[...] = jnp.zeros_like(branch_two)
        native[...] = jnp.zeros_like(native)

    def low(s, cc):
        return pltpu.make_async_copy(outs[3][s].at[cc * UNIT : (cc + 1) * UNIT, :], lower.at[cc], low_sem.at[cc])

    def feed_start(s):
        if s == 0:
            ready(3)
        ready(4 + s)
        for cc in (0, 1):
            low(s, cc).start()
            for p in range(3):
                fetch(4 + s, p, cc, cc).start()

    def spans(s):
        half = [64 * n for n in WIDTHS[4 + s]]
        return [(0, half[0]), (half[0], half[1]), (half[0] + half[1], half[2])]

    def feed_open(s, cc):
        for p, (lo, n) in enumerate(spans(s)):
            fetch(4 + s, p, cc, cc).wait()
            opened[:, lo : lo + n] = jnp.dot(entry[p], tiles[cc, p, :, 0:n], preferred_element_type=f32)

    def feed_act(s, cc):
        low(s, cc).wait()
        begin = D + 2 * UNIT * (2 * s + cc)

        def act(i, carry):
            lanes = pl.ds(pl.multiple_of(i * 256, 256), 256)
            given = last(rhs_v[:, 0:D], lower[cc, lanes, :])
            gate = opened[:, lanes]
            upper = opened[:, pl.ds(pl.multiple_of(UNIT + i * 256, 256), 256)]
            sigma = jax.nn.sigmoid(gate)
            shut = gate * sigma
            rhs_v[:, pl.ds(pl.multiple_of(begin + i * 256, 256), 256)] = (
                given * upper * sigma * (1.0 + gate * (1.0 - sigma))).astype(bf)
            rhs_v[:, pl.ds(pl.multiple_of(begin + UNIT + i * 256, 256), 256)] = (given * shut).astype(bf)
            opened[:, lanes] = shut * upper
            return carry

        lax.fori_loop(0, UNIT // 256, act, 0)
        hidden = opened[:, 0:UNIT]
        by_axis = hidden.T.astype(bf).reshape(4, 4, 4, 16, 128)
        for a in range(4):
            for b in range(4):
                if s == 0:
                    lhs_v[cc, s, :, b, a] = by_axis[a, b]
                elif s == 1:
                    lhs_v[cc, s, a, :, b] = by_axis[a, b]
                else:
                    lhs_v[cc, s, b, a] = by_axis[a, b]
        branch_two[...] += jnp.dot(hidden.astype(bf), lower[cc], preferred_element_type=f32)

    def feed_back(s, cc):
        begin = D + 2 * UNIT * (2 * s + cc)
        for p, (lo, n) in enumerate(spans(s)):
            put_back(native, p, last(tiles[cc, p, :, 0:n], rhs_v[:, begin + lo : begin + lo + n]))

    def norm_in():
        native_columns(native, dn)

    tasks = {}
    for i in range(4):
        tasks[i] = functools.partial(open_block, i)
    tasks[4], tasks[5], tasks[6], tasks[7], tasks[8] = arrange_first, project_keys, keys_turn, project_queries, queries_turn
    for i in range(8):
        tasks[9 + i] = functools.partial(attend, i // 4, i % 4)
    tasks[17], tasks[18] = output, between
    for s in range(3):
        tasks[19 + 7 * s] = functools.partial(feed_start, s)
        for cc in (0, 1):
            for n, part in enumerate((feed_open, feed_act, feed_back)):
                tasks[20 + 7 * s + 3 * cc + n] = functools.partial(part, s, cc)
    tasks[40], tasks[41], tasks[42] = norm_in, own_others, own_expansion

    barrier = pltpu.get_barrier_semaphore()
    others = [sibling, moved(spot, 0, 2)] + [moved(spot, axis, step) for axis in range(3) for step in (1, 3)]
    for other in others:
        pl.semaphore_signal(barrier, inc=1, device_id=ident(*other), device_id_type=MESH)
    pl.semaphore_wait(barrier, len(others))
    own_projection()
    for kind, a, b in SEQUENCE:
        if kind == 0:
            event(a, b)
        elif kind == 1:
            kv_event(a, b)
        else:
            tasks[a]()

    aways = [pltpu.make_async_copy(lhs_v, lhs, move_sem.at[0]), pltpu.make_async_copy(rhs_v, rhs, move_sem.at[1])]
    for copy in aways:
        copy.start()
    for w in range(ARRAYS):
        for p in range(3):
            for k in range(3):
                for j in (0, 1) + onward(k):
                    ring(w, p, k, j).wait_send()
            for slot in range(4):
                spread(w, p, slot).wait_send()
    for m in (0, 1):
        for p in range(2):
            for j in range(9):
                kv_hop(m, p, j).wait_send()
    for copy in aways:
        copy.wait()


def run_forward(shards, tokens, coming, mix, cosine, sine, marks, collective_id):
    bf = jnp.bfloat16
    f32 = jnp.float32
    v = pltpu.VMEM
    dma = pltpu.SemaphoreType.DMA
    hbm = pl.BlockSpec(memory_space=pl.ANY)
    near = pl.BlockSpec(memory_space=pltpu.VMEM)
    S = jax.ShapeDtypeStruct
    return pl.pallas_call(
        forward_pass,
        out_shape=[S((2048, 128 * n), bf) for widths in WIDTHS for n in widths] + [
            S((2, 6, 4, 4, 4, 16, 128), bf),
            S((128, D + 12 * UNIT), bf),
            S((2, ROWS, 256), bf),
            S((2, 2, 4, 4, 64, 512), bf),
            S((2, ROWS, 256), f32),
            S((2, ROWS, 128), f32),
            S((128, D), f32),
            S((128, 4 * D), f32),
            S((128, D), f32),
            S((128, D), f32),
        ],
        in_specs=[near] * 4 + [hbm] * 2 + [pl.BlockSpec(memory_space=pltpu.SMEM)] + [near] * 3,
        out_specs=[hbm] * (3 * ARRAYS + 2) + [near] * 5 + [hbm] + [near] * 2,
        scratch_shapes=[
            v((16, 512), bf),
            v((16, D), bf),
            v((16, D), bf),
            v((48, D), bf),
            v((16, 12 * UNIT), bf),
            v((5632, 16), f32),
            v((3, 128, D), bf),
            v((2, 6, 4, 4, 4, 16, 128), bf),
            v((128, D + 12 * UNIT), bf),
            v((KV, ROWS, 1), f32),
            v((KV, ROWS, 1), f32),
            v((128, 2560), f32),
            v((2, 4, 4, 2, 2, 16, 128), f32),
            v((128, 2 * UNIT), f32),
            v((2, 3, 2048, 768), bf),
            v((2, UNIT, D), bf),
            dma((ARRAYS, 3, 2)),
            dma((ARRAYS, 3, 3, 4)),
            dma((ARRAYS, 3, 3, 4)),
            dma((ARRAYS, 3, 4)),
            dma((ARRAYS, 3, 4)),
            dma((2, 2, 9)),
            dma((2, 2, 9)),
            dma((2, 3)),
            dma((2,)),
            dma((2,)),
        ],
        compiler_params=pltpu.CompilerParams(
            collective_id=collective_id, has_side_effects=True, vmem_limit_bytes=62 * 1024 * 1024),
    )(*shards, tokens, coming, mix, cosine, sine, marks)


def adam(weight, grad, first, second, factor, rate, decay):
    grad = grad * factor
    first = BETA_ONE * first + (1.0 - BETA_ONE) * grad
    second = BETA_TWO * second + (1.0 - BETA_TWO) * grad * grad
    ahead = first / (1.0 - BETA_ONE**STEP)
    scaled = second / (1.0 - BETA_TWO**STEP)
    weight = weight - rate * (ahead / (jnp.sqrt(scaled) + ADAM_EPS) + decay * weight)
    return (weight, first, second)


def update_kernel(factor, grads, *refs):
    given, outs, ins, units, sems = refs[:12], refs[12:24], refs[24:36], refs[36], refs[37]
    copies = [pltpu.make_async_copy(given[n], ins[n], sems.at[n]) for n in range(12)]
    for copy in copies:
        copy.start()
    for copy in copies:
        copy.wait()

    def write(n, where, grad):
        news = adam(ins[3 * n][where], grad, ins[3 * n + 1][where], ins[3 * n + 2][where],
                    factor[0], RATE_MATRIX, DECAY_MATRIX)
        for out, new in zip(outs[3 * n : 3 * n + 3], news):
            out[where] = new

    everything = (slice(None), slice(None))
    queries = jnp.concatenate([grads[40 + n] for n in range(4)], axis=1)
    pairs = [queries[:, (KV * g + h) * HD : (KV * g + h + 1) * HD] for h in range(KV) for g in range(8)]
    write(0, (slice(None), slice(0, 2048)), jnp.concatenate(pairs, axis=1))
    write(0, (slice(None), slice(2048, 2560)), grads[44])
    write(1, everything, jnp.concatenate([grads[36 + n] for n in range(4)], axis=1))
    for half in (0, 1):
        for s in range(3):
            for cc in (0, 1):
                first_unit = 12 + 4 * (2 * s + cc) + 2 * half
                turned_rows = jnp.concatenate([grads[first_unit], grads[first_unit + 1]], axis=1).T
                for n in range(64):
                    d = unit_place(s, cc, n // 16, (n // 4) % 4, n % 4)
                    size = 12 if s == 2 else 16
                    units[44 * d + 16 * s : 44 * d + 16 * s + size, :] = turned_rows[16 * n : 16 * n + size]
        write(2, (slice(None), slice(half * FF, (half + 1) * FF)), units[...].T)
    for band in range(3):
        size = 12 if band == 2 else 16
        rows = jnp.concatenate([grads[4 * band + n] for n in range(4)], axis=1)
        write(3, (slice(16 * band, 16 * band + size), slice(None)), rows[:size])


def update(factor, grads, arrays):
    near = pl.BlockSpec(memory_space=pltpu.VMEM)
    return pl.pallas_call(
        update_kernel,
        out_shape=[jax.ShapeDtypeStruct(a.shape, jnp.float32) for a in arrays],
        in_specs=[pl.BlockSpec(memory_space=pltpu.SMEM), near] + [pl.BlockSpec(memory_space=pl.ANY)] * 12,
        out_specs=[near] * 12,
        scratch_shapes=[pltpu.VMEM(a.shape, jnp.float32) for a in arrays]
        + [pltpu.VMEM((FF, 16), jnp.float32), pltpu.SemaphoreType.DMA((12,))],
        compiler_params=pltpu.CompilerParams(vmem_limit_bytes=62 * 1024 * 1024),
    )(factor, grads, *arrays)


def tables(spots):
    freq = jnp.exp(jnp.arange(HD // 2, dtype=jnp.float32) * (-2.0 * math.log(THETA_BASE) / HD))
    angle = spots.reshape(2, 64, 1) * freq
    cosine, sine = jnp.cos(angle), jnp.sin(angle)
    return (jnp.tile(jnp.concatenate([cosine, cosine], axis=2), (1, 1, KV)),
            jnp.tile(jnp.concatenate([sine, -sine], axis=2), (1, 1, KV)))


def body(streams, doc_start, cotangent, mixing, w_project, w_output, w_expand, w_reduce,
         first_mixing, second_mixing, first_project, second_project, first_output, second_output,
         first_expand, second_expand, first_reduce, second_reduce):
    bf, f32 = jnp.bfloat16, jnp.float32
    anchor = lax.axis_index("ctx") * 64
    tokens = streams.reshape(128, 8192)
    coming = cotangent.reshape(128, 8192)
    starts = doc_start.reshape(2, 64)
    places = anchor + jnp.arange(64, dtype=jnp.int32)
    spots = (places[None, :] - starts).astype(f32).reshape(128)
    mix = mixing.reshape(48)

    cosine, sine = tables(spots)
    edges = jnp.stack([jnp.tile(starts, (1, 8)), jnp.broadcast_to(jnp.tile(places, 8), (2, ROWS))], axis=2).astype(f32)
    marks = jnp.pad(edges, ((0, 0), (0, 0), (8, 118)))

    got = run_forward([w_project, w_output, w_expand, w_reduce], tokens, coming, mix, cosine, sine, marks, 1)
    pieces, outputs = got[:6], got[6:9]
    lhs, rhs, query, kv, mixed, lse, branch_one, middle, branch_two, dn_two = got[21:]
    middle_grad, grad_one, notes = call(
        between_kernel, mix, [middle, coming, dn_two], [(8192, f32), (2048, bf)], 8)
    dout, stats = output_back(grad_one, outputs, mixed, lse, marks)
    grads, tokens_grad, fresh, total = run_backward(
        lhs, rhs, grad_one, query, dout, kv.reshape(2, 2048, 512), stats, cosine, sine, pieces,
        [tokens, middle_grad, middle, coming, branch_one, branch_two], mix, notes, 2)
    sums = jnp.sum(total, axis=1)
    two, one, zero = sums[:24], sums[24:48], sums[48:]
    mix_total = jnp.stack([
        jnp.concatenate([zero[:4, None], one[4:8, None], one[8:24].reshape(4, 4)], axis=1),
        jnp.concatenate([one[:4, None], two[:4, None], two[4:20].reshape(4, 4)], axis=1),
    ])

    norm = jnp.sqrt(zero[7] + jnp.sum(mix_total * mix_total))
    factor = THRESHOLD / jnp.maximum(norm, THRESHOLD)
    mix_new = adam(mixing, mix_total, first_mixing, second_mixing, factor, RATE_MIXING, 0.0)
    new = update(factor.reshape(1), grads, [
        w_project, first_project, second_project, w_output, first_output, second_output,
        w_expand, first_expand, second_expand, w_reduce, first_reduce, second_reduce])
    return (fresh.reshape(streams.shape), tokens_grad.reshape(streams.shape), norm,
            *mix_new, *new)


def solution(mesh):
    acts = P(None, "fsdp", "ctx", None, None)
    rows = P(("ctx", "fsdp"), None)
    return jax.shard_map(
        body,
        mesh=mesh,
        in_specs=(acts, P(None, "fsdp", "ctx"), acts, P()) + (rows,) * 4 + (P(), P()) + (rows,) * 8,
        out_specs=(acts, acts, P(), P(), P(), P()) + (rows,) * 12,
        check_vma=False,
    )
```

```python
import functools
import math

import jax
import jax.numpy as jnp
from jax import lax
from jax.experimental import pallas as pl
from jax.experimental.pallas import tpu as pltpu
from jax.sharding import PartitionSpec as P

H = 32
FF = 5632
STEP = 10
THETA_BASE = 10000.0
BETA_ONE = 0.9
BETA_TWO = 0.95
ADAM_EPS = 1e-08
RATE_MATRIX = 0.06
RATE_MIXING = 0.5
DECAY_MATRIX = 0.1
THRESHOLD = 1.0


MESH = pl.DeviceIdType.MESH


def place():
    ctx = lax.axis_index("ctx")
    fsdp = lax.axis_index("fsdp")
    return (2 * (ctx // 16) + fsdp // 2, (ctx // 4) % 4, ctx % 4, fsdp % 2)


def ident(x, y, z, c):
    return ((x // 2) * 16 + y * 4 + z, (x % 2) * 2 + c)


def moved(spot, axis, step):
    spot = list(spot)
    spot[axis] = (spot[axis] + step + 4) % 4
    return tuple(spot)


ROWS = 512
HD = 64
KV = 4


UNIT = 1024
WIDTHS = ((2, 1, 1), (6, 6, 4), (4, 6, 6), (16, 16, 16), (12, 12, 8), (8, 12, 12), (6, 4, 6), (6, 4, 6))
ARRAYS = 8


def offsets(w):
    a, b, _ = WIDTHS[w]
    return (0, 128 * a, 128 * (a + b))


def order(p):
    return (p, (p + 1) % 3, (p + 2) % 3)


def last(left, right):
    return lax.dot_general(left, right, (((1,), (1,)), ((), ())), preferred_element_type=jnp.float32)


def first(left, right):
    return lax.dot_general(left, right, (((0,), (0,)), ((), ())), preferred_element_type=jnp.float32)


def put_back(native, p, value, first=0, count=8):
    value = value.reshape(count, 4, 4, 16, 128)
    for i in range(count):
        c, a = (first + i) // 4, (first + i) % 4
        for b in range(4):
            if p == 0:
                native[:, b, a, :, c] += value[i, b].reshape(2, 2, 16, 128)
            elif p == 1:
                native[a // 2, :, b, a % 2, c] += value[i, b]
            else:
                native[b // 2, a, :, b % 2, c] += value[i, b]


def native_columns(native, out):
    for xh in (0, 1):
        for y in range(4):
            out[:, (xh * 4 + y) * 256 : (xh * 4 + y + 1) * 256] = native[xh, y].reshape(256, 128).T


def unit_place(s, c, a, b, n):
    at = [0, 0, 0]
    for axis, value in zip(order(s), (n, b, a)):
        at[axis] = value
    x, y, z = at
    return (x // 2) * 64 + y * 16 + z * 4 + (x % 2) * 2 + c


def unit_rows(s, c, read):
    got = []
    for a in range(4):
        for b in range(4):
            for n in range(4):
                got.append(read(unit_place(s, c, a, b, n)))
                if s == 2:
                    got.append(jnp.zeros((4, 16), jnp.float32))
    return jnp.concatenate(got, axis=0)


TB = 16
D = 2048
NORM_EPS = 1e-05


def stream(ref, s):
    return ref[:, s * D : (s + 1) * D].astype(jnp.float32)


def weight(mix, k, s, j):
    return mix[k * 24 + s * 6 + j]


def entry_of(parts, mix, k):
    return sum(weight(mix, k, s, 0) * parts[s] for s in range(4))


def normed_of(entry):
    center = entry - jnp.mean(entry, axis=-1, keepdims=True)
    inverse = lax.rsqrt(jnp.mean(center * center, axis=-1, keepdims=True) + NORM_EPS)
    return center * inverse, inverse


def norm_back(grad, normed, inverse):
    return inverse * (
        grad
        - jnp.mean(grad, axis=-1, keepdims=True)
        - normed * jnp.mean(grad * normed, axis=-1, keepdims=True)
    )


def mixed_out(parts, branch, mix, k, t):
    return sum(weight(mix, k, s, 2 + t) * parts[s] for s in range(4)) + weight(mix, k, t, 1) * branch


def inner(a, b):
    both = a * b
    folded = both[:, 0:128]
    for j in range(1, D // 128):
        folded = folded + both[:, j * 128 : (j + 1) * 128]
    return jnp.sum(folded, axis=0, keepdims=True)


def note(ref, row, value):
    ref[row : row + 1, :] += value


def start_notes(ref):
    @pl.when(pl.program_id(0) == 0)
    def _():
        ref[...] = jnp.zeros_like(ref)


def between_kernel(mix, middle, coming, dn, middle_grad, grad, notes):
    start_notes(notes)
    normed, inverse = normed_of(entry_of([stream(middle, s) for s in range(4)], mix, 1))
    dx = norm_back(dn[...], normed, inverse)
    e = None
    for s in range(4):
        note(notes, s, inner(stream(middle, s), dx))
        g = sum(weight(mix, 1, s, 2 + t) * stream(coming, t) for t in range(4)) + weight(mix, 1, s, 0) * dx
        middle_grad[:, s * D : (s + 1) * D] = g
        term = weight(mix, 0, s, 1) * g
        e = term if e is None else e + term
    grad[...] = e.astype(jnp.bfloat16)


def call(kernel, mix, arrays, outs, notes=0):
    rows = arrays[0].shape[0]
    shapes = [jax.ShapeDtypeStruct((rows, n), d) for n, d in outs]
    specs = [pl.BlockSpec((TB, n), lambda i: (i, 0)) for n, _ in outs]
    if notes:
        shapes.append(jax.ShapeDtypeStruct((notes, 128), jnp.float32))
        specs.append(pl.BlockSpec((notes, 128), lambda i: (0, 0)))
    return pl.pallas_call(
        kernel,
        out_shape=shapes,
        grid=(rows // TB,),
        in_specs=[pl.BlockSpec(memory_space=pltpu.SMEM)]
        + [pl.BlockSpec((TB, a.shape[1]), lambda i: (i, 0)) for a in arrays],
        out_specs=specs,
        compiler_params=pltpu.CompilerParams(vmem_limit_bytes=62 * 1024 * 1024),
    )(mix, *arrays)


def output_back_kernel(grad, far0, far1, far2, rows_out, lse, marks, dout, stats, native, piece0, piece1, piece2, sems):
    copies = [pltpu.make_async_copy(far, piece, sems.at[n]) for n, (far, piece) in enumerate(
        zip((far0, far1, far2), (piece0, piece1, piece2)))]
    for copy in copies:
        copy.start()
    native[...] = jnp.zeros_like(native)
    for p, piece in enumerate((piece0, piece1, piece2)):
        n = piece.shape[1]
        lo = offsets(2)[p]
        copies[p].wait()

        def step(i, carry, p=p, piece=piece, lo=lo, n=n):
            cc = i // 4
            value = last(piece[pl.ds(pl.multiple_of(i * 256, 256), 256), :], grad[:, lo : lo + n]).reshape(4, 4, 16, 128)
            for b in range(4):
                if p == 0:
                    native[:, b, i % 4, :, cc] += value[b].reshape(2, 2, 16, 128)
                elif p == 1:
                    native[(i % 4) // 2, :, b, i % 2, cc] += value[b]
                else:
                    native[b // 2, i % 4, :, b % 2, cc] += value[b]
            return carry

        lax.fori_loop(0, 8, step, 0)
    for g in range(8):
        turned_rows = jnp.concatenate(
            [native[h // 2, (h % 2) * 2 + g // 4, g % 4].reshape(64, 128) for h in range(KV)], axis=0).T.astype(jnp.bfloat16)
        for m in (0, 1):
            dout[m, g * 64 : (g + 1) * 64, :] = turned_rows[m * 64 : (m + 1) * 64]
    for m in (0, 1):
        lean = [
            jnp.sum(rows_out[m, :, h * HD : (h + 1) * HD] * dout[m, :, h * HD : (h + 1) * HD].astype(jnp.float32),
                    axis=1, keepdims=True)
            for h in range(KV)
        ]
        stats[m] = jnp.concatenate([lse[m, :, 0:4]] + lean + [marks[m, :, 8:]], axis=1)


def output_back(grad, pieces, rows_out, lse, marks):
    near = pl.BlockSpec(memory_space=pltpu.VMEM)
    hbm = pl.BlockSpec(memory_space=pl.ANY)
    return pl.pallas_call(
        output_back_kernel,
        out_shape=[jax.ShapeDtypeStruct((2, ROWS, 256), jnp.bfloat16), jax.ShapeDtypeStruct((2, ROWS, 128), jnp.float32)],
        in_specs=[near, hbm, hbm, hbm, near, near, near],
        out_specs=[near, near],
        scratch_shapes=[pltpu.VMEM((2, 4, 4, 2, 2, 16, 128), jnp.float32)]
        + [pltpu.VMEM(piece.shape, piece.dtype) for piece in pieces] + [pltpu.SemaphoreType.DMA((3,))],
        compiler_params=pltpu.CompilerParams(vmem_limit_bytes=62 * 1024 * 1024),
    )(grad, *pieces, rows_out, lse, marks)


W = 512
HALF = 256
UNITS = 45
CHUNKS = 15
SLOTS = 2
STAGES = 6
COLS = 2048 + 12288 + 2048 + 2560
JOINED = 16384
KB = 512
KEY_SCALE = HD**-0.5


def unit_spot(u):
    early = u // 12
    early = 1 - (1 // (1 + early))
    left = (1 - early) * (u // 4) + early * (3 + u // 36 + u // 40)
    column = (1 - early) * ((u % 4) * W) + early * (2048 + (u - 12) * W)
    return left, pl.multiple_of(column, W)


def turned(x, cosine, sine):
    lane = lax.broadcasted_iota(jnp.int32, x.shape, 1)
    swapped = jnp.where(lane % HD < HD // 2, pltpu.roll(x, x.shape[1] - HD // 2, 1), pltpu.roll(x, HD // 2, 1))
    return x * cosine + swapped * sine


def backward_pass(lhs, rhs, grad_one, query, dout, kv, stats, cosine, sine, keys0, keys1, keys2, query0, query1, query2, tokens, middle_grad, middle, coming, branch_one, branch_two, mix, notes_in,
                  grads, tokens_grad, fresh, total, left, right, acc1, acc2,
                  sa, ra, sb, rb, sc, rc, sd, rd, se, re, sf, rf, vsend, vrecv, out,
                  dq, terms, k1, k2, k3s, k3, k4s, k4, k5s, k5, kacc, kacc2, dn, native, notes,
                  send_sem, recv_sem, free_sem, local_sem, side_send, side_recv, out_sem, v_send_sem, v_recv_sem,
                  k_send, k_recv, tile_sem, late_send, late_recv):
    bf = jnp.bfloat16
    f32 = jnp.float32
    spot = place()
    x, y, z, c = spot
    pos = (x, y, z)
    xh = x // 2
    anchor = ((xh * 4 + y) * 4 + z) * 64
    sibling = (x, y, z, 1 - c)
    barrier = pltpu.get_barrier_semaphore()
    others = [sibling] + [moved(spot, axis, step) for axis in range(3) for step in (1, 2, 3)]
    for other in others:
        pl.semaphore_signal(barrier, inc=1, device_id=ident(*other), device_id_type=MESH)
    pl.semaphore_wait(barrier, len(others))

    parts = (((0, 3), (0, 2048)), ((3, 4), (2048, 14336)), ((4, 6), (14336, JOINED)))
    moves = []
    for j, ((l0, l1), (c0, c1)) in enumerate(parts):
        source = grad_one if j == 2 else rhs.at[:, c0:c1]
        own = [
            pltpu.make_async_copy(lhs.at[c, l0:l1], left.at[l0:l1, :, :, :, :, 0:128], local_sem.at[j, 0]),
            pltpu.make_async_copy(source, right.at[0:128, c0:c1], local_sem.at[j, 1]),
        ]
        far = [
            pltpu.make_async_remote_copy(
                lhs.at[1 - c, l0:l1], left.at[l0:l1, :, :, :, :, 128:256], side_send.at[j, 0], side_recv.at[j, 0],
                device_id=ident(*sibling), device_id_type=MESH),
            pltpu.make_async_remote_copy(
                source, right.at[128:256, c0:c1], side_send.at[j, 1], side_recv.at[j, 1],
                device_id=ident(*sibling), device_id_type=MESH),
        ]
        for copy in own + far:
            copy.start()
        moves.append((own, far))
    late = pltpu.make_async_remote_copy(
        right.at[0:128, JOINED:COLS], right.at[128:256, JOINED:COLS], late_send, late_recv,
        device_id=ident(*sibling), device_id_type=MESH)

    def arrive(j):
        for copy in moves[j][0]:
            copy.wait()
        for copy in moves[j][1]:
            copy.wait_recv()

    arrive(0)
    dq[...] = jnp.zeros_like(dq)
    notes[...] = jnp.zeros_like(notes)
    notes[24:32, :] = notes_in[...]
    native[...] = jnp.zeros_like(native)

    sends = (sa, sb, sc, sd, se, sf)
    recvs = (ra, rb, rc, rd, re, rf)

    def hop(stage, p, d, slot):
        axis = (p + stage // 2) % 3
        return pltpu.make_async_remote_copy(
            sends[stage].at[p, d, slot], recvs[stage].at[p, d, slot],
            send_sem.at[stage, p, d, slot], recv_sem.at[stage, p, d, slot],
            device_id=ident(*moved(spot, axis, 1 - 2 * d)), device_id_type=MESH)

    def before_send(stage, p, q):
        @pl.when(q >= SLOTS)
        def _():
            for d in (0, 1):
                hop(stage, p, d, q % SLOTS).wait_send()
                pl.semaphore_wait(free_sem.at[stage, p, d], 1)

    def give_back(stage, p, q):
        @pl.when(q < CHUNKS - SLOTS)
        def _():
            axis = (p + stage // 2) % 3
            for d in (0, 1):
                pl.semaphore_signal(free_sem.at[stage, p, d], inc=1,
                                    device_id=ident(*moved(spot, axis, 2 * d - 1)), device_id_type=MESH)

    def go(stage, p, q):
        for d in (0, 1):
            hop(stage, p, d, q % SLOTS).start()

    def come(stage, p, q):
        for d in (0, 1):
            hop(stage, p, d, q % SLOTS).wait_recv()

    def rows(p, l, a):
        if p == 0:
            got = left[l, a]
        elif p == 1:
            got = left[l, :, a]
        else:
            got = left[l, :, :, a]
        return got.reshape(256, 256)

    def product(p, q, a, lo, hi):
        l, column = unit_spot(3 * q + p)
        return jnp.dot(rows(p, l, a), right[:, pl.ds(pl.multiple_of(column + lo, HALF), hi - lo)],
                       preferred_element_type=f32)

    def at(p, step):
        return (pos[p] + step + 4) % 4

    def stage1(q):
        s = q % SLOTS
        for p in range(3):
            before_send(0, p, q)
            for d in (0, 1):
                sa[p, d, s] = product(p, q, at(p, 2), d * HALF, d * HALF + HALF).astype(bf)
            go(0, p, q)

    def stage2(q):
        s = q % SLOTS
        for p in range(3):
            before_send(1, p, q)
            come(0, p, q)
            for d in (0, 1):
                lo = d * HALF
                near = at(p, 1 - 2 * d)
                sb[p, d, s, :, lo : lo + HALF] = (
                    product(p, q, near, lo, lo + HALF) + ra[p, d, s].astype(f32)).astype(bf)
                other = HALF - lo
                sb[p, d, s, :, other : other + HALF] = product(p, q, near, other, other + HALF).astype(bf)
            give_back(0, p, q)
            go(1, p, q)

    def part(p, ref, b):
        return ref.at[:, b] if p == 1 else ref.at[b]

    def stage3(q):
        s = q % SLOTS
        for p in range(3):
            come(1, p, q)
            for lo in (0, HALF):
                both = (product(p, q, pos[p], lo, lo + HALF)
                        + rb[p, 0, s, :, lo : lo + HALF].astype(f32) + rb[p, 1, s, :, lo : lo + HALF].astype(f32))
                acc1[p, s, :, :, :, lo : lo + HALF] = both.reshape(4, 4, 16, HALF)
            give_back(1, p, q)
            before_send(2, p, q)
            ahead = at((p + 1) % 3, 2)
            for d in (0, 1):
                sc[p, d, s] = part(p, acc1.at[p, s], ahead)[:, :, d * HALF : d * HALF + HALF].astype(bf)
            go(2, p, q)

    def stage4(q):
        s = q % SLOTS
        for p in range(3):
            before_send(3, p, q)
            come(2, p, q)
            for d in (0, 1):
                lo = d * HALF
                other = HALF - lo
                mine = part(p, acc1.at[p, s], at((p + 1) % 3, 1 - 2 * d))
                sd[p, d, s, :, :, lo : lo + HALF] = (
                    mine[:, :, lo : lo + HALF] + rc[p, d, s].astype(f32)).astype(bf)
                sd[p, d, s, :, :, other : other + HALF] = mine[:, :, other : other + HALF].astype(bf)
            give_back(2, p, q)
            go(3, p, q)

    def stage5(q):
        s = q % SLOTS
        for p in range(3):
            come(3, p, q)
            acc2[p, s] = (part(p, acc1.at[p, s], pos[(p + 1) % 3])[...]
                          + rd[p, 0, s].astype(f32) + rd[p, 1, s].astype(f32))
            give_back(3, p, q)
            before_send(4, p, q)
            ahead = at((p + 2) % 3, 2)
            for d in (0, 1):
                se[p, d, s] = acc2[p, s, ahead, :, d * HALF : d * HALF + HALF].astype(bf)
            go(4, p, q)

    def stage6(q):
        s = q % SLOTS
        for p in range(3):
            before_send(5, p, q)
            come(4, p, q)
            for d in (0, 1):
                lo = d * HALF
                other = HALF - lo
                near = at((p + 2) % 3, 1 - 2 * d)
                sf[p, d, s, :, lo : lo + HALF] = (
                    acc2[p, s, near, :, lo : lo + HALF] + re[p, d, s].astype(f32)).astype(bf)
                sf[p, d, s, :, other : other + HALF] = acc2[p, s, near, :, other : other + HALF].astype(bf)
            give_back(4, p, q)
            go(5, p, q)

    def stage7(q):
        s = q % SLOTS
        for p in range(3):
            come(5, p, q)
            out[3 * q + p] = (acc2[p, s, pos[(p + 2) % 3]]
                              + rf[p, 0, s].astype(f32) + rf[p, 1, s].astype(f32))
            give_back(5, p, q)

    def attend(m, block):
        where = (m, block // 2, pl.ds((block % 2) * 2, 2))

        @pl.when(block * KB <= anchor + 63)
        def _():
            columns = (block * KB + lax.broadcasted_iota(jnp.int32, (ROWS, KB), 1)).astype(f32)
            keep = (columns >= stats[m, :, 8:9]) & (columns <= stats[m, :, 9:10])
            span = pl.ds(pl.multiple_of(block * KB, KB), KB)
            keys, values, queries = [], [], []
            for h in range(KV):
                lanes = slice(h * HD, (h + 1) * HD)
                k = kv[m, span, lanes]
                v = kv[m, span, 256 + h * HD : 256 + (h + 1) * HD]
                qh = query[m, :, lanes]
                doh = dout[m, :, lanes]
                p = jnp.exp(jnp.where(keep, last(qh, k) - stats[m, :, h : h + 1], -1e30))
                ds = (p * (last(doh, v) - stats[m, :, 4 + h : 5 + h])).astype(bf)
                queries.append(jnp.dot(ds, k, preferred_element_type=f32) * KEY_SCALE)
                keys.append(first(ds, qh))
                values.append(first(p.astype(bf), doh))
            dq[m] += jnp.concatenate(queries, axis=1)
            terms[where] = jnp.concatenate(keys + values, axis=1).astype(bf).reshape(2, 4, 64, 512)

        @pl.when(block * KB > anchor + 63)
        def _():
            terms[where] = jnp.zeros((2, 4, 64, 512), bf)

    cols = [slice(0, 256), slice(256, 512)]
    axes = [(2, 1), (1, 2)]

    def view(p, m, a):
        return terms.at[m, :, :, a, :, cols[p]] if p == 0 else terms.at[m, :, a, :, :, cols[p]]

    def khop(stage, p, d):
        if stage == 4:
            src, dst, to = k5s.at[p], k5.at[p], moved(spot, 0, 2)
        else:
            axis = axes[p][stage // 2]
            to = moved(spot, axis, 1 - 2 * d)
            if stage == 0:
                src, dst = view(p, d, (spot[axis] + 2) % 4), k1.at[p, d]
            elif stage == 1:
                src, dst = view(p, slice(None), (spot[axis] + 1 + 2 * d) % 4), k2.at[p, d]
            elif stage == 2:
                src, dst = k3s.at[p, d], k3.at[p, d]
            else:
                src, dst = k4s.at[p, d], k4.at[p, d]
        return pltpu.make_async_remote_copy(
            src, dst, k_send.at[stage, p, d], k_recv.at[stage, p, d], device_id=ident(*to), device_id_type=MESH)

    def terms1():
        for p in range(2):
            for d in (0, 1):
                khop(0, p, d).start()

    def terms2():
        for p in range(2):
            for d in (0, 1):
                khop(0, p, d).wait_recv()
                mine = view(p, d, (spot[axes[p][0]] + 1 + 2 * d) % 4)
                mine[...] = (mine[...].astype(f32) + k1[p, d].astype(f32)).astype(bf)
                khop(1, p, d).start()

    def terms3():
        for p in range(2):
            for d in (0, 1):
                khop(1, p, d).wait_recv()
            for m in (0, 1):
                kacc[p, m] = (view(p, m, spot[axes[p][0]])[...].astype(f32)
                              + k2[p, 0, m].astype(f32) + k2[p, 1, m].astype(f32))
            for d in (0, 1):
                k3s[p, d] = kacc[p, d, :, (spot[axes[p][1]] + 2) % 4].astype(bf)
                khop(2, p, d).start()

    def terms4():
        for p in range(2):
            for d in (0, 1):
                near = (spot[axes[p][1]] + 1 + 2 * d) % 4
                khop(2, p, d).wait_recv()
                k4s[p, d, d] = (kacc[p, d, :, near] + k3[p, d].astype(f32)).astype(bf)
                k4s[p, d, 1 - d] = kacc[p, 1 - d, :, near].astype(bf)
                khop(3, p, d).start()

    def terms5():
        for p in range(2):
            for d in (0, 1):
                khop(3, p, d).wait_recv()
            kacc2[p] = kacc[p, :, :, spot[axes[p][1]]] + k4[p, 0].astype(f32) + k4[p, 1].astype(f32)
            k5s[p] = kacc2[p, :, 1 - xh].astype(bf)
            khop(4, p, 0).start()

    def join():
        for m in (0, 1):
            here = slice(m * 64, m * 64 + 64)
            for g in range(8):
                right[here, JOINED + g * 256 : JOINED + (g + 1) * 256] = turned(
                    dq[m, g * 64 : (g + 1) * 64, :], cosine[m], sine[m]).astype(bf)
        for p in range(2):
            khop(4, p, 0).wait_recv()
        for m in (0, 1):
            here = slice(m * 64, m * 64 + 64)
            right[here, JOINED + 2048 : JOINED + 2304] = turned(
                kacc2[0, m, xh] + k5[0, m].astype(f32), cosine[m], sine[m]).astype(bf)
            right[here, JOINED + 2304 : COLS] = (kacc2[1, m, xh] + k5[1, m].astype(f32)).astype(bf)
        late.start()

    def entry(i):
        def inside(tiles):
            def copies(p):
                made = []
                for a, piece in enumerate(((keys0, keys1, keys2)[p], (query0, query1, query2)[p])):
                    n = piece.shape[1]
                    made.append(pltpu.make_async_copy(
                        piece.at[pl.ds(pl.multiple_of(i * 512, 512), 512)], tiles.at[p, a, :, 0:n], tile_sem.at[p, a]))
                return made

            for p in range(3):
                for copy in copies(p):
                    copy.start()
            for p in range(3):
                for copy in copies(p):
                    copy.wait()
                value = None
                for a, w in enumerate((0, 1)):
                    n = 128 * WIDTHS[w][p]
                    lo = JOINED + (2048 if w == 0 else 0) + offsets(w)[p]
                    term = last(tiles[p, a, :, 0:n], right[0:128, lo : lo + n])
                    value = term if value is None else value + term
                value = value.reshape(2, 4, 4, 16, 128)
                for r in (0, 1):
                    cc = i // 2
                    at_last = (i % 2) * 2 + r
                    for b in range(4):
                        if p == 0:
                            native[:, b, at_last, :, cc] += value[r, b].reshape(2, 2, 16, 128)
                        elif p == 1:
                            native[i % 2, :, b, r, cc] += value[r, b]
                        else:
                            native[b // 2, at_last, :, b % 2, cc] += value[r, b]

        pl.run_scoped(inside, pltpu.VMEM((3, 2, 512, 768), bf))

        @pl.when(i == 3)
        def _():
            native_columns(native, dn)

    def finish(i):
        span = pl.ds(pl.multiple_of(i * 32, 32), 32)

        def inside(held, grad, branch, back):
            ins = [pltpu.make_async_copy(tokens.at[span], held, tile_sem.at[0, 0]),
                   pltpu.make_async_copy(middle_grad.at[span], grad, tile_sem.at[1, 0]),
                   pltpu.make_async_copy(branch_one.at[span], branch, tile_sem.at[2, 0])]
            for copy in ins:
                copy.start()
            for copy in ins:
                copy.wait()
            normed, inverse = normed_of(entry_of([stream(held, s) for s in range(4)], mix, 0))
            dx = norm_back(dn[span, :], normed, inverse)
            for s in range(4):
                note(notes, 48 + s, inner(stream(held, s), dx))
                back[:, s * D : (s + 1) * D] = (
                    sum(weight(mix, 0, s, 2 + t) * stream(grad, t) for t in range(4)) + weight(mix, 0, s, 0) * dx)
            away = pltpu.make_async_copy(back, tokens_grad.at[span], tile_sem.at[0, 0])
            away.start()
            for s in range(4):
                g = stream(grad, s)
                note(notes, 28 + s, inner(branch[...], g))
                for r in range(4):
                    note(notes, 32 + 4 * r + s, inner(stream(held, r), g))
            away.wait()

        pl.run_scoped(inside, pltpu.VMEM((32, 4 * D), bf), pltpu.VMEM((32, 4 * D), f32),
                      pltpu.VMEM((32, D), f32), pltpu.VMEM((32, 4 * D), f32))

    def close(i):
        span = pl.ds(pl.multiple_of(i * 32, 32), 32)

        def inside(after, given, branch, made):
            ins = [pltpu.make_async_copy(middle.at[span], after, tile_sem.at[0, 0]),
                   pltpu.make_async_copy(coming.at[span], given, tile_sem.at[1, 0]),
                   pltpu.make_async_copy(branch_two.at[span], branch, tile_sem.at[2, 0])]
            for copy in ins:
                copy.start()
            for copy in ins:
                copy.wait()
            for t in range(4):
                made[:, t * D : (t + 1) * D] = mixed_out(
                    [stream(after, s) for s in range(4)], branch[...], mix, 1, t).astype(bf)
            away = pltpu.make_async_copy(made, fresh.at[span], tile_sem.at[0, 0])
            away.start()
            for t in range(4):
                g = stream(given, t)
                note(notes, t, inner(branch[...], g))
                for s in range(4):
                    note(notes, 4 + 4 * s + t, inner(stream(after, s), g))
            away.wait()

        pl.run_scoped(inside, pltpu.VMEM((32, 4 * D), f32), pltpu.VMEM((32, 4 * D), bf),
                      pltpu.VMEM((32, D), f32), pltpu.VMEM((32, 4 * D), bf))

    def step(t, carry):
        @pl.when(t == 4)
        def _():
            arrive(1)

        @pl.when(t == 12)
        def _():
            arrive(2)

        @pl.when(t == 13)
        def _():
            late.wait_recv()

        stages = (stage1, stage2, stage3, stage4, stage5, stage6, stage7)
        for lag in (0, 1, 6, 5, 4, 3, 2):
            @pl.when((t >= lag) & (t < CHUNKS + lag))
            def _(lag=lag):
                stages[lag](t - lag)

        @pl.when(t < 2)
        def _():
            attend(0, 2 * t)
            attend(0, 2 * t + 1)

        @pl.when((t >= 2) & (t < 6))
        def _():
            attend(1, t - 2)

        @pl.when((t >= 6) & (t < 10))
        def _():
            close(t - 6)

        for when, task in ((5, terms1), (6, terms2), (7, terms3), (8, terms4), (9, terms5), (10, join)):
            pl.when(t == when)(task)

        @pl.when((t >= 11) & (t < 15))
        def _():
            entry(t - 11)

        @pl.when((t >= 15) & (t < 19))
        def _():
            finish(t - 15)
        return carry

    lax.fori_loop(0, CHUNKS + 6, step, 0)

    def tail(q, carry):
        for stage in range(STAGES):
            for p in range(3):
                for d in (0, 1):
                    hop(stage, p, d, q % SLOTS).wait_send()
        return carry

    lax.fori_loop(CHUNKS - SLOTS, CHUNKS, tail, 0)
    for own, far in moves:
        for copy in far:
            copy.wait_send()
    late.wait_send()
    for stage in range(5):
        for p in range(2):
            for d in (0, 1) if stage < 4 else (0,):
                khop(stage, p, d).wait_send()

    write = pltpu.make_async_copy(out, grads, out_sem)
    write.start()

    def squares(u, carry):
        g = out[u]
        return carry + g * g

    summed = lax.fori_loop(0, UNITS, squares, jnp.zeros((16, W), f32))
    lanes = jnp.sum(summed, axis=0, keepdims=True)
    lanes = lanes[:, 0:128] + lanes[:, 128:256] + lanes[:, 256:384] + lanes[:, 384:512]
    notes[55:56, :] = lanes
    vector = notes[...]
    for phase in range(4):
        vsend[phase] = vector
        if phase == 0:
            targets = [(0, sibling)]
        else:
            targets = [(step - 1, moved(spot, phase - 1, step)) for step in (1, 2, 3)]
        copies = [
            pltpu.make_async_remote_copy(
                vsend.at[phase], vrecv.at[phase, k], v_send_sem.at[phase, k], v_recv_sem.at[phase, k],
                device_id=ident(*to), device_id_type=MESH)
            for k, to in targets
        ]
        for copy in copies:
            copy.start()
        for copy in copies:
            copy.wait()
        for k, _ in targets:
            vector = vector + vrecv[phase, k]
    total[...] = vector
    write.wait()


def run_backward(lhs, rhs, grad_one, query, dout, kv, stats, cosine, sine, pieces, arrays, mix, notes, collective_id):
    bf = jnp.bfloat16
    f32 = jnp.float32
    v = pltpu.VMEM
    dma = pltpu.SemaphoreType.DMA
    pair = lambda shape: [v((3, 2, SLOTS) + shape, bf)] * 2
    hbm = pl.BlockSpec(memory_space=pl.ANY)
    near = pl.BlockSpec(memory_space=pltpu.VMEM)
    return pl.pallas_call(
        backward_pass,
        out_shape=[jax.ShapeDtypeStruct((UNITS, 16, W), f32), jax.ShapeDtypeStruct((128, 4 * D), f32),
                   jax.ShapeDtypeStruct((128, 4 * D), bf), jax.ShapeDtypeStruct((56, 128), f32)],
        in_specs=[hbm, hbm, hbm, near, near, near, near, near, near] + [hbm] * 12 + [
                  pl.BlockSpec(memory_space=pltpu.SMEM), near],
        out_specs=[hbm, hbm, hbm, near],
        scratch_shapes=[
            v((6, 4, 4, 4, 16, 256), bf),
            v((256, COLS), bf),
            v((3, SLOTS, 4, 4, 16, W), f32),
            v((3, SLOTS, 4, 16, W), f32),
            *pair((256, HALF)),
            *pair((256, W)),
            *pair((4, 16, HALF)),
            *pair((4, 16, W)),
            *pair((16, HALF)),
            *pair((16, W)),
            v((4, 56, 128), f32),
            v((4, 3, 56, 128), f32),
            v((UNITS, 16, W), f32),
            v((2, ROWS, 256), f32),
            v((2, 2, 4, 4, 64, 512), bf),
            v((2, 2, 2, 4, 64, 256), bf),
            v((2, 2, 2, 2, 4, 64, 256), bf),
            v((2, 2, 2, 64, 256), bf), v((2, 2, 2, 64, 256), bf),
            v((2, 2, 2, 2, 64, 256), bf), v((2, 2, 2, 2, 64, 256), bf),
            v((2, 2, 64, 256), bf), v((2, 2, 64, 256), bf),
            v((2, 2, 2, 4, 64, 256), f32), v((2, 2, 2, 64, 256), f32),
            v((128, D), f32),
            v((2, 4, 4, 2, 2, 16, 128), f32),
            v((56, 128), f32),
            dma((STAGES, 3, 2, SLOTS)),
            dma((STAGES, 3, 2, SLOTS)),
            pltpu.SemaphoreType.REGULAR((STAGES, 3, 2)),
            dma((3, 2)),
            dma((3, 2)),
            dma((3, 2)),
            dma,
            dma((4, 3)),
            dma((4, 3)),
            dma((5, 2, 2)),
            dma((5, 2, 2)),
            dma((3, 2)),
            dma,
            dma,
        ],
        compiler_params=pltpu.CompilerParams(
            collective_id=collective_id, has_side_effects=True, vmem_limit_bytes=62 * 1024 * 1024),
    )(lhs, rhs, grad_one, query, dout, kv, stats, cosine, sine, *pieces, *arrays, mix, notes)


SEQUENCE = (
    (0, 0, 0), (0, 1, 0), (2, 41, 0), (0, 2, 0), (0, 3, 0), (0, 0, 1), (0, 1, 1), (2, 0, 0), (0, 2, 1), (2, 1, 0),
    (0, 0, 2), (0, 1, 2), (0, 2, 2), (2, 2, 0), (0, 0, 3), (0, 3, 1), (0, 1, 3), (2, 3, 0), (0, 0, 4), (0, 2, 3),
    (0, 3, 2), (2, 4, 0), (0, 0, 5), (0, 1, 4), (0, 0, 6), (0, 2, 4), (2, 5, 0), (2, 6, 0), (1, 0, 0), (1, 1, 0),
    (0, 1, 5), (2, 42, 0), (1, 0, 1), (0, 2, 5), (1, 1, 1), (1, 0, 2), (0, 3, 3), (0, 1, 6), (0, 4, 0), (0, 5, 0),
    (1, 1, 2), (0, 2, 6), (1, 0, 3), (2, 7, 0), (1, 1, 3), (2, 8, 0), (1, 0, 4), (0, 4, 1), (0, 5, 1), (0, 6, 0),
    (1, 1, 4), (0, 7, 0), (1, 0, 5), (2, 9, 0), (0, 4, 2), (1, 1, 5), (0, 3, 4), (2, 10, 0), (2, 11, 0), (2, 12, 0),
    (0, 4, 3), (0, 5, 2), (2, 13, 0), (0, 6, 1), (0, 7, 1), (2, 14, 0), (2, 15, 0), (0, 3, 5), (2, 16, 0), (0, 4, 4),
    (2, 17, 0), (0, 5, 3), (0, 3, 6), (2, 18, 0), (0, 6, 2), (0, 7, 2), (2, 49, 0), (0, 4, 5), (0, 5, 4), (2, 50, 0),
    (2, 51, 0), (0, 4, 6), (0, 6, 3), (0, 7, 3), (2, 43, 0), (2, 44, 0), (2, 20, 0), (2, 21, 0), (0, 5, 5), (0, 6, 4),
    (2, 22, 0), (0, 7, 4), (2, 23, 0), (2, 24, 0), (0, 5, 6), (2, 25, 0), (2, 45, 0), (2, 46, 0), (0, 6, 5), (2, 27, 0),
    (2, 28, 0), (2, 29, 0), (0, 7, 5), (0, 6, 6), (2, 30, 0), (2, 47, 0), (2, 31, 0), (0, 7, 6), (2, 32, 0), (2, 48, 0),
    (2, 34, 0), (2, 35, 0), (2, 36, 0), (2, 37, 0), (2, 38, 0), (2, 39, 0), (2, 40, 0),
)


def forward_pass(*refs):
    w_project, w_output, w_expand, w_reduce, tokens, coming, mix, cosine, sine, marks = refs[:10]
    flat = refs[10 : 10 + 3 * ARRAYS]
    outs = [flat[3 * w : 3 * w + 3] for w in range(ARRAYS)]
    (lhs, rhs, query, kv, rows_out, lse, branch_one, middle, branch_two, dn,
     w0, w1, w2, w3, w4, units, entry, lhs_v, rhs_v, dz, top, bottom, joined, native, opened, tiles, lower,
     own_sem, send, recv, csend, crecv, k_send, k_recv, tile_sem, low_sem, move_sem) = refs[10 + 3 * ARRAYS :]
    bf = jnp.bfloat16
    f32 = jnp.float32
    spot = place()
    x, y, z, c = spot
    xh = x // 2
    anchor = ((xh * 4 + y) * 4 + z) * 64
    sibling = (x, y, z, 1 - c)

    def rows_of(p, k, at=None):
        a = [spot[axis] for axis in order(p)]
        if at is not None:
            a[k] = at
        first_row = c * 4 + a[2]
        if k < 2:
            first_row = first_row * 4 + a[1]
        if k < 1:
            first_row = first_row * 4 + a[0]
        size = 16 * 4**k
        return first_row * size, size

    def rows(start, size):
        return pl.ds(pl.multiple_of(start, 16), size)

    def own_copies(w, p):
        n = 128 * WIDTHS[w][p]
        target = outs[w][p].at[rows(*rows_of(p, 0)), :]
        if w < 3:
            views = [((w0, w1, w2)[w].at[:, offsets(w)[p] : offsets(w)[p] + n], target)]
        elif w == 3:
            views = [(w3.at[16 * p : 16 * p + 16, :], target)]
        elif w > 5:
            begin = 2 * UNIT * (w - 2) + offsets(w)[p]
            views = [(w4.at[:, begin : begin + n], target)]
        else:
            half = n // 2
            begin = offsets(w)[p] // 2
            views = [
                (w4.at[:, 2 * UNIT * (2 * (w - 4) + cc) + begin : 2 * UNIT * (2 * (w - 4) + cc) + begin + half],
                 outs[w][p].at[rows(*rows_of(p, 0)), cc * half : (cc + 1) * half])
                for cc in (0, 1)
            ]
        return [pltpu.make_async_copy(src, dst, own_sem.at[w, p, n]) for n, (src, dst) in enumerate(views)]

    def place_own(arrays):
        for w in arrays:
            for p in range(3):
                for copy in own_copies(w, p):
                    copy.start()
        for w in arrays:
            for p in range(3):
                for copy in own_copies(w, p):
                    copy.wait()

    def own_projection():
        w0[...] = w_project[:, 2048:].astype(bf)
        for g in range(8):
            for h in (0, 2):
                both = [w_project[:, (8 * (h + n) + g) * HD : (8 * (h + n) + g + 1) * HD] for n in (0, 1)]
                w1[:, (g * KV + h) * HD : (g * KV + h + 2) * HD] = jnp.concatenate(both, axis=1).astype(bf)
        place_own((0, 1))

    def own_others():
        w2[...] = w_output[...].astype(bf)
        w3[...] = jnp.concatenate([w_reduce[...], jnp.zeros((4, D), f32)], axis=0).astype(bf)
        place_own((2, 3))

    def own_expansion():
        def half(i, carry):
            units[...] = w_expand[:, pl.ds(pl.multiple_of(i * 5632, 128), 5632)].T
            for s in range(3):
                for cc in (0, 1):
                    got = unit_rows(s, cc, lambda d: units[44 * d + 16 * s : 44 * d + min(16 * s + 16, 44), :])
                    w4[:, pl.ds(pl.multiple_of(2 * UNIT * (2 * s + cc) + i * UNIT, UNIT), UNIT)] = got.T.astype(bf)
            return carry

        lax.fori_loop(0, 2, half, 0)
        place_own((4, 5, 6, 7))

    def ring(w, p, k, j):
        axis = order(p)[k]
        if j < 2:
            start, size = rows_of(p, k)
        else:
            start, size = rows_of(p, k, (spot[axis] + 3 + 2 * (j - 2)) % 4)
            if k:
                size = size // 2
                start = start + size * (j - 2)
        view = outs[w][p].at[rows(start, size), :]
        return pltpu.make_async_remote_copy(
            view, view, send.at[w, p, k, j], recv.at[w, p, k, j],
            device_id=ident(*moved(spot, axis, 1 - 2 * (j % 2))), device_id_type=MESH)

    def onward(k):
        return (2, 3) if k else (2,)

    def spread(w, p, slot):
        axis = order(p)[2]
        view = outs[w][p].at[rows(*rows_of(p, 2, (spot[axis] + (0, 3, 1, 2)[slot]) % 4)), :]
        return pltpu.make_async_remote_copy(
            view, view, csend.at[w, p, slot], crecv.at[w, p, slot], device_id=ident(*sibling), device_id_type=MESH)

    def event(w, e):
        k = e // 2
        for p in range(3):
            if e % 2 == 0:
                if k:
                    for j in onward(k - 1):
                        ring(w, p, k - 1, j).wait_recv()
                if e == 6:
                    spread(w, p, 3).start()
                else:
                    ring(w, p, k, 0).start()
                    ring(w, p, k, 1).start()
                    if k == 2:
                        spread(w, p, 0).start()
            else:
                for d in (0, 1):
                    ring(w, p, k, d).wait_recv()
                    if 2 + d in onward(k):
                        ring(w, p, k, 2 + d).start()
                    if k == 2:
                        spread(w, p, 1 + d).start()

    def ready(w):
        for p in range(3):
            for slot in range(4):
                spread(w, p, slot).wait_recv()

    def turn(value, l):
        native_rows = value.T.astype(bf).reshape(2, 4, 4, 2, 2, 16, 128)
        for cc in (0, 1):
            for xx in range(4):
                lhs_v[cc, l, xx] = native_rows[xx // 2, :, :, xx % 2, cc]

    def arrange(l):
        def step(i, carry):
            cc, a = i // 4, i % 4
            for p in range(3):
                if p == 0:
                    got = jnp.concatenate([lhs_v[cc, l, :, b, a].reshape(64, 128) for b in range(4)], axis=0)
                elif p == 1:
                    got = jnp.concatenate([lhs_v[cc, l, a, :, b].reshape(64, 128) for b in range(4)], axis=0)
                else:
                    got = lhs_v[cc, l, :, a].reshape(256, 128)
                entry[p, :, pl.ds(pl.multiple_of(i * 256, 256), 256)] = got.astype(f32).T.astype(bf)
            return carry

        lax.fori_loop(0, 8, step, 0)

    def open_block(i):
        span = slice(32 * i, 32 * i + 32)

        def inside(held, given):
            ins = [pltpu.make_async_copy(tokens.at[span], held, move_sem.at[0]),
                   pltpu.make_async_copy(coming.at[span], given, move_sem.at[1])]
            for copy in ins:
                copy.start()
            for copy in ins:
                copy.wait()
            opened[span, :] = normed_of(entry_of([stream(held, s) for s in range(4)], mix, 0))[0]
            rhs_v[span, 0:D] = sum(weight(mix, 1, t, 1) * stream(given, t) for t in range(4)).astype(bf)

        pl.run_scoped(inside, pltpu.VMEM((32, 4 * D), bf), pltpu.VMEM((32, 4 * D), bf))

    def arrange_first():
        turn(opened[...], 5)
        arrange(5)

    def fetch(w, p, slot, cc=None):
        n = 128 * WIDTHS[w][p]
        view = outs[w][p]
        if cc is not None:
            n = n // 2
            view = view.at[:, cc * n : (cc + 1) * n]
        return pltpu.make_async_copy(view, tiles.at[slot, p, :, 0:n], tile_sem.at[slot, p])

    def multiply(w, slot, out, begin):
        for p in range(3):
            fetch(w, p, slot).start()
        for p in range(3):
            fetch(w, p, slot).wait()
            n = 128 * WIDTHS[w][p]
            lo = begin + offsets(w)[p]
            out[:, lo : lo + n] = jnp.dot(entry[p], tiles[slot, p, :, 0:n], preferred_element_type=f32)

    def project_keys():
        ready(0)
        multiply(0, 0, joined, 2048)

    def keys_turn():
        for m in (0, 1):
            here = slice(m * 64, m * 64 + 64)
            kv[m, xh, y, z, :, 0:256] = turned(joined[here, 2048:2304], cosine[m], -sine[m]).astype(bf)
            kv[m, xh, y, z, :, 256:512] = joined[here, 2304:2560].astype(bf)

    def project_queries():
        ready(1)
        multiply(1, 0, joined, 0)

    def queries_turn():
        for m in (0, 1):
            here = slice(m * 64, m * 64 + 64)
            for g in range(8):
                query[m, g * 64 : (g + 1) * 64, :] = (turned(
                    joined[here, g * 256 : (g + 1) * 256], cosine[m], -sine[m]) * KEY_SCALE).astype(bf)

    cols = [slice(0, 256), slice(256, 512)]

    def kv_hop(m, p, j):
        if j == 0:
            view, to = kv.at[m, xh, y, z, :, cols[p]], moved(spot, 0, 2)
        else:
            k, d = (j - 1) // 4, (j - 1) % 2
            axis = (1, 2)[(p + k) % 2]
            to = moved(spot, axis, 1 - 2 * d)
            if (j - 1) % 4 < 2:
                if k == 0:
                    view = kv.at[m, :, y, z, :, cols[p]]
                elif axis == 2:
                    view = kv.at[m, :, :, z, :, cols[p]]
                else:
                    view = kv.at[m, :, y, :, :, cols[p]]
            else:
                near = (spot[axis] + 3 + 2 * d) % 4
                half = slice(p * 256 + d * 128, p * 256 + d * 128 + 128)
                if k == 0:
                    view = kv.at[m, :, y, near, :, half] if axis == 2 else kv.at[m, :, near, z, :, half]
                else:
                    view = kv.at[m, :, :, near, :, half] if axis == 2 else kv.at[m, :, near, :, :, half]
        return pltpu.make_async_remote_copy(
            view, view, k_send.at[m, p, j], k_recv.at[m, p, j], device_id=ident(*to), device_id_type=MESH)

    def kv_event(m, e):
        for p in range(2):
            if e == 0:
                kv_hop(m, p, 0).start()
            elif e in (1, 3):
                for j in (0,) if e == 1 else (3, 4):
                    kv_hop(m, p, j).wait_recv()
                kv_hop(m, p, 2 * e - 1).start()
                kv_hop(m, p, 2 * e).start()
            elif e in (2, 4):
                for d in (0, 1):
                    kv_hop(m, p, 2 * e - 3 + d).wait_recv()
                    kv_hop(m, p, 2 * e - 1 + d).start()
            else:
                kv_hop(m, p, 7).wait_recv()
                kv_hop(m, p, 8).wait_recv()

    def attend(m, block):
        if block == 0:
            top[...] = jnp.full_like(top, -1e30)
            bottom[...] = jnp.zeros_like(bottom)
            rows_out[m] = jnp.zeros((ROWS, KV * HD), f32)

        @pl.when(block * KB <= anchor + 63)
        def _():
            columns = (block * KB + lax.broadcasted_iota(jnp.int32, (ROWS, KB), 1)).astype(f32)
            keep = (columns >= marks[m, :, 8:9]) & (columns <= marks[m, :, 9:10])
            held = kv[m, block // 2, (block % 2) * 2 : (block % 2) * 2 + 2].reshape(KB, 512)
            done = []
            for h in range(KV):
                lanes = slice(h * HD, (h + 1) * HD)
                s = jnp.where(keep, last(query[m, :, lanes], held[:, lanes]), -1e30)
                high = jnp.maximum(top[h], jnp.max(s, axis=1, keepdims=True))
                fade = jnp.exp(top[h] - high)
                e = jnp.exp(s - high)
                bottom[h] = bottom[h] * fade + jnp.sum(e, axis=1, keepdims=True)
                done.append(rows_out[m, :, lanes] * fade + jnp.dot(
                    e.astype(bf), held[:, 256 + h * HD : 256 + (h + 1) * HD], preferred_element_type=f32))
                top[h] = high
            rows_out[m] = jnp.concatenate(done, axis=1)

        if block == 3:
            rows_out[m] = jnp.concatenate(
                [rows_out[m, :, h * HD : (h + 1) * HD] / bottom[h] for h in range(KV)], axis=1)
            lse[m] = jnp.concatenate(
                [top[h] + jnp.log(bottom[h]) for h in range(KV)] + [jnp.zeros((ROWS, 124), f32)], axis=1)

    def output():
        for g in range(8):
            left = jnp.concatenate([rows_out[m, g * 64 : (g + 1) * 64, :] for m in (0, 1)], axis=0)
            native_rows = left.T.astype(bf).reshape(4, 2, 2, 16, 128)
            for h in range(KV):
                for cc in (0, 1):
                    for xl in (0, 1):
                        lhs_v[cc, 4, 2 * (h // 2) + xl, (h % 2) * 2 + g // 4, g % 4] = native_rows[h, xl, cc]
        arrange(4)
        ready(2)
        multiply(2, 1, branch_one, 0)

    def between():
        def inside(held, made_rows):
            def step(i, carry):
                span = pl.ds(pl.multiple_of(i * 32, 32), 32)
                inward = pltpu.make_async_copy(tokens.at[span], held, move_sem.at[0])
                inward.start()
                inward.wait()
                branch = branch_one[span, :]
                after = None
                for t in range(4):
                    out = mixed_out([stream(held, s) for s in range(4)], branch, mix, 0, t)
                    made_rows[:, t * D : (t + 1) * D] = out
                    term = weight(mix, 1, t, 0) * out
                    after = term if after is None else after + term
                outward = pltpu.make_async_copy(made_rows, middle.at[span], move_sem.at[1])
                outward.start()
                opened[span, :] = normed_of(after)[0]
                outward.wait()
                return carry

            lax.fori_loop(0, 4, step, 0)

        pl.run_scoped(inside, pltpu.VMEM((32, 4 * D), bf), pltpu.VMEM((32, 4 * D), f32))
        turn(opened[...], 3)
        arrange(3)
        branch_two[...] = jnp.zeros_like(branch_two)
        native[...] = jnp.zeros_like(native)

    def low(s, cc):
        return pltpu.make_async_copy(outs[3][s].at[cc * UNIT : (cc + 1) * UNIT, :], lower.at[cc], low_sem.at[cc])

    def hidden_back(s):
        if s == 0:
            ready(3)
        for cc in (0, 1):
            low(s, cc).start()
        for cc in (0, 1):
            low(s, cc).wait()

            def part(i, carry, cc=cc):
                lanes = pl.ds(pl.multiple_of(i * 256, 256), 256)
                dz[:, pl.ds(pl.multiple_of((2 * s + cc) * UNIT + i * 256, 256), 256)] = last(
                    rhs_v[:, 0:D], lower[cc, lanes, :])
                return carry

            lax.fori_loop(0, UNIT // 256, part, 0)

    def share(s, cc, p):
        return fetch(4 + s, p, cc, cc) if s < 2 else fetch(6 + cc, p, cc)

    def feed_start(s, cc):
        if s == 2:
            ready(6 + cc)
        elif cc == 0:
            ready(4 + s)
        for p in range(3):
            share(s, cc, p).start()
        low(s, cc).start()

    def spans(s):
        half = [64 * n for n in WIDTHS[4 + s]] if s < 2 else [128 * n for n in WIDTHS[6]]
        return [(0, half[0]), (half[0], half[1]), (half[0] + half[1], half[2])]

    def feed_open(s, cc):
        for p, (lo, n) in enumerate(spans(s)):
            share(s, cc, p).wait()
            opened[:, lo : lo + n] = jnp.dot(entry[p], tiles[cc, p, :, 0:n], preferred_element_type=f32)

    def feed_act(s, cc):
        begin = D + 2 * UNIT * (2 * s + cc)

        def act(i, carry):
            lanes = pl.ds(pl.multiple_of(i * 256, 256), 256)
            given = dz[:, pl.ds(pl.multiple_of((2 * s + cc) * UNIT + i * 256, 256), 256)]
            gate = opened[:, lanes]
            upper = opened[:, pl.ds(pl.multiple_of(UNIT + i * 256, 256), 256)]
            sigma = jax.nn.sigmoid(gate)
            shut = gate * sigma
            rhs_v[:, pl.ds(pl.multiple_of(begin + i * 256, 256), 256)] = (
                given * upper * sigma * (1.0 + gate * (1.0 - sigma))).astype(bf)
            rhs_v[:, pl.ds(pl.multiple_of(begin + UNIT + i * 256, 256), 256)] = (given * shut).astype(bf)
            opened[:, lanes] = shut * upper
            return carry

        lax.fori_loop(0, UNIT // 256, act, 0)
        low(s, cc).wait()
        hidden = opened[:, 0:UNIT]
        by_axis = hidden.T.astype(bf).reshape(4, 4, 4, 16, 128)
        for a in range(4):
            for b in range(4):
                if s == 0:
                    lhs_v[cc, s, :, b, a] = by_axis[a, b]
                elif s == 1:
                    lhs_v[cc, s, a, :, b] = by_axis[a, b]
                else:
                    lhs_v[cc, s, b, a] = by_axis[a, b]
        branch_two[...] += jnp.dot(hidden.astype(bf), lower[cc], preferred_element_type=f32)

    def feed_back(s, cc):
        begin = D + 2 * UNIT * (2 * s + cc)
        for p, (lo, n) in enumerate(spans(s)):
            put_back(native, p, last(tiles[cc, p, :, 0:n], rhs_v[:, begin + lo : begin + lo + n]))

    def norm_in():
        native_columns(native, dn)

    tasks = {}
    for i in range(4):
        tasks[i] = functools.partial(open_block, i)
    tasks[4], tasks[5], tasks[6], tasks[7], tasks[8] = arrange_first, project_keys, keys_turn, project_queries, queries_turn
    for i in range(8):
        tasks[9 + i] = functools.partial(attend, i // 4, i % 4)
    tasks[17], tasks[18] = output, between
    for s in range(3):
        for cc in (0, 1):
            tasks[43 + 2 * s + cc] = functools.partial(feed_start, s, cc)
            for n, part in enumerate((feed_open, feed_act, feed_back)):
                tasks[20 + 7 * s + 3 * cc + n] = functools.partial(part, s, cc)
    for s in range(3):
        tasks[49 + s] = functools.partial(hidden_back, s)
    tasks[40], tasks[41], tasks[42] = norm_in, own_others, own_expansion

    barrier = pltpu.get_barrier_semaphore()
    others = [sibling, moved(spot, 0, 2)] + [moved(spot, axis, step) for axis in range(3) for step in (1, 3)]
    for other in others:
        pl.semaphore_signal(barrier, inc=1, device_id=ident(*other), device_id_type=MESH)
    pl.semaphore_wait(barrier, len(others))
    own_projection()
    for kind, a, b in SEQUENCE:
        if kind == 0:
            event(a, b)
        elif kind == 1:
            kv_event(a, b)
        else:
            tasks[a]()

    aways = [pltpu.make_async_copy(lhs_v, lhs, move_sem.at[0]), pltpu.make_async_copy(rhs_v, rhs, move_sem.at[1])]
    for copy in aways:
        copy.start()
    for w in range(ARRAYS):
        for p in range(3):
            for k in range(3):
                for j in (0, 1) + onward(k):
                    ring(w, p, k, j).wait_send()
            for slot in range(4):
                spread(w, p, slot).wait_send()
    for m in (0, 1):
        for p in range(2):
            for j in range(9):
                kv_hop(m, p, j).wait_send()
    for copy in aways:
        copy.wait()


def run_forward(shards, tokens, coming, mix, cosine, sine, marks, collective_id):
    bf = jnp.bfloat16
    f32 = jnp.float32
    v = pltpu.VMEM
    dma = pltpu.SemaphoreType.DMA
    hbm = pl.BlockSpec(memory_space=pl.ANY)
    near = pl.BlockSpec(memory_space=pltpu.VMEM)
    S = jax.ShapeDtypeStruct
    return pl.pallas_call(
        forward_pass,
        out_shape=[S((2048, 128 * n), bf) for widths in WIDTHS for n in widths] + [
            S((2, 6, 4, 4, 4, 16, 128), bf),
            S((128, D + 12 * UNIT), bf),
            S((2, ROWS, 256), bf),
            S((2, 2, 4, 4, 64, 512), bf),
            S((2, ROWS, 256), f32),
            S((2, ROWS, 128), f32),
            S((128, D), f32),
            S((128, 4 * D), f32),
            S((128, D), f32),
            S((128, D), f32),
        ],
        in_specs=[near] * 4 + [hbm] * 2 + [pl.BlockSpec(memory_space=pltpu.SMEM)] + [near] * 3,
        out_specs=[hbm] * (3 * ARRAYS + 2) + [near] * 5 + [hbm] + [near] * 2,
        scratch_shapes=[
            v((16, 512), bf),
            v((16, D), bf),
            v((16, D), bf),
            v((48, D), bf),
            v((16, 12 * UNIT), bf),
            v((5632, 16), f32),
            v((3, 128, D), bf),
            v((2, 6, 4, 4, 4, 16, 128), bf),
            v((128, D + 12 * UNIT), bf),
            v((128, 6 * UNIT), f32),
            v((KV, ROWS, 1), f32),
            v((KV, ROWS, 1), f32),
            v((128, 2560), f32),
            v((2, 4, 4, 2, 2, 16, 128), f32),
            v((128, 2 * UNIT), f32),
            v((2, 3, 2048, 768), bf),
            v((2, UNIT, D), bf),
            dma((ARRAYS, 3, 2)),
            dma((ARRAYS, 3, 3, 4)),
            dma((ARRAYS, 3, 3, 4)),
            dma((ARRAYS, 3, 4)),
            dma((ARRAYS, 3, 4)),
            dma((2, 2, 9)),
            dma((2, 2, 9)),
            dma((2, 3)),
            dma((2,)),
            dma((2,)),
        ],
        compiler_params=pltpu.CompilerParams(
            collective_id=collective_id, has_side_effects=True, vmem_limit_bytes=62 * 1024 * 1024),
    )(*shards, tokens, coming, mix, cosine, sine, marks)


def adam(weight, grad, first, second, factor, rate, decay):
    grad = grad * factor
    first = BETA_ONE * first + (1.0 - BETA_ONE) * grad
    second = BETA_TWO * second + (1.0 - BETA_TWO) * grad * grad
    ahead = first / (1.0 - BETA_ONE**STEP)
    scaled = second / (1.0 - BETA_TWO**STEP)
    weight = weight - rate * (ahead / (jnp.sqrt(scaled) + ADAM_EPS) + decay * weight)
    return (weight, first, second)


def update_kernel(factor, grads, *refs):
    given, outs, ins, units, sems = refs[:12], refs[12:24], refs[24:36], refs[36], refs[37]
    copies = [pltpu.make_async_copy(given[n], ins[n], sems.at[n]) for n in range(12)]
    for copy in copies:
        copy.start()
    waited = []

    def write(n, where, grad):
        if n not in waited:
            waited.append(n)
            for copy in copies[3 * n : 3 * n + 3]:
                copy.wait()
        news = adam(ins[3 * n][where], grad, ins[3 * n + 1][where], ins[3 * n + 2][where],
                    factor[0], RATE_MATRIX, DECAY_MATRIX)
        for out, new in zip(outs[3 * n : 3 * n + 3], news):
            out[where] = new

    everything = (slice(None), slice(None))
    queries = jnp.concatenate([grads[40 + n] for n in range(4)], axis=1)
    pairs = [queries[:, (KV * g + h) * HD : (KV * g + h + 1) * HD] for h in range(KV) for g in range(8)]
    write(0, (slice(None), slice(0, 2048)), jnp.concatenate(pairs, axis=1))
    write(0, (slice(None), slice(2048, 2560)), grads[44])
    write(1, everything, jnp.concatenate([grads[36 + n] for n in range(4)], axis=1))
    for half in (0, 1):
        for s in range(3):
            for cc in (0, 1):
                first_unit = 12 + 4 * (2 * s + cc) + 2 * half
                turned_rows = jnp.concatenate([grads[first_unit], grads[first_unit + 1]], axis=1).T
                for n in range(64):
                    d = unit_place(s, cc, n // 16, (n // 4) % 4, n % 4)
                    size = 12 if s == 2 else 16
                    units[44 * d + 16 * s : 44 * d + 16 * s + size, :] = turned_rows[16 * n : 16 * n + size]
        write(2, (slice(None), slice(half * FF, (half + 1) * FF)), units[...].T)
    for band in range(3):
        size = 12 if band == 2 else 16
        rows = jnp.concatenate([grads[4 * band + n] for n in range(4)], axis=1)
        write(3, (slice(16 * band, 16 * band + size), slice(None)), rows[:size])


def update(factor, grads, arrays):
    near = pl.BlockSpec(memory_space=pltpu.VMEM)
    return pl.pallas_call(
        update_kernel,
        out_shape=[jax.ShapeDtypeStruct(a.shape, jnp.float32) for a in arrays],
        in_specs=[pl.BlockSpec(memory_space=pltpu.SMEM), near] + [pl.BlockSpec(memory_space=pl.ANY)] * 12,
        out_specs=[near] * 12,
        scratch_shapes=[pltpu.VMEM(a.shape, jnp.float32) for a in arrays]
        + [pltpu.VMEM((FF, 16), jnp.float32), pltpu.SemaphoreType.DMA((12,))],
        compiler_params=pltpu.CompilerParams(vmem_limit_bytes=62 * 1024 * 1024),
    )(factor, grads, *arrays)


def tables(spots):
    freq = jnp.exp(jnp.arange(HD // 2, dtype=jnp.float32) * (-2.0 * math.log(THETA_BASE) / HD))
    angle = spots.reshape(2, 64, 1) * freq
    cosine, sine = jnp.cos(angle), jnp.sin(angle)
    return (jnp.tile(jnp.concatenate([cosine, cosine], axis=2), (1, 1, KV)),
            jnp.tile(jnp.concatenate([sine, -sine], axis=2), (1, 1, KV)))


def body(streams, doc_start, cotangent, mixing, w_project, w_output, w_expand, w_reduce,
         first_mixing, second_mixing, first_project, second_project, first_output, second_output,
         first_expand, second_expand, first_reduce, second_reduce):
    bf, f32 = jnp.bfloat16, jnp.float32
    anchor = lax.axis_index("ctx") * 64
    tokens = streams.reshape(128, 8192)
    coming = cotangent.reshape(128, 8192)
    starts = doc_start.reshape(2, 64)
    places = anchor + jnp.arange(64, dtype=jnp.int32)
    spots = (places[None, :] - starts).astype(f32).reshape(128)
    mix = mixing.reshape(48)

    cosine, sine = tables(spots)
    edges = jnp.stack([jnp.tile(starts, (1, 8)), jnp.broadcast_to(jnp.tile(places, 8), (2, ROWS))], axis=2).astype(f32)
    marks = jnp.pad(edges, ((0, 0), (0, 0), (8, 118)))

    got = run_forward([w_project, w_output, w_expand, w_reduce], tokens, coming, mix, cosine, sine, marks, 1)
    pieces, outputs = got[:6], got[6:9]
    lhs, rhs, query, kv, mixed, lse, branch_one, middle, branch_two, dn_two = got[24:]
    middle_grad, grad_one, notes = call(
        between_kernel, mix, [middle, coming, dn_two], [(8192, f32), (2048, bf)], 8)
    dout, stats = output_back(grad_one, outputs, mixed, lse, marks)
    grads, tokens_grad, fresh, total = run_backward(
        lhs, rhs, grad_one, query, dout, kv.reshape(2, 2048, 512), stats, cosine, sine, pieces,
        [tokens, middle_grad, middle, coming, branch_one, branch_two], mix, notes, 2)
    sums = jnp.sum(total, axis=1)
    two, one, zero = sums[:24], sums[24:48], sums[48:]
    mix_total = jnp.stack([
        jnp.concatenate([zero[:4, None], one[4:8, None], one[8:24].reshape(4, 4)], axis=1),
        jnp.concatenate([one[:4, None], two[:4, None], two[4:20].reshape(4, 4)], axis=1),
    ])

    norm = jnp.sqrt(zero[7] + jnp.sum(mix_total * mix_total))
    factor = THRESHOLD / jnp.maximum(norm, THRESHOLD)
    mix_new = adam(mixing, mix_total, first_mixing, second_mixing, factor, RATE_MIXING, 0.0)
    new = update(factor.reshape(1), grads, [
        w_project, first_project, second_project, w_output, first_output, second_output,
        w_expand, first_expand, second_expand, w_reduce, first_reduce, second_reduce])
    return (fresh.reshape(streams.shape), tokens_grad.reshape(streams.shape), norm,
            *mix_new, *new)


def solution(mesh):
    acts = P(None, "fsdp", "ctx", None, None)
    rows = P(("ctx", "fsdp"), None)
    return jax.shard_map(
        body,
        mesh=mesh,
        in_specs=(acts, P(None, "fsdp", "ctx"), acts, P()) + (rows,) * 4 + (P(), P()) + (rows,) * 8,
        out_specs=(acts, acts, P(), P(), P(), P()) + (rows,) * 12,
        check_vma=False,
    )
```
